32 devices in a mesh: dp: 4 (over y, x), fsdp: 8 (over z, core).
Axes of the slice: x: 2, y: 2, z: 4, core: 2. Of those that a mesh axis runs over, the one named last changes fastest.
Arguments:
- tokens: bfloat16 [32768, 1024], P(('dp', 'fsdp')), may hold values from -6 to 6
- lengths: int32 [64], P(('dp', 'fsdp')), may hold values from 64 to 512, as said below
- w_qkv: bfloat16 [1024, 3072], P(('dp', 'fsdp')), may hold values from -0.1875 to 0.1875
- w_out: bfloat16 [1024, 1024], P(('dp', 'fsdp')), may hold values from -1.5 to 1.5
- w_in: bfloat16 [1024, 4096], P(('dp', 'fsdp')), may hold values from -0.1875 to 0.1875
- w_down: bfloat16 [4096, 1024], P(('dp', 'fsdp')), may hold values from -0.09375 to 0.09375
- gain_one: float32 [1024], replicated, may hold values from 0.5 to 1.5
- gain_two: float32 [1024], replicated, may hold values from 0.5 to 1.5
- bias_q: float32 [1024], replicated, may hold values from -3 to 3
- bias_v: float32 [1024], replicated, may hold values from -3 to 3
- bias_out: float32 [1024], replicated, may hold values from -3 to 3
- beta_one: float32 [1024], replicated, may hold values from -3 to 3
- bias_in: float32 [4096], replicated, may hold values from -3 to 3
- bias_down: float32 [1024], replicated, may hold values from -3 to 3
- beta_two: float32 [1024], replicated, may hold values from -3 to 3
- cotangent: bfloat16 [32768, 1024], P(('dp', 'fsdp')), may hold values from -6 to 6
Outputs:
- output: bfloat16 [32768, 1024], P(('dp', 'fsdp'))
- input_grad: bfloat16 [32768, 1024], P(('dp', 'fsdp'))
- grad_bias_q: float32 [1024], P(('dp', 'fsdp'))
- grad_bias_v: float32 [1024], P(('dp', 'fsdp'))
- grad_bias_out: float32 [1024], P(('dp', 'fsdp'))
- grad_beta_one: float32 [1024], P(('dp', 'fsdp'))
- grad_bias_in: float32 [4096], P(('dp', 'fsdp'))
- grad_bias_down: float32 [1024], P(('dp', 'fsdp'))
- grad_beta_two: float32 [1024], P(('dp', 'fsdp'))
The draws below stay inside these ranges and needn't reach their ends.
Inputs may be any that keep to these rules, and one draw needn't show every extreme that they name: `lengths`: one sequence, drawn from the seed, has exactly 512 live tokens.
All inputs are finite; a program needn't handle non-finite values.
Results may differ from the reference program's by a relative error of at most 0.013.
Values may be sent and summed in bfloat16 or wider, within the bound.
No kernel may reach another device: no remote copies, remote signals or barrier semaphores. Data moves between devices by JAX's collectives and lax.ppermute only.
A program may use at most 192 MiB of HBM per device.

```python
import math
import jax
import jax.numpy as jnp
from jax import lax

D = 1024
HD = 64
FF = 4096
L = 512
NSEQ = 64
TOKENS = 32768


def draw_lengths(key, part):
    key = jax.random.fold_in(key, 11)
    first_key, second_key = jax.random.split(key)
    drawn = jax.random.randint(first_key, (NSEQ,), max(1, L // 8), L + 1)
    chosen = jax.random.randint(second_key, (), 0, NSEQ)
    return jnp.where(jnp.arange(NSEQ) == chosen, L, drawn).astype(jnp.int32)


def strengthened(values, own_key, source, target, shards_of, factor):
    def block_of(axis_at):
        return (jnp.arange(values.shape[axis_at]) // (values.shape[axis_at] // shards_of)).reshape((-1,) + (1,) * (values.ndim - 1 - axis_at))

    one_side = jax.random.permutation(own_key, shards_of)[block_of(target)]
    second = (block_of(target) + shards_of // 2) % shards_of
    return jnp.where((block_of(source) == one_side) | (block_of(source) == second), factor * values, values)


def steps_of(rng, extent, cuts, low, largest):
    gain = 1.0
    for dim, blocks in cuts:
        heights = jax.random.uniform(jax.random.fold_in(jax.random.fold_in(rng, 6), dim), (blocks,), jnp.float32, low / len(cuts), largest / len(cuts))
        gain = gain * jnp.repeat(jnp.exp(heights), extent[dim] // blocks).reshape((-1,) + (1,) * (len(extent) - 1 - dim))
    return gain


def centred(own_key, dims, width, bound, shards=(), held_as=jnp.bfloat16):
    values = jax.random.normal(own_key, dims, jnp.float32) * width
    if len(shards) > 0:
        values = steps_of(own_key, dims, shards, -0.22, 0.18) * values
    return jnp.clip(values, min=-bound, max=bound).astype(held_as)


def noise_with(stream_key, shape, spread, bound, cuts, heavy, kind=jnp.bfloat16):
    values = spread * jax.random.normal(stream_key, shape, jnp.float32)
    if cuts:
        values = values * steps_of(stream_key, shape, cuts, -0.22, 0.18)
    return jnp.clip(strengthened(values, jax.random.fold_in(stream_key, 3), *heavy), -bound, bound).astype(kind)


def setup_inputs(seed: int = 0) -> dict:
    key_of = jax.random.split(jax.random.key(seed), 17)
    tokens = centred(key_of[0], (TOKENS, D), 1.0, 6.0, ((0, 32),))
    lengths = draw_lengths(jax.random.fold_in(key_of[16], 71), 0)
    w_qkv = centred(key_of[2], (D, 3 * D), D ** -0.5, 0.1875, ((0, 32),))
    w_out = centred(key_of[3], (D, D), (D // 64) ** -0.5, 1.5, ((0, 32),))
    w_in = centred(key_of[4], (D, FF), D ** -0.5, 0.1875, ((0, 32),))
    w_down = centred(key_of[5], (FF, D), FF ** -0.5, 0.09375, ((0, 32),))
    gain_one = jnp.clip(1.0 + 0.1 * jax.random.normal(key_of[6], (D,), jnp.float32), 0.5, 1.5)
    gain_two = jnp.clip(1.0 + 0.1 * jax.random.normal(key_of[7], (D,), jnp.float32), 0.5, 1.5)
    bias_q = centred(key_of[8], (D,), 0.5, 3.0, (), jnp.float32)
    bias_v = centred(key_of[9], (D,), 0.5, 3.0, (), jnp.float32)
    bias_out = centred(key_of[10], (D,), 0.5, 3.0, (), jnp.float32)
    beta_one = centred(key_of[11], (D,), 0.5, 3.0, (), jnp.float32)
    bias_in = centred(key_of[12], (FF,), 0.5, 3.0, (), jnp.float32)
    bias_down = centred(key_of[13], (D,), 0.5, 3.0, (), jnp.float32)
    beta_two = centred(key_of[14], (D,), 0.5, 3.0, (), jnp.float32)
    cotangent = noise_with(key_of[15], (TOKENS, D), 1.0, 6.0, ((0, 32),), (0, 1, 32, 2.75))
    return dict(tokens=tokens, lengths=lengths, w_qkv=w_qkv, w_out=w_out, w_in=w_in, w_down=w_down, gain_one=gain_one, gain_two=gain_two, bias_q=bias_q, bias_v=bias_v, bias_out=bias_out, beta_one=beta_one, bias_in=bias_in, bias_down=bias_down, beta_two=beta_two, cotangent=cotangent)


HIGH = lax.Precision.HIGHEST
LN_EPS = 1e-12

@jax.custom_vjp
def low(v):
    return lax.optimization_barrier(v.astype(jnp.bfloat16)).astype(jnp.float32)

@jax.custom_vjp
def low_back(v):
    return v

def low_keep(v):
    return (low(v), None)

def low_pass(kept, grad):
    return (grad,)

def back_keep(v):
    return (v, None)

def back_low(kept, grad):
    return (low(grad),)
low.defvjp(low_keep, low_pass)
low_back.defvjp(back_keep, back_low)

def norm_rows(hidden, gain_vec, shift_vec):
    row_mean = lax.optimization_barrier(jnp.mean(hidden, axis=-1, keepdims=True))
    centered = hidden - row_mean
    row_var = lax.optimization_barrier(jnp.mean(centered * centered, axis=-1, keepdims=True))
    return centered * lax.rsqrt(row_var + LN_EPS) * gain_vec + shift_vec

def layer_group(inputs, seq_lengths, matrices, gains, biases):
    w_qkv, w_out, w_in, w_down = matrices
    gain_one, gain_two = gains
    bias_q, bias_v, bias_out, beta_one, bias_in, bias_down, beta_two = biases
    seq_count = inputs.shape[0]
    model_width = w_out.shape[0]
    head_count = model_width // HD
    score_scale = 1.0 / math.sqrt(HD)
    projected = jnp.einsum('bld,de->ble', inputs, w_qkv, precision=HIGH)
    queries = low(low_back(projected[..., :model_width] + bias_q))
    key_vals = low(low_back(projected[..., model_width:2 * model_width]))
    values = low(low_back(projected[..., 2 * model_width:] + bias_v))
    queries = queries.reshape(seq_count, L, head_count, HD)
    key_vals = key_vals.reshape(seq_count, L, head_count, HD)
    values = values.reshape(seq_count, L, head_count, HD)
    scores = jnp.einsum('bqhe,bkhe->bhqk', queries, key_vals, precision=HIGH) * score_scale
    scores = low_back(scores)
    live_keys = jnp.arange(L)[None, :] < seq_lengths[:, None]
    scores = jnp.where(live_keys[:, None, None, :], scores, -1e+30)
    peak = lax.optimization_barrier(jnp.max(scores, axis=-1, keepdims=True))
    powers = jnp.exp(scores - peak)
    attn_probs = low(powers / lax.optimization_barrier(jnp.sum(powers, axis=-1, keepdims=True)))
    context = jnp.einsum('bhqk,bkhe->bqhe', attn_probs, values, precision=HIGH)
    context = low(low_back(context.reshape(seq_count, L, model_width)))
    attended = low_back(jnp.einsum('bld,de->ble', context, w_out, precision=HIGH) + bias_out)
    normed_one = norm_rows(inputs + attended, gain_one, beta_one)
    hidden_pre = low_back(jnp.einsum('bld,df->blf', low(normed_one), w_in, precision=HIGH) + bias_in)
    active = low(jax.nn.gelu(hidden_pre, approximate=False))
    branch_out = low_back(jnp.einsum('blf,fd->bld', active, w_down, precision=HIGH) + bias_down)
    return norm_rows(normed_one + branch_out, gain_two, beta_two)

def reference(tokens, lengths, w_qkv, w_out, w_in, w_down, gain_one, gain_two, bias_q, bias_v, bias_out, beta_one, bias_in, bias_down, beta_two, cotangent):
    matrices = (w_qkv.astype(jnp.float32), w_out.astype(jnp.float32), w_in.astype(jnp.float32), w_down.astype(jnp.float32))
    gains = (gain_one.astype(jnp.float32), gain_two.astype(jnp.float32))
    biases = (bias_q.astype(jnp.float32), bias_v.astype(jnp.float32), bias_out.astype(jnp.float32), beta_one.astype(jnp.float32), bias_in.astype(jnp.float32), bias_down.astype(jnp.float32), beta_two.astype(jnp.float32))
    per_step = math.gcd(NSEQ, max(1, 4096 // L))
    step_count = NSEQ // per_step
    inputs_all = tokens.astype(jnp.float32).reshape(step_count, per_step, L, D)
    cot_all = cotangent.astype(jnp.float32).reshape(step_count, per_step, L, D)
    lengths_all = lengths.astype(jnp.int32).reshape(step_count, per_step)

    def one_step(accumulated, pieces):
        inputs, seq_lengths, cot_rows = pieces
        live_rows = (jnp.arange(L)[None, :] < seq_lengths[:, None]).astype(jnp.float32)

        def run(layer_in, bias_set):
            return layer_group(layer_in, seq_lengths, matrices, gains, bias_set)
        result, pullback = jax.vjp(run, inputs, biases)
        grad_in, grad_bias = pullback(cot_rows * live_rows[:, :, None])
        accumulated = jax.tree.map(lambda left, right: left + right, accumulated, grad_bias)
        return (accumulated, (result.astype(jnp.bfloat16), grad_in.astype(jnp.bfloat16)))
    zeros_start = tuple((jnp.zeros_like(vector) for vector in biases))
    accumulated, (results, grads) = lax.scan(one_step, zeros_start, (inputs_all, lengths_all, cot_all))
    return (results.reshape(TOKENS, D), grads.reshape(TOKENS, D), accumulated[0], accumulated[1], accumulated[2], accumulated[3], accumulated[4], accumulated[5], accumulated[6])
```

```python
import functools
import math

import jax
import jax.numpy as jnp
from jax import lax
from jax.experimental import pallas as pl
from jax.experimental.pallas import tpu as pltpu
from jax.sharding import PartitionSpec as P

HD = 64
L = 512
LN_EPS = 1e-12
MIB = 2**20
BF = jnp.bfloat16
F32 = jnp.float32


def params(limit=60, semantics=None):
    return pltpu.CompilerParams(vmem_limit_bytes=limit * MIB, dimension_semantics=semantics)


def dot(left, right, on_left, on_right):
    return lax.dot_general(
        left, right, (((on_left,), (on_right,)), ((), ())), preferred_element_type=F32
    )


def shape_of(dims, kind):
    return jax.ShapeDtypeStruct(dims, kind)


def project_body(x_ref, w_ref, bias_ref, scale_ref, out_ref):
    total = dot(x_ref[...], w_ref[...], 1, 0) + bias_ref[...]
    out_ref[...] = (total * scale_ref[...]).astype(BF)


def project(rows, w_qkv, bias, scale):
    count, width = rows.shape
    wide = w_qkv.shape[1]
    step = 512
    return pl.pallas_call(
        project_body,
        out_shape=shape_of((count, wide), BF),
        grid=(wide // step,),
        in_specs=[
            pl.BlockSpec((count, width), lambda j: (0, 0)),
            pl.BlockSpec((width, step), lambda j: (0, j)),
            pl.BlockSpec((1, step), lambda j: (0, j)),
            pl.BlockSpec((1, step), lambda j: (0, j)),
        ],
        out_specs=pl.BlockSpec((count, step), lambda j: (0, j)),
        compiler_params=params(),
        name="project",
    )(rows, w_qkv, bias, scale)


def lane_halves(kind):
    lane = lax.broadcasted_iota(jnp.int32, (1, 128), 1)
    return [(lane < HD).astype(F32).astype(kind), (lane >= HD).astype(F32).astype(kind)]


QUAD = 256


def attend_body(len_ref, q_ref, k_ref, v_ref, o_ref, e_ref, r_ref):
    length = len_ref[pl.program_id(0)]
    halves = lane_halves(BF)
    lane = lax.broadcasted_iota(jnp.int32, (L, 128), 1)
    row = lax.broadcasted_iota(jnp.int32, (L, 128), 0)
    q_side = jnp.where(lane == 0, 1.0, 0.0).astype(BF)
    k_side = jnp.where((lane == 0) & (row >= length), -1e30, 0.0).astype(BF)
    for pair in range(QUAD // 128):
        part = slice(pair * 128, (pair + 1) * 128)
        q_pair = jnp.concatenate([q_ref[:, part], q_side], axis=1)
        k_pair = k_ref[:, part]
        v_pair = v_ref[:, part]
        powers = []
        for head in range(2):
            k_one = jnp.concatenate([k_pair * halves[head], k_side], axis=1)
            scores = dot(q_pair, k_one, 1, 1)
            peak = jnp.max(scores, axis=1, keepdims=True)
            power = jnp.exp(scores - peak).astype(BF)
            e_ref[2 * pair + head] = power
            powers.append(power)
        right = jnp.concatenate(
            [
                jnp.concatenate([v_pair * half, jnp.broadcast_to(half, (L, 128))], axis=1)
                for half in halves
            ],
            axis=0,
        )
        both = dot(jnp.concatenate(powers, axis=1), right, 1, 0)
        inverse = 1.0 / both[:, 128:]
        r_ref[:, part] = inverse
        o_ref[:, part] = (both[:, :128] * inverse).astype(BF)


def attend(lengths, qkv, width):
    count = qkv.shape[0]
    seqs = count // L
    quads = width // QUAD
    heads = QUAD // HD
    return pl.pallas_call(
        attend_body,
        out_shape=(
            shape_of((count, width), BF),
            shape_of((seqs * width // HD, L, L), BF),
            shape_of((count, width), F32),
        ),
        grid_spec=pltpu.PrefetchScalarGridSpec(
            num_scalar_prefetch=1,
            grid=(seqs, quads),
            in_specs=[
                pl.BlockSpec((L, QUAD), lambda i, j, n: (i, j)),
                pl.BlockSpec((L, QUAD), lambda i, j, n: (i, quads + j)),
                pl.BlockSpec((L, QUAD), lambda i, j, n: (i, 2 * quads + j)),
            ],
            out_specs=[
                pl.BlockSpec((L, QUAD), lambda i, j, n: (i, j)),
                pl.BlockSpec((heads, L, L), lambda i, j, n: (i * quads + j, 0, 0)),
                pl.BlockSpec((L, QUAD), lambda i, j, n: (i, j)),
            ],
        ),
        compiler_params=params(),
        name="attend",
    )(lengths, qkv, qkv, qkv)


def feed_body(x_ref, o_ref, wo_ref, wi_ref, vec_ref, bi_ref, u_ref, s_ref, gl_ref, gp_ref, ub_ref):
    @pl.when(pl.program_id(1) == 0)
    def _():
        joined = dot(o_ref[...], wo_ref[...], 1, 0) + vec_ref[0:1, :] + x_ref[...].astype(F32)
        centered = joined - jnp.mean(joined, axis=1, keepdims=True)
        spread = lax.rsqrt(jnp.mean(centered * centered, axis=1, keepdims=True) + LN_EPS)
        normed = centered * spread * vec_ref[1:2, :] + vec_ref[2:3, :]
        u_ref[...] = normed
        s_ref[...] = jnp.broadcast_to(spread, s_ref.shape)
        ub_ref[...] = normed.astype(BF)

    step = 256
    for part in range(gl_ref.shape[1] // step):
        cols = slice(part * step, (part + 1) * step)
        pre = dot(ub_ref[...], wi_ref[:, cols], 1, 0) + bi_ref[:, cols]
        phi = 0.5 + 0.5 * lax.erf(pre * math.sqrt(0.5))
        slope = phi + pre * jnp.exp(-0.5 * pre * pre) * (1.0 / math.sqrt(2.0 * math.pi))
        gl_ref[:, cols] = (pre * phi).astype(BF)
        gp_ref[:, cols] = slope.astype(BF)


def feed(rows, context, w_out, w_in, vectors, bias_in):
    count, width = rows.shape
    wide = w_in.shape[1]
    step = 1024
    return pl.pallas_call(
        feed_body,
        out_shape=(
            shape_of((count, width), F32),
            shape_of((count, 128), F32),
            shape_of((count, wide), BF),
            shape_of((count, wide), BF),
        ),
        grid=(count // L, wide // step),
        in_specs=[
            pl.BlockSpec((L, width), lambda i, j: (i, 0)),
            pl.BlockSpec((L, width), lambda i, j: (i, 0)),
            pl.BlockSpec((width, width), lambda i, j: (0, 0)),
            pl.BlockSpec((width, step), lambda i, j: (0, j)),
            pl.BlockSpec((8, width), lambda i, j: (0, 0)),
            pl.BlockSpec((1, step), lambda i, j: (0, j)),
        ],
        out_specs=[
            pl.BlockSpec((L, width), lambda i, j: (i, 0)),
            pl.BlockSpec((L, 128), lambda i, j: (i, 0)),
            pl.BlockSpec((L, step), lambda i, j: (i, j)),
            pl.BlockSpec((L, step), lambda i, j: (i, j)),
        ],
        scratch_shapes=[pltpu.VMEM((L, width), BF)],
        compiler_params=params(),
        name="feed",
    )(rows, context, w_out, w_in, vectors, bias_in)


ROWS = 256


def turn_body(
    len_ref, gl_ref, gp_ref, u_ref, s_ref, r_ref, c_ref, wd_any, wi_any, wo_any, vec_ref,
    y_ref, dh_ref, do_ref, gv_ref, gi_ref, wd_ref, wi_ref, wo_ref, sems,
):
    index = pl.program_id(0)
    width = u_ref.shape[1]
    wide = gl_ref.shape[1]
    parts = 4
    step = wide // parts
    down = [
        pltpu.make_async_copy(
            wd_any.at[pl.ds(part * step, step)], wd_ref.at[pl.ds(part * step, step)], sems.at[part]
        )
        for part in range(parts)
    ]
    whole_in = pltpu.make_async_copy(wi_any, wi_ref, sems.at[parts])
    whole_out = pltpu.make_async_copy(wo_any, wo_ref, sems.at[parts + 1])

    @pl.when(index == 0)
    def _():
        for copy in down:
            copy.start()
        whole_in.start()
        whole_out.start()
        gv_ref[...] = jnp.zeros_like(gv_ref)
        gi_ref[...] = jnp.zeros_like(gi_ref)

    gain_one, beta_one, gain_two, beta_two, bias_down = (vec_ref[n : n + 1, :] for n in range(1, 6))
    normed = u_ref[...]
    total = normed + bias_down
    for part in range(parts):
        pl.when(index == 0)(down[part].wait)
        rows = slice(part * step, (part + 1) * step)
        total = total + dot(gl_ref[:, rows], wd_ref[rows, :], 1, 0)
    centered = total - jnp.mean(total, axis=1, keepdims=True)
    spread = lax.rsqrt(jnp.mean(centered * centered, axis=1, keepdims=True) + LN_EPS)
    hat = centered * spread
    y_ref[...] = (hat * gain_two + beta_two).astype(BF)
    per_seq = L // ROWS
    first = lax.rem(index, per_seq) * ROWS
    live = lax.broadcasted_iota(jnp.int32, (ROWS, 1), 0) + first < len_ref[index // per_seq]
    dy = jnp.where(live, c_ref[...].astype(F32), 0.0)
    gv_ref[4:5, :] += jnp.sum(dy, axis=0, keepdims=True)
    scaled = dy * gain_two
    d_two = spread * (
        scaled
        - jnp.mean(scaled, axis=1, keepdims=True)
        - hat * jnp.mean(scaled * hat, axis=1, keepdims=True)
    )
    d_branch = d_two.astype(BF)
    gv_ref[3:4, :] += jnp.sum(d_branch.astype(F32), axis=0, keepdims=True)
    pl.when(index == 0)(whole_in.wait)
    total = d_two
    half = step // 2
    for part in range(2 * parts):
        rows = slice(part * half, (part + 1) * half)
        d_hidden = dot(d_branch, wd_ref[rows, :], 1, 1) * gp_ref[:, rows].astype(F32)
        d_hidden = d_hidden.astype(BF)
        gi_ref[:, rows] += jnp.sum(d_hidden.astype(F32), axis=0, keepdims=True)
        total = total + dot(d_hidden, wi_ref[:, rows], 1, 1)
    gv_ref[2:3, :] += jnp.sum(total, axis=0, keepdims=True)
    scaled = total * gain_one
    hat = (normed - beta_one) * (1.0 / gain_one)
    d_one = s_ref[:, 0:1] * (
        scaled
        - jnp.mean(scaled, axis=1, keepdims=True)
        - hat * jnp.mean(scaled * hat, axis=1, keepdims=True)
    )
    dh_ref[...] = d_one
    d_att = d_one.astype(BF)
    gv_ref[1:2, :] += jnp.sum(d_att.astype(F32), axis=0, keepdims=True)
    pl.when(index == 0)(whole_out.wait)
    d_context = dot(d_att, wo_ref[...], 1, 1).astype(BF).astype(F32)
    gv_ref[0:1, :] += jnp.sum(d_context, axis=0, keepdims=True)
    do_ref[...] = (d_context * r_ref[...]).astype(BF)


def turn(lengths, gl, gp, normed, spread, inverse, cotangent, w_down, w_in, w_out, vectors):
    count, width = normed.shape
    wide = gl.shape[1]
    block = lambda cols: pl.BlockSpec((ROWS, cols), lambda i, n: (i, 0))
    anywhere = pl.BlockSpec(memory_space=pl.ANY)
    return pl.pallas_call(
        turn_body,
        out_shape=(
            shape_of((count, width), BF),
            shape_of((count, width), F32),
            shape_of((count, width), BF),
            shape_of((8, width), F32),
            shape_of((1, wide), F32),
        ),
        grid_spec=pltpu.PrefetchScalarGridSpec(
            num_scalar_prefetch=1,
            grid=(count // ROWS,),
            in_specs=[
                block(wide), block(wide), block(width), block(128), block(width), block(width),
                anywhere, anywhere, anywhere, pl.BlockSpec((8, width), lambda i, n: (0, 0)),
            ],
            out_specs=[
                block(width), block(width), block(width),
                pl.BlockSpec((8, width), lambda i, n: (0, 0)),
                pl.BlockSpec((1, wide), lambda i, n: (0, 0)),
            ],
            scratch_shapes=[
                pltpu.VMEM(w_down.shape, BF),
                pltpu.VMEM(w_in.shape, BF),
                pltpu.VMEM(w_out.shape, BF),
                pltpu.SemaphoreType.DMA((6,)),
            ],
        ),
        compiler_params=params(),
        name="turn",
    )(lengths, gl, gp, normed, spread, inverse, cotangent, w_down, w_in, w_out, vectors)


def back_body(
    q_ref, k_ref, v_ref, o_ref, do_ref, e_ref, dh_ref, w_any, dx_ref, gq_ref, all_ref, w_ref, sem
):
    seq, quad = pl.program_id(0), pl.program_id(1)
    quads = pl.num_programs(1)
    width = dh_ref.shape[1]
    whole = pltpu.make_async_copy(w_any, w_ref, sem)

    @pl.when((seq == 0) & (quad == 0))
    def _():
        whole.start()
        gq_ref[...] = jnp.zeros_like(gq_ref)

    halves = lane_halves(BF)
    halves_wide = lane_halves(F32)
    lane = lax.broadcasted_iota(jnp.int32, (L, 128), 1)
    for pair in range(QUAD // 128):
        part = slice(pair * 128, (pair + 1) * 128)
        q_pair, k_pair, v_pair, do_pair = (r[:, part] for r in (q_ref, k_ref, v_ref, do_ref))
        products = do_pair.astype(F32) * o_ref[:, part].astype(F32)
        shifts = [jnp.sum(products * half, axis=1, keepdims=True) for half in halves_wide]
        rough = [shift.astype(BF).astype(F32) for shift in shifts]
        side = jnp.where(
            lane == 0,
            -rough[0],
            jnp.where(
                lane == 1,
                rough[0] - shifts[0],
                jnp.where(lane == 2, -rough[1], jnp.where(lane == 3, rough[1] - shifts[1], 0.0)),
            ),
        ).astype(BF)
        left = jnp.concatenate([do_pair, side], axis=1)
        q_turned = q_pair.T
        do_turned = do_pair.T
        d_scores, d_keys, d_values = [], [], []
        for head in range(2):
            rows = slice(head * HD, (head + 1) * HD)
            power = e_ref[2 * pair + head]
            marks = jnp.where(lane // 2 == head, 1.0, 0.0).astype(BF)
            right = jnp.concatenate([v_pair * halves[head], marks], axis=1)
            d_score = (power.astype(F32) * dot(left, right, 1, 1)).astype(BF)
            d_scores.append(d_score)
            d_keys.append(dot(q_turned[rows], d_score, 1, 0))
            d_values.append(dot(do_turned[rows], power, 1, 0))
        right = jnp.concatenate([k_pair * half for half in halves], axis=0)
        d_query = (dot(jnp.concatenate(d_scores, axis=1), right, 1, 0) * (HD**-0.5)).astype(BF)
        cols = pl.multiple_of(quad * QUAD + pair * 128, 128)
        gq_ref[:, pl.ds(cols, 128)] += jnp.sum(d_query.astype(F32), axis=0, keepdims=True)
        all_ref[:, pl.ds(cols, 128)] = d_query
        all_ref[:, pl.ds(width + cols, 128)] = jnp.concatenate(d_keys, axis=0).T.astype(BF)
        all_ref[:, pl.ds(2 * width + cols, 128)] = jnp.concatenate(d_values, axis=0).T.astype(BF)

    pl.when((seq == 0) & (quad == quads - 1))(whole.wait)

    @pl.when(quad == quads - 1)
    def _():
        dx_ref[...] = (dh_ref[...] + dot(all_ref[...], w_ref[...], 1, 1)).astype(BF)


def back(qkv, context, d_context, powers, d_joined, w_qkv):
    count, width = d_joined.shape
    quads = width // QUAD
    heads = QUAD // HD
    col = lambda n: pl.BlockSpec((L, QUAD), lambda i, j: (i, n * quads + j))
    return pl.pallas_call(
        back_body,
        out_shape=(shape_of((count, width), BF), shape_of((1, width), F32)),
        grid=(count // L, quads),
        in_specs=[
            col(0), col(1), col(2), col(0), col(0),
            pl.BlockSpec((heads, L, L), lambda i, j: (i * quads + j, 0, 0)),
            pl.BlockSpec((L, width), lambda i, j: (i, 0)),
            pl.BlockSpec(memory_space=pl.ANY),
        ],
        out_specs=[
            pl.BlockSpec((L, width), lambda i, j: (i, 0)),
            pl.BlockSpec((1, width), lambda i, j: (0, 0)),
        ],
        scratch_shapes=[
            pltpu.VMEM((L, 3 * width), BF),
            pltpu.VMEM(w_qkv.shape, BF),
            pltpu.SemaphoreType.DMA,
        ],
        compiler_params=params(),
        name="back",
    )(qkv, qkv, qkv, context, d_context, powers, d_joined, w_qkv)


BOTH = ("dp", "fsdp")


def on_device(
    tokens, lengths, w_qkv, w_out, w_in, w_down, gain_one, gain_two,
    bias_q, bias_v, bias_out, beta_one, bias_in, bias_down, beta_two, cotangent,
):
    width = w_out.shape[1]
    full_qkv = lax.all_gather(w_qkv, BOTH, axis=0, tiled=True)
    full_out = lax.all_gather(w_out, BOTH, axis=0, tiled=True)
    full_in = lax.all_gather(w_in, BOTH, axis=0, tiled=True)
    full_down = lax.all_gather(w_down, BOTH, axis=0, tiled=True)
    score_scale = HD**-0.5
    ones = jnp.ones((width,), F32)
    zeros = jnp.zeros((width,), F32)
    bias = jnp.concatenate([bias_q, zeros, bias_v])[None]
    scale = jnp.concatenate([ones * score_scale, ones, ones])[None]
    vectors = jnp.stack([bias_out, gain_one, beta_one, gain_two, beta_two, bias_down, zeros, zeros])
    qkv = project(tokens, full_qkv, bias, scale)
    context, powers, inverse = attend(lengths, qkv, width)
    normed, spread, gl, gp = feed(tokens, context, full_out, full_in, vectors, bias_in[None])
    output, d_joined, d_context, sums, sum_in = turn(
        lengths, gl, gp, normed, spread, inverse, cotangent, full_down, full_in, full_out, vectors
    )
    input_grad, sum_q = back(qkv, context, d_context, powers, d_joined, full_qkv)
    parts = (sum_q[0], sums[0], sums[1], sums[2], sum_in[0], sums[3], sums[4])
    shares = lax.psum_scatter(parts, BOTH, scatter_dimension=0, tiled=True)
    return (output, input_grad, *shares)


def solution(mesh):
    split, rows, copied = P(BOTH), P(BOTH, None), P()
    in_specs = (rows, split, rows, rows, rows, rows, *([copied] * 9), rows)
    out_specs = (rows, rows, *([split] * 7))
    return jax.shard_map(
        on_device, mesh=mesh, in_specs=in_specs, out_specs=out_specs, check_vma=False
    )
```

```python
import functools
import math

import jax
import jax.numpy as jnp
from jax import lax
from jax.experimental import pallas as pl
from jax.experimental.pallas import tpu as pltpu
from jax.sharding import PartitionSpec as P

HD = 64
L = 512
LN_EPS = 1e-12
MIB = 2**20
BF = jnp.bfloat16
F32 = jnp.float32


def params(limit=60, semantics=None):
    return pltpu.CompilerParams(vmem_limit_bytes=limit * MIB, dimension_semantics=semantics)


def dot(left, right, on_left, on_right):
    return lax.dot_general(
        left, right, (((on_left,), (on_right,)), ((), ())), preferred_element_type=F32
    )


def shape_of(dims, kind):
    return jax.ShapeDtypeStruct(dims, kind)


def cost(flops):
    return pl.CostEstimate(flops=flops, bytes_accessed=0, transcendentals=0)


def issue(sources, buf, sem, place, height):
    plane_at, z_at, core_at = place
    cols = buf.shape[1]
    for source, tag in sources:
        if tag is None:
            pltpu.make_async_copy(source, buf, sem).start()
            continue
        chip, zs, first, turned = tag
        tall = source.shape[0] // len(zs)
        for step, z in enumerate(zs):
            row = ((plane_at ^ chip) * 8 + (z_at ^ z) * 2 + (core_at ^ turned)) * height
            for block in range(height // tall):
                pltpu.make_async_copy(
                    source.at[pl.ds(step * tall, tall), pl.ds(first + block * cols, cols)],
                    buf.at[pl.ds(pl.multiple_of(row + block * tall, tall), tall)],
                    sem,
                ).start()


def settle(buf, sem):
    pltpu.make_async_copy(buf, buf, sem).wait()


def tagged(refs, tags):
    return list(zip(refs, tags))


def tags_of(sources):
    return [tag for _, tag in sources]


def arrays_of(sources):
    return [array for array, _ in sources]


def place_of(scalars, seqs):
    return scalars[seqs], scalars[seqs + 1], scalars[seqs + 2]


ANYWHERE = pl.BlockSpec(memory_space=pl.ANY)

def pack_body(qkv_ref, out_ref, in_ref, down_ref, own_ref, feed_ref):
    height = qkv_ref.shape[0]
    at = 0
    for ref in (qkv_ref, out_ref, in_ref):
        own_ref[:, at : at + ref.shape[1]] = ref[...]
        at += ref.shape[1]
    for first in range(0, down_ref.shape[0], height):
        own_ref[:, at : at + down_ref.shape[1]] = down_ref[first : first + height, :]
        at += down_ref.shape[1]
    feed_ref[:, : out_ref.shape[1]] = out_ref[...]
    feed_ref[:, out_ref.shape[1] :] = in_ref[...]


def pack(w_qkv, w_out, w_in, w_down):
    height = w_qkv.shape[0]
    feed_wide = w_out.shape[1] + w_in.shape[1]
    wide = w_qkv.shape[1] + feed_wide + w_down.shape[0] // height * w_down.shape[1]
    return pl.pallas_call(
        pack_body,
        out_shape=(shape_of((height, wide), BF), shape_of((height, feed_wide), BF)),
        compiler_params=params(20),
        name="pack",
    )(w_qkv, w_out, w_in, w_down)


def project_body(seqs, tags, len_ref, x_ref, bias_ref, scale_ref, *refs):
    sources, (out_ref, buf, sem) = tagged(refs, tags), refs[len(tags) :]

    @pl.when(pl.program_id(0) == 0)
    def _():
        issue(sources, buf, sem, place_of(len_ref, seqs), buf.shape[0] // 32)
        settle(buf, sem)

    step = out_ref.shape[1]
    cols = pl.ds(pl.multiple_of(pl.program_id(0) * step, step), step)
    total = dot(x_ref[...], buf[:, cols], 1, 0) + bias_ref[...]
    out_ref[...] = (total * scale_ref[...]).astype(BF)


def project(scalars, seqs, rows, sources, bias, scale):
    count, width = rows.shape
    wide = bias.shape[1]
    step = 1024
    return pl.pallas_call(
        functools.partial(project_body, seqs, tags_of(sources)),
        out_shape=shape_of((count, wide), BF),
        grid_spec=pltpu.PrefetchScalarGridSpec(
            num_scalar_prefetch=1,
            grid=(wide // step,),
            in_specs=[
                pl.BlockSpec((count, width), lambda j, n: (0, 0)),
                pl.BlockSpec((1, step), lambda j, n: (0, j)),
                pl.BlockSpec((1, step), lambda j, n: (0, j)),
                *([ANYWHERE] * len(sources)),
            ],
            out_specs=pl.BlockSpec((count, step), lambda j, n: (0, j)),
            scratch_shapes=[pltpu.VMEM((width, wide), BF), pltpu.SemaphoreType.DMA],
        ),
        compiler_params=params(),
        cost_estimate=cost(2 * count * width * wide),
        name="project",
    )(scalars, rows, bias, scale, *arrays_of(sources))


def lane_halves(kind):
    lane = lax.broadcasted_iota(jnp.int32, (1, 128), 1)
    return [(lane < HD).astype(F32).astype(kind), (lane >= HD).astype(F32).astype(kind)]


QUAD = 256


def attend_body(seq, len_ref, q_ref, k_ref, v_ref, *refs):
    o_ref, e_ref, r_ref = refs[-3:]
    length = len_ref[seq]
    halves = lane_halves(BF)
    lane = lax.broadcasted_iota(jnp.int32, (L, 128), 1)
    row = lax.broadcasted_iota(jnp.int32, (L, 128), 0)
    q_side = jnp.where(lane == 0, 1.0, 0.0).astype(BF)
    k_side = jnp.where((lane == 0) & (row >= length), -1e30, 0.0).astype(BF)
    for pair in range(QUAD // 128):
        part = slice(pair * 128, (pair + 1) * 128)
        q_pair = jnp.concatenate([q_ref[:, part], q_side], axis=1)
        k_pair = k_ref[:, part]
        v_pair = v_ref[:, part]
        powers = []
        for head in range(2):
            k_one = jnp.concatenate([k_pair * halves[head], k_side], axis=1)
            scores = dot(q_pair, k_one, 1, 1)
            peak = jnp.max(scores, axis=1, keepdims=True)
            power = jnp.exp(scores - peak).astype(BF)
            e_ref[2 * pair + head] = power
            powers.append(power)
        right = jnp.concatenate(
            [
                jnp.concatenate([v_pair * half, jnp.broadcast_to(half, (L, 128))], axis=1)
                for half in halves
            ],
            axis=0,
        )
        both = dot(jnp.concatenate(powers, axis=1), right, 1, 0)
        inverse = 1.0 / both[:, 128:]
        r_ref[:, part] = inverse
        o_ref[:, part] = (both[:, :128] * inverse).astype(BF)


def attend(scalars, qkv, width, seq, earlier):
    count = qkv.shape[0]
    quads = width // QUAD
    heads = QUAD // HD
    return pl.pallas_call(
        functools.partial(attend_body, seq),
        out_shape=(
            shape_of((count, width), BF),
            shape_of((count // L * width // HD, L, L), BF),
            shape_of((count, width), F32),
        ),
        grid_spec=pltpu.PrefetchScalarGridSpec(
            num_scalar_prefetch=1,
            grid=(quads,),
            in_specs=[
                pl.BlockSpec((L, QUAD), lambda j, n: (seq, j)),
                pl.BlockSpec((L, QUAD), lambda j, n: (seq, quads + j)),
                pl.BlockSpec((L, QUAD), lambda j, n: (seq, 2 * quads + j)),
                *([ANYWHERE] * len(earlier)),
            ],
            out_specs=[
                pl.BlockSpec((L, QUAD), lambda j, n: (seq, j)),
                pl.BlockSpec((heads, L, L), lambda j, n: (seq * quads + j, 0, 0)),
                pl.BlockSpec((L, QUAD), lambda j, n: (seq, j)),
            ],
        ),
        compiler_params=params(),
        input_output_aliases={4 + n: n for n in range(len(earlier))},
        cost_estimate=cost(16 * L * width * L),
        name="attend",
    )(scalars, qkv, qkv, qkv, *earlier)


ROWS = 256


def feed_body(seqs, tags, len_ref, x_ref, o_ref, vec_ref, bi_ref, *refs):
    sources, (u_ref, s_ref, gl_ref, gp_ref, buf, sem) = tagged(refs, tags), refs[-6:]

    @pl.when(pl.program_id(0) == 0)
    def _():
        issue(sources, buf, sem, place_of(len_ref, seqs), buf.shape[0] // 32)
        settle(buf, sem)

    width = x_ref.shape[1]
    joined = dot(o_ref[...], buf[:, :width], 1, 0) + vec_ref[0:1, :] + x_ref[...].astype(F32)
    centered = joined - jnp.mean(joined, axis=1, keepdims=True)
    spread = lax.rsqrt(jnp.mean(centered * centered, axis=1, keepdims=True) + LN_EPS)
    normed = centered * spread * vec_ref[1:2, :] + vec_ref[2:3, :]
    u_ref[...] = normed
    s_ref[...] = jnp.broadcast_to(spread, s_ref.shape)
    rounded = normed.astype(BF)
    step = 512
    for part in range(gl_ref.shape[1] // step):
        cols = slice(part * step, (part + 1) * step)
        pre = dot(rounded, buf[:, width + part * step : width + (part + 1) * step], 1, 0)
        pre = pre + bi_ref[:, cols]
        phi = 0.5 + 0.5 * lax.erf(pre * math.sqrt(0.5))
        slope = phi + pre * jnp.exp(-0.5 * pre * pre) * (1.0 / math.sqrt(2.0 * math.pi))
        gl_ref[:, cols] = (pre * phi).astype(BF)
        gp_ref[:, cols] = slope.astype(BF)


def feed(scalars, seqs, rows, context, sources, vectors, bias_in, seq, earlier):
    count, width = rows.shape
    wide = bias_in.shape[1]
    steps = L // ROWS
    block = lambda cols: pl.BlockSpec((ROWS, cols), lambda i, n: (seq * steps + i, 0))
    return pl.pallas_call(
        functools.partial(feed_body, seqs, tags_of(sources)),
        out_shape=(
            shape_of((count, width), F32),
            shape_of((count, 128), F32),
            shape_of((count, wide), BF),
            shape_of((count, wide), BF),
        ),
        grid_spec=pltpu.PrefetchScalarGridSpec(
            num_scalar_prefetch=1,
            grid=(steps,),
            in_specs=[
                block(width),
                block(width),
                pl.BlockSpec((8, width), lambda i, n: (0, 0)),
                pl.BlockSpec((1, wide), lambda i, n: (0, 0)),
                *([ANYWHERE] * (len(sources) + len(earlier))),
            ],
            out_specs=[block(width), block(128), block(wide), block(wide)],
            scratch_shapes=[pltpu.VMEM((width, width + wide), BF), pltpu.SemaphoreType.DMA],
        ),
        compiler_params=params(),
        input_output_aliases={5 + len(sources) + n: n for n in range(len(earlier))},
        cost_estimate=cost(2 * L * width * (width + wide)),
        name="feed",
    )(scalars, rows, context, vectors, bias_in, *arrays_of(sources), *earlier)


def turn_body(
    seqs, feed_tags, down_tags, len_ref, gl_ref, gp_ref, u_ref, s_ref, r_ref, c_ref, vec_ref, *refs
):
    feeds, downs = tagged(refs, feed_tags), tagged(refs[len(feed_tags) :], down_tags)
    y_ref, dh_ref, do_ref, gv_ref, gi_ref, buf, down, sems = refs[-8:]
    index = pl.program_id(0)
    width = u_ref.shape[1]
    wide = gl_ref.shape[1]
    parts = 4
    step = wide // parts

    @pl.when(index == 0)
    def _():
        place = place_of(len_ref, seqs)
        issue(downs, down, sems.at[0], place, wide // 32)
        issue(feeds, buf, sems.at[1], place, width // 32)
        gv_ref[...] = jnp.zeros_like(gv_ref)
        gi_ref[...] = jnp.zeros_like(gi_ref)
        settle(down, sems.at[0])

    gain_one, beta_one, gain_two, beta_two, bias_down = (vec_ref[n : n + 1, :] for n in range(1, 6))
    normed = u_ref[...]
    total = normed + bias_down
    for part in range(parts):
        rows = slice(part * step, (part + 1) * step)
        total = total + dot(gl_ref[:, rows], down[rows, :], 1, 0)
    centered = total - jnp.mean(total, axis=1, keepdims=True)
    spread = lax.rsqrt(jnp.mean(centered * centered, axis=1, keepdims=True) + LN_EPS)
    hat = centered * spread
    y_ref[...] = (hat * gain_two + beta_two).astype(BF)
    per_seq = L // ROWS
    first = lax.rem(index, per_seq) * ROWS
    live = lax.broadcasted_iota(jnp.int32, (ROWS, 1), 0) + first < len_ref[index // per_seq]
    dy = jnp.where(live, c_ref[...].astype(F32), 0.0)
    gv_ref[4:5, :] += jnp.sum(dy, axis=0, keepdims=True)
    scaled = dy * gain_two
    d_two = spread * (
        scaled
        - jnp.mean(scaled, axis=1, keepdims=True)
        - hat * jnp.mean(scaled * hat, axis=1, keepdims=True)
    )
    d_branch = d_two.astype(BF)
    gv_ref[3:4, :] += jnp.sum(d_branch.astype(F32), axis=0, keepdims=True)
    pl.when(index == 0)(functools.partial(settle, buf, sems.at[1]))
    total = d_two
    half = step // 2
    for part in range(2 * parts):
        rows = slice(part * half, (part + 1) * half)
        d_hidden = dot(d_branch, down[rows, :], 1, 1) * gp_ref[:, rows].astype(F32)
        d_hidden = d_hidden.astype(BF)
        gi_ref[:, rows] += jnp.sum(d_hidden.astype(F32), axis=0, keepdims=True)
        total = total + dot(d_hidden, buf[:, width + part * half : width + (part + 1) * half], 1, 1)
    gv_ref[2:3, :] += jnp.sum(total, axis=0, keepdims=True)
    scaled = total * gain_one
    hat = (normed - beta_one) * (1.0 / gain_one)
    d_one = s_ref[:, 0:1] * (
        scaled
        - jnp.mean(scaled, axis=1, keepdims=True)
        - hat * jnp.mean(scaled * hat, axis=1, keepdims=True)
    )
    dh_ref[...] = d_one
    d_att = d_one.astype(BF)
    gv_ref[1:2, :] += jnp.sum(d_att.astype(F32), axis=0, keepdims=True)
    d_context = dot(d_att, buf[:, :width], 1, 1).astype(BF).astype(F32)
    gv_ref[0:1, :] += jnp.sum(d_context, axis=0, keepdims=True)
    do_ref[...] = (d_context * r_ref[...]).astype(BF)


def turn(scalars, seqs, gl, gp, normed, spread, inverse, cotangent, feeds, downs, vectors):
    count, width = normed.shape
    wide = gl.shape[1]
    block = lambda cols: pl.BlockSpec((ROWS, cols), lambda i, n: (i, 0))
    return pl.pallas_call(
        functools.partial(turn_body, seqs, tags_of(feeds), tags_of(downs)),
        out_shape=(
            shape_of((count, width), BF),
            shape_of((count, width), F32),
            shape_of((count, width), BF),
            shape_of((8, width), F32),
            shape_of((1, wide), F32),
        ),
        grid_spec=pltpu.PrefetchScalarGridSpec(
            num_scalar_prefetch=1,
            grid=(count // ROWS,),
            in_specs=[
                block(wide),
                block(wide),
                block(width),
                block(128),
                block(width),
                block(width),
                pl.BlockSpec((8, width), lambda i, n: (0, 0)),
                *([ANYWHERE] * (len(feeds) + len(downs))),
            ],
            out_specs=[
                block(width),
                block(width),
                block(width),
                pl.BlockSpec((8, width), lambda i, n: (0, 0)),
                pl.BlockSpec((1, wide), lambda i, n: (0, 0)),
            ],
            scratch_shapes=[
                pltpu.VMEM((width, width + wide), BF),
                pltpu.VMEM((wide, width), BF),
                pltpu.SemaphoreType.DMA((2,)),
            ],
        ),
        compiler_params=params(),
        cost_estimate=cost(2 * count * width * (width + 3 * wide)),
        name="turn",
    )(scalars, gl, gp, normed, spread, inverse, cotangent, vectors, *arrays_of(feeds), *arrays_of(downs))


def back_body(
    seqs, tags, len_ref, q_ref, k_ref, v_ref, o_ref, do_ref, e_ref, dh_ref, *refs
):
    sources, (dx_ref, gq_ref, all_ref, w_ref, sem) = tagged(refs, tags), refs[len(tags) :]
    seq, quad = pl.program_id(0), pl.program_id(1)
    quads = pl.num_programs(1)
    width = dh_ref.shape[1]

    @pl.when((seq == 0) & (quad == 0))
    def _():
        issue(sources, w_ref, sem, place_of(len_ref, seqs), width // 32)
        gq_ref[...] = jnp.zeros_like(gq_ref)

    halves = lane_halves(BF)
    halves_wide = lane_halves(F32)
    lane = lax.broadcasted_iota(jnp.int32, (L, 128), 1)
    for pair in range(QUAD // 128):
        part = slice(pair * 128, (pair + 1) * 128)
        q_pair, k_pair, v_pair, do_pair = (r[:, part] for r in (q_ref, k_ref, v_ref, do_ref))
        products = do_pair.astype(F32) * o_ref[:, part].astype(F32)
        shifts = [jnp.sum(products * half, axis=1, keepdims=True) for half in halves_wide]
        rough = [shift.astype(BF).astype(F32) for shift in shifts]
        side = jnp.where(
            lane == 0,
            -rough[0],
            jnp.where(
                lane == 1,
                rough[0] - shifts[0],
                jnp.where(lane == 2, -rough[1], jnp.where(lane == 3, rough[1] - shifts[1], 0.0)),
            ),
        ).astype(BF)
        left = jnp.concatenate([do_pair, side], axis=1)
        q_turned = q_pair.T
        do_turned = do_pair.T
        d_scores, d_keys, d_values = [], [], []
        for head in range(2):
            rows = slice(head * HD, (head + 1) * HD)
            power = e_ref[2 * pair + head]
            marks = jnp.where(lane // 2 == head, 1.0, 0.0).astype(BF)
            right = jnp.concatenate([v_pair * halves[head], marks], axis=1)
            d_score = (power.astype(F32) * dot(left, right, 1, 1)).astype(BF)
            d_scores.append(d_score)
            d_keys.append(dot(q_turned[rows], d_score, 1, 0))
            d_values.append(dot(do_turned[rows], power, 1, 0))
        right = jnp.concatenate([k_pair * half for half in halves], axis=0)
        d_query = (dot(jnp.concatenate(d_scores, axis=1), right, 1, 0) * (HD**-0.5)).astype(BF)
        cols = pl.multiple_of(quad * QUAD + pair * 128, 128)
        gq_ref[:, pl.ds(cols, 128)] += jnp.sum(d_query.astype(F32), axis=0, keepdims=True)
        all_ref[:, pl.ds(cols, 128)] = d_query
        all_ref[:, pl.ds(width + cols, 128)] = jnp.concatenate(d_keys, axis=0).T.astype(BF)
        all_ref[:, pl.ds(2 * width + cols, 128)] = jnp.concatenate(d_values, axis=0).T.astype(BF)

    pl.when((seq == 0) & (quad == quads - 1))(functools.partial(settle, w_ref, sem))

    @pl.when(quad == quads - 1)
    def _():
        dx_ref[...] = (dh_ref[...] + dot(all_ref[...], w_ref[...], 1, 1)).astype(BF)


def back(scalars, seqs, qkv, context, d_context, powers, d_joined, sources):
    count, width = d_joined.shape
    quads = width // QUAD
    heads = QUAD // HD
    col = lambda n: pl.BlockSpec((L, QUAD), lambda i, j, s: (i, n * quads + j))
    return pl.pallas_call(
        functools.partial(back_body, seqs, tags_of(sources)),
        out_shape=(shape_of((count, width), BF), shape_of((1, width), F32)),
        grid_spec=pltpu.PrefetchScalarGridSpec(
            num_scalar_prefetch=1,
            grid=(seqs, quads),
            in_specs=[
                col(0),
                col(1),
                col(2),
                col(0),
                col(0),
                pl.BlockSpec((heads, L, L), lambda i, j, s: (i * quads + j, 0, 0)),
                pl.BlockSpec((L, width), lambda i, j, s: (i, 0)),
                *([ANYWHERE] * len(sources)),
            ],
            out_specs=[
                pl.BlockSpec((L, width), lambda i, j, s: (i, 0)),
                pl.BlockSpec((1, width), lambda i, j, s: (0, 0)),
            ],
            scratch_shapes=[
                pltpu.VMEM((L, 3 * width), BF),
                pltpu.VMEM((width, 3 * width), BF),
                pltpu.SemaphoreType.DMA,
            ],
        ),
        compiler_params=params(),
        cost_estimate=cost(2 * count * width * 3 * width + 20 * count * width * L),
        name="back",
    )(scalars, qkv, qkv, qkv, context, d_context, powers, d_joined, *arrays_of(sources))


BOTH = ("dp", "fsdp")


def hop(block, axis, flip):
    size = lax.axis_size(axis)
    return lax.ppermute(block, axis, [(i, i ^ flip) for i in range(size)])


def over_x(block):
    return hop(block, "dp", 1)


def over_y(block):
    return hop(block, "dp", 2)


def over_core(block):
    return hop(block, "fsdp", 1)


def over_z(block, k):
    return hop(block, "fsdp", 2 * k)


def after(value, *earlier):
    return lax.optimization_barrier((value, *earlier))[0]


MOVES = {
    "x": over_x,
    "y": over_y,
    "c": over_core,
    "1": functools.partial(over_z, k=1),
    "2": functools.partial(over_z, k=2),
    "3": functools.partial(over_z, k=3),
}


def stage(lanes, blocks, *earlier):
    blocks = after(tuple(blocks), *earlier)
    return lax.optimization_barrier(tuple(MOVES[lane](block) for lane, block in zip(lanes, blocks)))


def both(mine, others):
    return [(array, (*tag, 0)) for array, tag in mine] + [
        (array, (*tag, 1)) for array, (_, tag) in zip(others, mine)
    ]


def stack(*blocks):
    return jnp.concatenate(blocks, axis=0)


def whole(array):
    return [(array, None)]


def reduce_shares(block, slots):
    dp, fsdp = lax.axis_size("dp"), lax.axis_size("fsdp")
    block = block.reshape(dp, fsdp, slots)
    for axis, dim in (("dp", 0), ("fsdp", 0)):
        size = lax.axis_size(axis)
        at = lax.axis_index(axis)
        pick = lambda k: lax.dynamic_index_in_dim(block, at ^ k, 0, keepdims=False)
        block = functools.reduce(
            lambda left, right: left + right, [pick(0)] + [hop(pick(k), axis, k) for k in range(1, size)]
        )
    return block


def on_device(
    tokens, lengths, w_qkv, w_out, w_in, w_down, gain_one, gain_two,
    bias_q, bias_v, bias_out, beta_one, bias_in, bias_down, beta_two, cotangent,
):
    width = w_out.shape[1]
    seqs = lengths.shape[0]
    chip = lax.axis_index("fsdp")
    scalars = jnp.concatenate(
        [lengths, jnp.stack([lax.axis_index("dp"), chip // 2, chip % 2]).astype(jnp.int32)]
    )
    score_scale = HD**-0.5
    ones = jnp.ones((width,), F32)
    zeros = jnp.zeros((width,), F32)
    bias = jnp.concatenate([bias_q, zeros, bias_v])[None]
    scale = jnp.concatenate([ones * score_scale, ones, ones])[None]
    vectors = jnp.stack([bias_out, gain_one, beta_one, gain_two, beta_two, bias_down, zeros, zeros])
    special = (lax.axis_size("dp"), lax.axis_size("fsdp")) == (4, 8)
    if special:
        own, w_feed = pack(w_qkv, w_out, w_in, w_down)
        at_feed = w_qkv.shape[1]
        at_down = at_feed + w_feed.shape[1]
        z_one, z_two, z_three, near_x, near_y = stage("123xy", (w_qkv, w_qkv, w_qkv, own, own))
        far = stack(z_one, z_two, z_three)
        x_far, y_far, feed_two, own_core, near_x_core = stage(
            "xy2cc", (far, far, w_feed, own, near_x)
        )
        left = stack(near_x[:, :at_feed], x_far[:32])
        crossed, crossed_more, feed_one, near_y_core, far_core = stage(
            "yx1cc", (left, y_far[32:], w_feed, near_y, far), feed_two, own_core, near_x_core
        )
        x_far_core, y_far_core, crossed_core, crossed_more_core = stage(
            "cccc", (x_far, y_far, crossed, crossed_more), feed_one, near_y_core, far_core
        )
        near = (own, near_x, near_y)
        near_core = (own_core, near_x_core, near_y_core)
        rest = (1, 2, 3)
        qkv_parts = both(
            [
                *((array, (chip, (0,), 0)) for chip, array in enumerate(near)),
                (far, (0, rest, 0)),
                (x_far, (1, rest, 0)),
                (y_far, (2, rest, 0)),
                (crossed, (3, (0, 1), 0)),
                (crossed_more, (3, (2, 3), 0)),
            ],
            [*near_core, far_core, x_far_core, y_far_core, crossed_core, crossed_more_core],
        )
        pair = stack(feed_one, feed_two)
        x_pair, y_pair, feed_three, pair_core = stage(
            "xy3c", (pair, pair, w_feed, pair), y_far_core, crossed_core, crossed_more_core
        )
        first = after(tokens, pair)
    else:
        first = tokens
        w_feed = jnp.concatenate([w_out, w_in], axis=1)
        qkv_parts = whole(lax.all_gather(w_qkv, BOTH, axis=0, tiled=True))
        feed_parts = whole(lax.all_gather(w_feed, BOTH, axis=0, tiled=True))
        down_parts = whole(lax.all_gather(w_down, BOTH, axis=0, tiled=True))
    qkv = project(scalars, seqs, first, qkv_parts, bias, scale)
    if special:
        x_last, y_last, cross_down, down_one, down_two = stage(
            "xyy12", (feed_three, feed_three, near_x[:, at_down:], w_down, w_down), qkv, pair_core
        )
    attended = []
    for seq in range(seqs):
        if special and seq == 1:
            x_last, y_last, *attended = after((x_last, y_last, *attended), cross_down, down_one)
            left = stack(near_x[:, at_feed:at_down], x_pair[:32])
            crossed, crossed_more, down_three, x_pair_core, y_pair_core = stage(
                "yx3cc", (left, stack(y_pair[32:], y_last), w_down, x_pair, y_pair), x_last, *attended
            )
        attended = attend(scalars, qkv, width, seq, attended)
    context, powers, inverse = attended
    if special:
        cores = stage(
            "ccccc", (feed_three, x_last, y_last, crossed, crossed_more), context, down_three
        )
        feed_parts = both(
            [
                *((array, (chip, (0,), at_feed)) for chip, array in enumerate(near)),
                (pair, (0, (1, 2), 0)),
                (x_pair, (1, (1, 2), 0)),
                (y_pair, (2, (1, 2), 0)),
                (feed_three, (0, (3,), 0)),
                (x_last, (1, (3,), 0)),
                (y_last, (2, (3,), 0)),
                (crossed, (3, (0, 1), 0)),
                (crossed_more, (3, (2, 3), 0)),
            ],
            [*near_core, pair_core, x_pair_core, y_pair_core, *cores],
        )
        far = stack(down_one, down_two, down_three)
        x_far, y_far, *diagonal = stage(
            "xy123", (far, far, cross_down, cross_down, cross_down), *cores
        )
    fed = []
    for seq in range(seqs):
        fed = feed(scalars, seqs, tokens, context, feed_parts, vectors, bias_in[None], seq, fed)
        if special and seq == 0:
            x_far, cross_down, *fed = after((x_far, cross_down, *fed), y_far, *diagonal)
    normed, spread, gl, gp = fed
    if special:
        mine = [
            (after(far, x_far), (0, rest, 0)),
            (x_far, (1, rest, 0)),
            (y_far, (2, rest, 0)),
            (cross_down, (3, (0,), 0)),
            *((block, (3, (k,), 0)) for block, k in zip(diagonal, rest)),
        ]
        down_parts = both(
            [*((array, (chip, (0,), at_down)) for chip, array in enumerate(near)), *mine],
            [*near_core, *(over_core(block) for block, _ in mine)],
        )
    output, d_joined, d_context, sums, sum_in = turn(
        scalars, seqs, gl, gp, normed, spread, inverse, cotangent, feed_parts, down_parts, vectors
    )
    input_grad, sum_q = back(scalars, seqs, qkv, context, d_context, powers, d_joined, qkv_parts)
    devices = lax.axis_size("dp") * lax.axis_size("fsdp")
    parts = (sum_q[0], sums[0], sums[1], sums[2], sum_in[0], sums[3], sums[4])
    rows = jnp.concatenate([part.reshape(devices, -1) for part in parts], axis=1)
    mine = reduce_shares(rows, rows.shape[1])
    shares, at = [], 0
    for part in parts:
        shares.append(mine[at : at + part.shape[0] // devices])
        at += part.shape[0] // devices
    return (output, input_grad, *shares)


def solution(mesh):
    split, rows, copied = P(BOTH), P(BOTH, None), P()
    in_specs = (rows, split, rows, rows, rows, rows, *([copied] * 9), rows)
    out_specs = (rows, rows, *([split] * 7))
    return jax.shard_map(
        on_device, mesh=mesh, in_specs=in_specs, out_specs=out_specs, check_vma=False
    )
```

```python
import functools
import math

import jax
import jax.numpy as jnp
from jax import lax
from jax.experimental import pallas as pl
from jax.experimental.pallas import tpu as pltpu
from jax.sharding import PartitionSpec as P

HD = 64
L = 512
LN_EPS = 1e-12
MIB = 2**20
BF = jnp.bfloat16
F32 = jnp.float32


def params(limit=60, semantics=None):
    return pltpu.CompilerParams(vmem_limit_bytes=limit * MIB, dimension_semantics=semantics)


def dot(left, right, on_left, on_right):
    return lax.dot_general(
        left, right, (((on_left,), (on_right,)), ((), ())), preferred_element_type=F32
    )


def shape_of(dims, kind):
    return jax.ShapeDtypeStruct(dims, kind)


def cost(flops):
    return pl.CostEstimate(flops=flops, bytes_accessed=0, transcendentals=0)


def issue(sources, buf, sem, place, height, window=0):
    plane_at, z_at, core_at = place
    cols = buf.shape[1]
    for source, tag in sources:
        if tag is None:
            pltpu.make_async_copy(source.at[:, pl.ds(window, cols)], buf, sem).start()
            continue
        chip, zs, first, turned = tag
        tall = source.shape[0] // len(zs)
        for step, z in enumerate(zs):
            row = ((plane_at ^ chip) * 8 + (z_at ^ z) * 2 + (core_at ^ turned)) * height
            for block in range(height // tall):
                pltpu.make_async_copy(
                    source.at[pl.ds(step * tall, tall), pl.ds(first + window + block * cols, cols)],
                    buf.at[pl.ds(pl.multiple_of(row + block * tall, tall), tall)],
                    sem,
                ).start()


def settle(buf, sem):
    pltpu.make_async_copy(buf, buf, sem).wait()


def tagged(refs, tags):
    return list(zip(refs, tags))


def tags_of(sources):
    return [tag for _, tag in sources]


def arrays_of(sources):
    return [array for array, _ in sources]


def place_of(scalars, seqs):
    return scalars[seqs], scalars[seqs + 1], scalars[seqs + 2]


ANYWHERE = pl.BlockSpec(memory_space=pl.ANY)

def pack_body(qkv_ref, out_ref, in_ref, down_ref, own_ref, feed_ref):
    height = qkv_ref.shape[0]
    at = 0
    for ref in (qkv_ref, out_ref, in_ref):
        own_ref[:, at : at + ref.shape[1]] = ref[...]
        at += ref.shape[1]
    for first in range(0, down_ref.shape[0], height):
        own_ref[:, at : at + down_ref.shape[1]] = down_ref[first : first + height, :]
        at += down_ref.shape[1]
    feed_ref[:, : out_ref.shape[1]] = out_ref[...]
    feed_ref[:, out_ref.shape[1] :] = in_ref[...]


def pack(w_qkv, w_out, w_in, w_down):
    height = w_qkv.shape[0]
    feed_wide = w_out.shape[1] + w_in.shape[1]
    wide = w_qkv.shape[1] + feed_wide + w_down.shape[0] // height * w_down.shape[1]
    return pl.pallas_call(
        pack_body,
        out_shape=(shape_of((height, wide), BF), shape_of((height, feed_wide), BF)),
        compiler_params=params(20),
        name="pack",
    )(w_qkv, w_out, w_in, w_down)


def glue_body(plans, count, *refs):
    sources, targets = refs[:count], refs[count:]
    for plan, target in zip(plans, targets):
        at = 0
        for number, top, rows, left in plan:
            target[at : at + rows, :] = sources[number][top : top + rows, left : left + target.shape[1]]
            at += rows


def glue(arrays, *plans):
    return pl.pallas_call(
        functools.partial(glue_body, [plan[1:] for plan in plans], len(arrays)),
        out_shape=[shape_of((sum(w[2] for w in plan[1:]), plan[0]), BF) for plan in plans],
        compiler_params=params(20),
        name="glue",
    )(*arrays)


def project_body(seqs, tags, len_ref, x_ref, bias_ref, scale_ref, *refs):
    sources, (out_ref, buf, sems) = tagged(refs, tags), refs[len(tags) :]
    here = pl.program_id(0)
    step = out_ref.shape[1]

    @pl.when(here == 0)
    def _():
        place = place_of(len_ref, seqs)
        for part in range(buf.shape[0]):
            issue(sources, buf.at[part], sems.at[part], place, buf.shape[1] // 32, part * step)

    settle(buf.at[here], sems.at[here])
    total = dot(x_ref[...], buf[here], 1, 0) + bias_ref[...]
    out_ref[...] = (total * scale_ref[...]).astype(BF)


def project(scalars, seqs, rows, sources, bias, scale):
    count, width = rows.shape
    wide = bias.shape[1]
    step = PROJECT
    return pl.pallas_call(
        functools.partial(project_body, seqs, tags_of(sources)),
        out_shape=shape_of((count, wide), BF),
        grid_spec=pltpu.PrefetchScalarGridSpec(
            num_scalar_prefetch=1,
            grid=(wide // step,),
            in_specs=[
                pl.BlockSpec((count, width), lambda j, n: (0, 0)),
                pl.BlockSpec((1, step), lambda j, n: (0, j)),
                pl.BlockSpec((1, step), lambda j, n: (0, j)),
                *([ANYWHERE] * len(sources)),
            ],
            out_specs=pl.BlockSpec((count, step), lambda j, n: (0, j)),
            scratch_shapes=[
                pltpu.VMEM((wide // step, width, step), BF),
                pltpu.SemaphoreType.DMA((wide // step,)),
            ],
        ),
        compiler_params=params(),
        cost_estimate=cost(2 * count * width * wide),
        name="project",
    )(scalars, rows, bias, scale, *arrays_of(sources))


PROJECT = 512


def lane_halves(kind):
    lane = lax.broadcasted_iota(jnp.int32, (1, 128), 1)
    return [(lane < HD).astype(F32).astype(kind), (lane >= HD).astype(F32).astype(kind)]


QUAD = 256


def attend_body(seq, len_ref, q_ref, k_ref, v_ref, *refs):
    o_ref, e_ref, r_ref = refs[-3:]
    length = len_ref[seq]
    halves = lane_halves(BF)
    lane = lax.broadcasted_iota(jnp.int32, (L, 128), 1)
    row = lax.broadcasted_iota(jnp.int32, (L, 128), 0)
    q_side = jnp.where(lane == 0, 1.0, 0.0).astype(BF)
    k_side = jnp.where((lane == 0) & (row >= length), -1e30, 0.0).astype(BF)
    for pair in range(QUAD // 128):
        part = slice(pair * 128, (pair + 1) * 128)
        q_pair = jnp.concatenate([q_ref[:, part], q_side], axis=1)
        k_pair = k_ref[:, part]
        v_pair = v_ref[:, part]
        powers = []
        for head in range(2):
            k_one = jnp.concatenate([k_pair * halves[head], k_side], axis=1)
            scores = dot(q_pair, k_one, 1, 1)
            peak = jnp.max(scores, axis=1, keepdims=True)
            power = jnp.exp(scores - peak).astype(BF)
            e_ref[2 * pair + head] = power
            powers.append(power)
        right = jnp.concatenate(
            [
                jnp.concatenate([v_pair * half, jnp.broadcast_to(half, (L, 128))], axis=1)
                for half in halves
            ],
            axis=0,
        )
        both = dot(jnp.concatenate(powers, axis=1), right, 1, 0)
        inverse = 1.0 / both[:, 128:]
        r_ref[:, part] = inverse
        o_ref[:, part] = (both[:, :128] * inverse).astype(BF)


def attend(scalars, qkv, width, seq, earlier):
    count = qkv.shape[0]
    quads = width // QUAD
    heads = QUAD // HD
    return pl.pallas_call(
        functools.partial(attend_body, seq),
        out_shape=(
            shape_of((count, width), BF),
            shape_of((count // L * width // HD, L, L), BF),
            shape_of((count, width), F32),
        ),
        grid_spec=pltpu.PrefetchScalarGridSpec(
            num_scalar_prefetch=1,
            grid=(quads,),
            in_specs=[
                pl.BlockSpec((L, QUAD), lambda j, n: (seq, j)),
                pl.BlockSpec((L, QUAD), lambda j, n: (seq, quads + j)),
                pl.BlockSpec((L, QUAD), lambda j, n: (seq, 2 * quads + j)),
                *([ANYWHERE] * len(earlier)),
            ],
            out_specs=[
                pl.BlockSpec((L, QUAD), lambda j, n: (seq, j)),
                pl.BlockSpec((heads, L, L), lambda j, n: (seq * quads + j, 0, 0)),
                pl.BlockSpec((L, QUAD), lambda j, n: (seq, j)),
            ],
        ),
        compiler_params=params(),
        input_output_aliases={4 + n: n for n in range(len(earlier))},
        cost_estimate=cost(16 * L * width * L),
        name="attend",
    )(scalars, qkv, qkv, qkv, *earlier)


ROWS = 256
FEED = 512


def hidden(rounded, buf, bi_ref, gl_ref, gp_ref):
    for part in range(gl_ref.shape[1] // FEED):
        cols = slice(part * FEED, (part + 1) * FEED)
        pre = dot(rounded, buf[:, cols], 1, 0) + bi_ref[:, cols]
        phi = 0.5 + 0.5 * lax.erf(pre * math.sqrt(0.5))
        power = (-0.5 / math.log(2.0)) * pre * pre - 0.5 * math.log2(2.0 * math.pi)
        gl_ref[:, cols] = (pre * phi).astype(BF)
        gp_ref[:, cols] = (phi + pre * jnp.exp2(power)).astype(BF)


def join_body(seqs, tags, len_ref, x_ref, o_ref, vec_ref, bi_ref, *refs):
    sources = tagged(refs, tags)
    u_ref, s_ref, gl_ref, gp_ref, out, buf, sems = refs[-7:]
    width = x_ref.shape[1]

    @pl.when(pl.program_id(0) == 0)
    def _():
        place = place_of(len_ref, seqs)
        issue(sources, out, sems.at[0], place, width // 32)
        issue(sources, buf, sems.at[1], place, width // 32, width)
        settle(out, sems.at[0])

    joined = dot(o_ref[...], out[...], 1, 0) + vec_ref[0:1, :] + x_ref[...].astype(F32)
    centered = joined - jnp.mean(joined, axis=1, keepdims=True)
    spread = lax.rsqrt(jnp.mean(centered * centered, axis=1, keepdims=True) + LN_EPS)
    normed = centered * spread * vec_ref[1:2, :] + vec_ref[2:3, :]
    u_ref[...] = normed
    s_ref[...] = jnp.broadcast_to(spread, s_ref.shape)
    rounded = normed.astype(BF)
    pl.when(pl.program_id(0) == 0)(functools.partial(settle, buf, sems.at[1]))
    hidden(rounded, buf, bi_ref, gl_ref, gp_ref)


def join(scalars, seqs, rows, context, sources, vectors, bias_in):
    count, width = rows.shape
    wide = bias_in.shape[1]
    block = lambda cols: pl.BlockSpec((ROWS, cols), lambda i, n: (i, 0))
    return pl.pallas_call(
        functools.partial(join_body, seqs, tags_of(sources)),
        out_shape=(
            shape_of((count, width), F32),
            shape_of((count, 128), F32),
            shape_of((count, wide), BF),
            shape_of((count, wide), BF),
        ),
        grid_spec=pltpu.PrefetchScalarGridSpec(
            num_scalar_prefetch=1,
            grid=(count // ROWS,),
            in_specs=[
                block(width),
                block(width),
                pl.BlockSpec((8, width), lambda i, n: (0, 0)),
                pl.BlockSpec((1, wide), lambda i, n: (0, 0)),
                *([ANYWHERE] * len(sources)),
            ],
            out_specs=[block(width), block(128), block(wide), block(wide)],
            scratch_shapes=[
                pltpu.VMEM((width, width), BF),
                pltpu.VMEM((width, wide), BF),
                pltpu.SemaphoreType.DMA((2,)),
            ],
        ),
        compiler_params=params(),
        cost_estimate=cost(2 * count * width * (width + wide)),
        name="join",
    )(scalars, rows, context, vectors, bias_in, *arrays_of(sources))


def turn_body(
    seqs, feed_tags, down_tags, len_ref, gl_ref, u_ref, s_ref, c_ref, vec_ref, gp_any, r_any, *refs
):
    feeds, downs = tagged(refs, feed_tags), tagged(refs[len(feed_tags) :], down_tags)
    y_ref, dh_ref, do_ref, gv_ref, gi_ref, out, buf, down, gp_ref, r_ref, sems, gp_sems = refs[-12:]
    index = pl.program_id(0)
    first = index == 0
    width = u_ref.shape[1]
    wide = gl_ref.shape[1]
    parts = 4
    step = wide // parts
    steps = gp_ref.shape[0]
    slopes = [
        pltpu.make_async_copy(gp_any.at[pl.ds(n * ROWS, ROWS)], gp_ref.at[n], gp_sems.at[n])
        for n in range(steps)
    ]
    inverse = pltpu.make_async_copy(r_any, r_ref, sems.at[3])

    @pl.when(first)
    def _():
        place = place_of(len_ref, seqs)
        issue(downs, down, sems.at[0], place, wide // 32)
        slopes[0].start()
        issue(feeds, buf, sems.at[1], place, width // 32, width)
        issue(feeds, out, sems.at[2], place, width // 32)
        for copy in slopes[1:]:
            copy.start()
        inverse.start()
        gv_ref[...] = jnp.zeros_like(gv_ref)
        gi_ref[...] = jnp.zeros_like(gi_ref)
        settle(down, sems.at[0])

    gain_one, beta_one, gain_two, beta_two, bias_down = (vec_ref[n : n + 1, :] for n in range(1, 6))
    normed = u_ref[...]
    total = normed + bias_down + dot(gl_ref[...], down[...], 1, 0)
    centered = total - jnp.mean(total, axis=1, keepdims=True)
    spread = lax.rsqrt(jnp.mean(centered * centered, axis=1, keepdims=True) + LN_EPS)
    hat = centered * spread
    y_ref[...] = (hat * gain_two + beta_two).astype(BF)
    per_seq = L // ROWS
    start = lax.rem(index, per_seq) * ROWS
    live = lax.broadcasted_iota(jnp.int32, (ROWS, 1), 0) + start < len_ref[index // per_seq]
    dy = jnp.where(live, c_ref[...].astype(F32), 0.0)
    gv_ref[4:5, :] += jnp.sum(dy, axis=0, keepdims=True)
    scaled = dy * gain_two
    d_two = spread * (
        scaled
        - jnp.mean(scaled, axis=1, keepdims=True)
        - hat * jnp.mean(scaled * hat, axis=1, keepdims=True)
    )
    d_branch = d_two.astype(BF)
    gv_ref[3:4, :] += jnp.sum(d_branch.astype(F32), axis=0, keepdims=True)
    pl.when(first)(functools.partial(settle, buf, sems.at[1]))
    for n in range(steps):
        pl.when(index == n)(slopes[n].wait)
    total = d_two
    for part in range(parts):
        rows = slice(part * step, (part + 1) * step)
        d_hidden = dot(d_branch, down[rows, :], 1, 1) * gp_ref[index, :, rows].astype(F32)
        d_hidden = d_hidden.astype(BF)
        gi_ref[:, rows] += jnp.sum(d_hidden.astype(F32), axis=0, keepdims=True)
        total = total + dot(d_hidden, buf[:, rows], 1, 1)
    gv_ref[2:3, :] += jnp.sum(total, axis=0, keepdims=True)
    scaled = total * gain_one
    hat = (normed - beta_one) * (1.0 / gain_one)
    d_one = s_ref[:, 0:1] * (
        scaled
        - jnp.mean(scaled, axis=1, keepdims=True)
        - hat * jnp.mean(scaled * hat, axis=1, keepdims=True)
    )
    dh_ref[...] = d_one
    d_att = d_one.astype(BF)
    gv_ref[1:2, :] += jnp.sum(d_att.astype(F32), axis=0, keepdims=True)

    @pl.when(first)
    def _():
        settle(out, sems.at[2])
        inverse.wait()

    d_context = dot(d_att, out[...], 1, 1).astype(BF).astype(F32)
    gv_ref[0:1, :] += jnp.sum(d_context, axis=0, keepdims=True)
    rows = pl.ds(pl.multiple_of(index * ROWS, ROWS), ROWS)
    do_ref[...] = (d_context * r_ref[rows, :]).astype(BF)


def turn(scalars, seqs, gl, gp, normed, spread, inverse, cotangent, feeds, downs, vectors):
    count, width = normed.shape
    wide = gl.shape[1]
    steps = count // ROWS
    block = lambda cols: pl.BlockSpec((ROWS, cols), lambda i, n: (i, 0))
    return pl.pallas_call(
        functools.partial(turn_body, seqs, tags_of(feeds), tags_of(downs)),
        out_shape=(
            shape_of((count, width), BF),
            shape_of((count, width), F32),
            shape_of((count, width), BF),
            shape_of((8, width), F32),
            shape_of((1, wide), F32),
        ),
        grid_spec=pltpu.PrefetchScalarGridSpec(
            num_scalar_prefetch=1,
            grid=(steps,),
            in_specs=[
                block(wide),
                block(width),
                block(128),
                block(width),
                pl.BlockSpec((8, width), lambda i, n: (0, 0)),
                *([ANYWHERE] * (2 + len(feeds) + len(downs))),
            ],
            out_specs=[
                block(width),
                block(width),
                block(width),
                pl.BlockSpec((8, width), lambda i, n: (0, 0)),
                pl.BlockSpec((1, wide), lambda i, n: (0, 0)),
            ],
            scratch_shapes=[
                pltpu.VMEM((width, width), BF),
                pltpu.VMEM((width, wide), BF),
                pltpu.VMEM((wide, width), BF),
                pltpu.VMEM((steps, ROWS, wide), BF),
                pltpu.VMEM((count, width), F32),
                pltpu.SemaphoreType.DMA((4,)),
                pltpu.SemaphoreType.DMA((steps,)),
            ],
        ),
        compiler_params=params(),
        cost_estimate=cost(2 * count * width * (width + 3 * wide)),
        name="turn",
    )(
        scalars, gl, normed, spread, cotangent, vectors, gp, inverse, *arrays_of(feeds), *arrays_of(downs)
    )


def back_body(
    seqs, tags, len_ref, q_ref, k_ref, v_ref, o_ref, do_ref, e_ref, dh_ref, *refs
):
    sources, (dx_ref, gq_ref, all_ref, w_ref, sem) = tagged(refs, tags), refs[len(tags) :]
    seq, quad = pl.program_id(0), pl.program_id(1)
    quads = pl.num_programs(1)
    width = dh_ref.shape[1]

    @pl.when((seq == 0) & (quad == 0))
    def _():
        issue(sources, w_ref, sem, place_of(len_ref, seqs), width // 32)
        gq_ref[...] = jnp.zeros_like(gq_ref)

    halves = lane_halves(BF)
    halves_wide = lane_halves(F32)
    lane = lax.broadcasted_iota(jnp.int32, (L, 128), 1)
    for pair in range(QUAD // 128):
        part = slice(pair * 128, (pair + 1) * 128)
        q_pair, k_pair, v_pair, do_pair = (r[:, part] for r in (q_ref, k_ref, v_ref, do_ref))
        products = do_pair.astype(F32) * o_ref[:, part].astype(F32)
        shifts = [jnp.sum(products * half, axis=1, keepdims=True) for half in halves_wide]
        rough = [shift.astype(BF).astype(F32) for shift in shifts]
        side = jnp.where(
            lane == 0,
            -rough[0],
            jnp.where(
                lane == 1,
                rough[0] - shifts[0],
                jnp.where(lane == 2, -rough[1], jnp.where(lane == 3, rough[1] - shifts[1], 0.0)),
            ),
        ).astype(BF)
        left = jnp.concatenate([do_pair, side], axis=1)
        q_turned = q_pair.T
        do_turned = do_pair.T
        d_scores, d_keys, d_values = [], [], []
        for head in range(2):
            rows = slice(head * HD, (head + 1) * HD)
            power = e_ref[2 * pair + head]
            marks = jnp.where(lane // 2 == head, 1.0, 0.0).astype(BF)
            right = jnp.concatenate([v_pair * halves[head], marks], axis=1)
            d_score = (power.astype(F32) * dot(left, right, 1, 1)).astype(BF)
            d_scores.append(d_score)
            d_keys.append(dot(q_turned[rows], d_score, 1, 0))
            d_values.append(dot(do_turned[rows], power, 1, 0))
        right = jnp.concatenate([k_pair * half for half in halves], axis=0)
        d_query = (dot(jnp.concatenate(d_scores, axis=1), right, 1, 0) * (HD**-0.5)).astype(BF)
        cols = pl.multiple_of(quad * QUAD + pair * 128, 128)
        gq_ref[:, pl.ds(cols, 128)] += jnp.sum(d_query.astype(F32), axis=0, keepdims=True)
        all_ref[:, pl.ds(cols, 128)] = d_query
        all_ref[:, pl.ds(width + cols, 128)] = jnp.concatenate(d_keys, axis=0).T.astype(BF)
        all_ref[:, pl.ds(2 * width + cols, 128)] = jnp.concatenate(d_values, axis=0).T.astype(BF)

    pl.when((seq == 0) & (quad == quads - 1))(functools.partial(settle, w_ref, sem))

    @pl.when(quad == quads - 1)
    def _():
        dx_ref[...] = (dh_ref[...] + dot(all_ref[...], w_ref[...], 1, 1)).astype(BF)


def back(scalars, seqs, qkv, context, d_context, powers, d_joined, sources):
    count, width = d_joined.shape
    quads = width // QUAD
    heads = QUAD // HD
    col = lambda n: pl.BlockSpec((L, QUAD), lambda i, j, s: (i, n * quads + j))
    return pl.pallas_call(
        functools.partial(back_body, seqs, tags_of(sources)),
        out_shape=(shape_of((count, width), BF), shape_of((1, width), F32)),
        grid_spec=pltpu.PrefetchScalarGridSpec(
            num_scalar_prefetch=1,
            grid=(seqs, quads),
            in_specs=[
                col(0),
                col(1),
                col(2),
                col(0),
                col(0),
                pl.BlockSpec((heads, L, L), lambda i, j, s: (i * quads + j, 0, 0)),
                pl.BlockSpec((L, width), lambda i, j, s: (i, 0)),
                *([ANYWHERE] * len(sources)),
            ],
            out_specs=[
                pl.BlockSpec((L, width), lambda i, j, s: (i, 0)),
                pl.BlockSpec((1, width), lambda i, j, s: (0, 0)),
            ],
            scratch_shapes=[
                pltpu.VMEM((L, 3 * width), BF),
                pltpu.VMEM((width, 3 * width), BF),
                pltpu.SemaphoreType.DMA,
            ],
        ),
        compiler_params=params(),
        cost_estimate=cost(2 * count * width * 3 * width + 20 * count * width * L),
        name="back",
    )(scalars, qkv, qkv, qkv, context, d_context, powers, d_joined, *arrays_of(sources))


BOTH = ("dp", "fsdp")


def hop(block, axis, flip):
    size = lax.axis_size(axis)
    return lax.ppermute(block, axis, [(i, i ^ flip) for i in range(size)])


def over_x(block):
    return hop(block, "dp", 1)


def over_y(block):
    return hop(block, "dp", 2)


def over_core(block):
    return hop(block, "fsdp", 1)


def over_z(block, k):
    return hop(block, "fsdp", 2 * k)


def after(value, *earlier):
    return lax.optimization_barrier((value, *earlier))[0]


MOVES = {
    "x": over_x,
    "y": over_y,
    "c": over_core,
    "1": functools.partial(over_z, k=1),
    "2": functools.partial(over_z, k=2),
    "3": functools.partial(over_z, k=3),
}


def stage(lanes, blocks, *earlier):
    blocks = after(tuple(blocks), *earlier)
    return lax.optimization_barrier(tuple(MOVES[lane](block) for lane, block in zip(lanes, blocks)))


def both(mine, others):
    return [(array, (*tag, 0)) for array, tag in mine] + [
        (array, (*tag, 1)) for array, (_, tag) in zip(others, mine)
    ]


def whole(array):
    return [(array, None)]


def on_device(
    tokens, lengths, w_qkv, w_out, w_in, w_down, gain_one, gain_two,
    bias_q, bias_v, bias_out, beta_one, bias_in, bias_down, beta_two, cotangent,
):
    width = w_out.shape[1]
    seqs = lengths.shape[0]
    chip = lax.axis_index("fsdp")
    scalars = jnp.concatenate(
        [lengths, jnp.stack([lax.axis_index("dp"), chip // 2, chip % 2]).astype(jnp.int32)]
    )
    score_scale = HD**-0.5
    ones = jnp.ones((width,), F32)
    zeros = jnp.zeros((width,), F32)
    bias = jnp.concatenate([bias_q, zeros, bias_v])[None]
    scale = jnp.concatenate([ones * score_scale, ones, ones])[None]
    vectors = jnp.stack([bias_out, gain_one, beta_one, gain_two, beta_two, bias_down, zeros, zeros])
    special = (lax.axis_size("dp"), lax.axis_size("fsdp")) == (4, 8)
    if special:
        own, w_feed = pack(w_qkv, w_out, w_in, w_down)
        at_feed = w_qkv.shape[1]
        at_down = at_feed + w_feed.shape[1]
        z_one, z_two, z_three, near_x, near_y = stage("123xy", (w_qkv, w_qkv, w_qkv, own, own))
        tall, cols_feed = w_qkv.shape[0], w_feed.shape[1]
        (far,) = glue(
            (z_one, z_two, z_three), (at_feed, *((n, 0, tall, 0) for n in range(3)))
        )
        x_far, y_far, feed_two, own_core, near_x_core = stage(
            "xy2cc", (far, far, w_feed, own, near_x)
        )
        left, right = glue(
            (near_x, x_far, y_far),
            (at_feed, (0, 0, tall, 0), (1, 0, tall, 0)),
            (at_feed, (2, tall, 2 * tall, 0)),
        )
        crossed, crossed_more, feed_one, near_y_core, far_core = stage(
            "yx1cc", (left, right, w_feed, near_y, far), feed_two, own_core, near_x_core
        )
        x_far_core, y_far_core, crossed_core, crossed_more_core = stage(
            "cccc", (x_far, y_far, crossed, crossed_more), feed_one, near_y_core, far_core
        )
        near = (own, near_x, near_y)
        near_core = (own_core, near_x_core, near_y_core)
        rest = (1, 2, 3)
        qkv_parts = both(
            [
                *((array, (chip, (0,), 0)) for chip, array in enumerate(near)),
                (far, (0, rest, 0)),
                (x_far, (1, rest, 0)),
                (y_far, (2, rest, 0)),
                (crossed, (3, (0, 1), 0)),
                (crossed_more, (3, (2, 3), 0)),
            ],
            [*near_core, far_core, x_far_core, y_far_core, crossed_core, crossed_more_core],
        )
        pair, near_x_down = glue(
            (feed_one, feed_two, near_x),
            (cols_feed, (0, 0, tall, 0), (1, 0, tall, 0)),
            (w_down.shape[0] // tall * width, (2, 0, tall, at_down)),
        )
        x_pair, y_pair, feed_three, pair_core = stage(
            "xy3c", (pair, pair, w_feed, pair), y_far_core, crossed_core, crossed_more_core
        )
        first = after(tokens, pair)
    else:
        first = tokens
        w_feed = jnp.concatenate([w_out, w_in], axis=1)
        qkv_parts = whole(lax.all_gather(w_qkv, BOTH, axis=0, tiled=True))
        feed_parts = whole(lax.all_gather(w_feed, BOTH, axis=0, tiled=True))
        down_parts = whole(lax.all_gather(w_down, BOTH, axis=0, tiled=True))
    qkv = project(scalars, seqs, first, qkv_parts, bias, scale)
    if special:
        x_last, y_last, cross_down, down_one, down_two = stage(
            "xyy12", (feed_three, feed_three, near_x_down, w_down, w_down), qkv, pair_core
        )
    attended = []
    for seq in range(seqs):
        if special and seq == 1:
            x_last, y_last, *attended = after((x_last, y_last, *attended), cross_down, down_one)
            left, right = glue(
                (near_x, x_pair, y_pair, y_last),
                (cols_feed, (0, 0, tall, at_feed), (1, 0, tall, 0)),
                (cols_feed, (2, tall, tall, 0), (3, 0, tall, 0)),
            )
            crossed, crossed_more, down_three, x_pair_core, y_pair_core = stage(
                "yx3cc", (left, right, w_down, x_pair, y_pair), x_last, *attended
            )
        attended = attend(scalars, qkv, width, seq, attended)
    context, powers, inverse = attended
    if special:
        cores = stage(
            "ccccc", (feed_three, x_last, y_last, crossed, crossed_more), context, down_three
        )
        feed_parts = both(
            [
                *((array, (chip, (0,), at_feed)) for chip, array in enumerate(near)),
                (pair, (0, (1, 2), 0)),
                (x_pair, (1, (1, 2), 0)),
                (y_pair, (2, (1, 2), 0)),
                (feed_three, (0, (3,), 0)),
                (x_last, (1, (3,), 0)),
                (y_last, (2, (3,), 0)),
                (crossed, (3, (0, 1), 0)),
                (crossed_more, (3, (2, 3), 0)),
            ],
            [*near_core, pair_core, x_pair_core, y_pair_core, *cores],
        )
        (far,) = glue(
            (down_one, down_two, down_three),
            (width, *((n, 0, w_down.shape[0], 0) for n in range(3))),
        )
        x_far, y_far, *diagonal = stage(
            "xy123", (far, far, cross_down, cross_down, cross_down), *cores
        )
    normed, spread, gl, gp = join(
        scalars, seqs, tokens, context, feed_parts, vectors, bias_in[None]
    )
    if special:
        x_far, cross_down, gl = after((x_far, cross_down, gl), y_far, *diagonal)
    if special:
        mine = [
            (after(far, x_far), (0, rest, 0)),
            (x_far, (1, rest, 0)),
            (y_far, (2, rest, 0)),
            (cross_down, (3, (0,), 0)),
            *((block, (3, (k,), 0)) for block, k in zip(diagonal, rest)),
        ]
        down_parts = both(
            [*((array, (chip, (0,), at_down)) for chip, array in enumerate(near)), *mine],
            [*near_core, *(over_core(block) for block, _ in mine)],
        )
    output, d_joined, d_context, sums, sum_in = turn(
        scalars, seqs, gl, gp, normed, spread, inverse, cotangent, feed_parts, down_parts, vectors
    )
    input_grad, sum_q = back(scalars, seqs, qkv, context, d_context, powers, d_joined, qkv_parts)
    devices = lax.axis_size("dp") * lax.axis_size("fsdp")
    parts = (sum_q[0], sums[0], sums[1], sums[2], sum_in[0], sums[3], sums[4])
    rows = jnp.concatenate([part.reshape(devices, -1) for part in parts], axis=1)
    mine = jnp.sum(lax.all_to_all(rows, BOTH, 0, 0, tiled=True), axis=0)
    small = width // devices
    sizes = (small, small, small, small, sum_in.shape[1] // devices, small, small)
    shares, at = [], 0
    for size in sizes:
        shares.append(mine[at : at + size])
        at += size
    return (output, input_grad, *shares)


def solution(mesh):
    split, rows, copied = P(BOTH), P(BOTH, None), P()
    in_specs = (rows, split, rows, rows, rows, rows, *([copied] * 9), rows)
    out_specs = (rows, rows, *([split] * 7))
    return jax.shard_map(
        on_device, mesh=mesh, in_specs=in_specs, out_specs=out_specs, check_vma=False
    )
```

```python
import functools
import math

import jax
import jax.numpy as jnp
from jax import lax
from jax.experimental import pallas as pl
from jax.experimental.pallas import tpu as pltpu
from jax.sharding import PartitionSpec as P

HD = 64
L = 512
LN_EPS = 1e-12
MIB = 2**20
BF = jnp.bfloat16
F32 = jnp.float32


def params(limit=60, semantics=None):
    return pltpu.CompilerParams(vmem_limit_bytes=limit * MIB, dimension_semantics=semantics)


def dot(left, right, on_left, on_right):
    return lax.dot_general(
        left, right, (((on_left,), (on_right,)), ((), ())), preferred_element_type=F32
    )


def shape_of(dims, kind):
    return jax.ShapeDtypeStruct(dims, kind)


def cost(flops):
    return pl.CostEstimate(flops=flops, bytes_accessed=0, transcendentals=0)


def issue(sources, buf, sem, place, height, window=0):
    plane_at, z_at, core_at = place
    cols = buf.shape[1]
    for source, tag in sources:
        if tag is None:
            pltpu.make_async_copy(source.at[:, pl.ds(window, cols)], buf, sem).start()
            continue
        chip, zs, first, turned = tag
        tall = source.shape[0] // len(zs)
        for step, z in enumerate(zs):
            row = ((plane_at ^ chip) * 8 + (z_at ^ z) * 2 + (core_at ^ turned)) * height
            for block in range(height // tall):
                pltpu.make_async_copy(
                    source.at[pl.ds(step * tall, tall), pl.ds(first + window + block * cols, cols)],
                    buf.at[pl.ds(pl.multiple_of(row + block * tall, tall), tall)],
                    sem,
                ).start()


def settle(buf, sem):
    pltpu.make_async_copy(buf, buf, sem).wait()


def tagged(refs, tags):
    return list(zip(refs, tags))


def tags_of(sources):
    return [tag for _, tag in sources]


def arrays_of(sources):
    return [array for array, _ in sources]


def place_of(scalars, seqs):
    return scalars[seqs], scalars[seqs + 1], scalars[seqs + 2]


ANYWHERE = pl.BlockSpec(memory_space=pl.ANY)

def pack_body(qkv_ref, out_ref, in_ref, down_ref, own_ref, feed_ref, sem):
    height = qkv_ref.shape[0]
    copies, at = [], 0
    for ref in (qkv_ref, out_ref, in_ref):
        copies.append(pltpu.make_async_copy(ref, own_ref.at[:, pl.ds(at, ref.shape[1])], sem))
        at += ref.shape[1]
    for first in range(0, down_ref.shape[0], height):
        window = down_ref.at[pl.ds(first, height)]
        copies.append(pltpu.make_async_copy(window, own_ref.at[:, pl.ds(at, down_ref.shape[1])], sem))
        at += down_ref.shape[1]
    for copy in copies:
        copy.start()
    settle(own_ref, sem)
    first = qkv_ref.shape[1]
    feed_ref[...] = own_ref[:, first : first + feed_ref.shape[1]]


def pack(w_qkv, w_out, w_in, w_down):
    height = w_qkv.shape[0]
    feed_wide = w_out.shape[1] + w_in.shape[1]
    wide = w_qkv.shape[1] + feed_wide + w_down.shape[0] // height * w_down.shape[1]
    return pl.pallas_call(
        pack_body,
        out_shape=(shape_of((height, wide), BF), shape_of((height, feed_wide), BF)),
        in_specs=[ANYWHERE] * 4,
        scratch_shapes=[pltpu.SemaphoreType.DMA],
        compiler_params=params(),
        name="pack",
    )(w_qkv, w_out, w_in, w_down)


def glue_body(plans, count, *refs):
    sources, targets = refs[:count], refs[count:]
    for plan, target in zip(plans, targets):
        at = 0
        for number, top, rows, left in plan:
            target[at : at + rows, :] = sources[number][top : top + rows, left : left + target.shape[1]]
            at += rows


def glue(arrays, *plans):
    return pl.pallas_call(
        functools.partial(glue_body, [plan[1:] for plan in plans], len(arrays)),
        out_shape=[shape_of((sum(w[2] for w in plan[1:]), plan[0]), BF) for plan in plans],
        compiler_params=params(20),
        name="glue",
    )(*arrays)


def project_body(seqs, tags, len_ref, x_ref, bias_ref, scale_ref, *refs):
    sources, (out_ref, buf, sems) = tagged(refs, tags), refs[len(tags) :]
    here = pl.program_id(0)
    step = out_ref.shape[1]

    @pl.when(here == 0)
    def _():
        place = place_of(len_ref, seqs)
        for part in range(buf.shape[0]):
            issue(sources, buf.at[part], sems.at[part], place, buf.shape[1] // 32, part * step)

    settle(buf.at[here], sems.at[here])
    total = dot(x_ref[...], buf[here], 1, 0) + bias_ref[...]
    out_ref[...] = (total * scale_ref[...]).astype(BF)


def project(scalars, seqs, rows, sources, bias, scale):
    count, width = rows.shape
    wide = bias.shape[1]
    step = PROJECT
    return pl.pallas_call(
        functools.partial(project_body, seqs, tags_of(sources)),
        out_shape=shape_of((count, wide), BF),
        grid_spec=pltpu.PrefetchScalarGridSpec(
            num_scalar_prefetch=1,
            grid=(wide // step,),
            in_specs=[
                pl.BlockSpec((count, width), lambda j, n: (0, 0)),
                pl.BlockSpec((1, step), lambda j, n: (0, j)),
                pl.BlockSpec((1, step), lambda j, n: (0, j)),
                *([ANYWHERE] * len(sources)),
            ],
            out_specs=pl.BlockSpec((count, step), lambda j, n: (0, j)),
            scratch_shapes=[
                pltpu.VMEM((wide // step, width, step), BF),
                pltpu.SemaphoreType.DMA((wide // step,)),
            ],
        ),
        compiler_params=params(),
        cost_estimate=cost(2 * count * width * wide),
        name="project",
    )(scalars, rows, bias, scale, *arrays_of(sources))


PROJECT = 512


def lane_halves(kind):
    lane = lax.broadcasted_iota(jnp.int32, (1, 128), 1)
    return [(lane < HD).astype(F32).astype(kind), (lane >= HD).astype(F32).astype(kind)]


QUAD = 256


def attend_body(seq, len_ref, q_ref, k_ref, v_ref, *refs):
    o_ref, e_ref, r_ref = refs[-3:]
    length = len_ref[seq]
    halves = lane_halves(BF)
    lane = lax.broadcasted_iota(jnp.int32, (L, 128), 1)
    row = lax.broadcasted_iota(jnp.int32, (L, 128), 0)
    q_side = jnp.where(lane == 0, 1.0, 0.0).astype(BF)
    k_side = jnp.where((lane == 0) & (row >= length), -1e30, 0.0).astype(BF)
    for pair in range(QUAD // 128):
        part = slice(pair * 128, (pair + 1) * 128)
        q_pair = jnp.concatenate([q_ref[:, part], q_side], axis=1)
        k_pair = k_ref[:, part]
        v_pair = v_ref[:, part]
        powers = []
        for head in range(2):
            k_one = jnp.concatenate([k_pair * halves[head], k_side], axis=1)
            scores = dot(q_pair, k_one, 1, 1)
            peak = jnp.max(scores, axis=1, keepdims=True)
            power = jnp.exp(scores - peak).astype(BF)
            e_ref[2 * pair + head] = power
            powers.append(power)
        right = jnp.concatenate(
            [
                jnp.concatenate([v_pair * half, jnp.broadcast_to(half, (L, 128))], axis=1)
                for half in halves
            ],
            axis=0,
        )
        both = dot(jnp.concatenate(powers, axis=1), right, 1, 0)
        inverse = 1.0 / both[:, 128:]
        r_ref[:, part] = inverse
        o_ref[:, part] = (both[:, :128] * inverse).astype(BF)


def attend(scalars, qkv, width, seq, earlier):
    count = qkv.shape[0]
    quads = width // QUAD
    heads = QUAD // HD
    return pl.pallas_call(
        functools.partial(attend_body, seq),
        out_shape=(
            shape_of((count, width), BF),
            shape_of((count // L * width // HD, L, L), BF),
            shape_of((count, width), F32),
        ),
        grid_spec=pltpu.PrefetchScalarGridSpec(
            num_scalar_prefetch=1,
            grid=(quads,),
            in_specs=[
                pl.BlockSpec((L, QUAD), lambda j, n: (seq, j)),
                pl.BlockSpec((L, QUAD), lambda j, n: (seq, quads + j)),
                pl.BlockSpec((L, QUAD), lambda j, n: (seq, 2 * quads + j)),
                *([ANYWHERE] * len(earlier)),
            ],
            out_specs=[
                pl.BlockSpec((L, QUAD), lambda j, n: (seq, j)),
                pl.BlockSpec((heads, L, L), lambda j, n: (seq * quads + j, 0, 0)),
                pl.BlockSpec((L, QUAD), lambda j, n: (seq, j)),
            ],
        ),
        compiler_params=params(),
        input_output_aliases={4 + n: n for n in range(len(earlier))},
        cost_estimate=cost(16 * L * width * L),
        name="attend",
    )(scalars, qkv, qkv, qkv, *earlier)


ROWS = 256
FEED = 512


def hidden(rounded, buf, bi_ref, gl_ref, gp_ref):
    for part in range(gl_ref.shape[1] // FEED):
        cols = slice(part * FEED, (part + 1) * FEED)
        pre = dot(rounded, buf[:, cols], 1, 0) + bi_ref[:, cols]
        phi = 0.5 + 0.5 * lax.erf(pre * math.sqrt(0.5))
        power = (-0.5 / math.log(2.0)) * pre * pre - 0.5 * math.log2(2.0 * math.pi)
        gl_ref[:, cols] = (pre * phi).astype(BF)
        gp_ref[:, cols] = (phi + pre * jnp.exp2(power)).astype(BF)


def join_body(seqs, tags, len_ref, x_ref, o_ref, vec_ref, bi_ref, *refs):
    sources = tagged(refs, tags)
    u_ref, s_ref, gl_ref, gp_ref, out, buf, sems = refs[-7:]
    width = x_ref.shape[1]

    @pl.when(pl.program_id(0) == 0)
    def _():
        place = place_of(len_ref, seqs)
        issue(sources, out, sems.at[0], place, width // 32)
        issue(sources, buf, sems.at[1], place, width // 32, width)
        settle(out, sems.at[0])

    joined = dot(o_ref[...], out[...], 1, 0) + vec_ref[0:1, :] + x_ref[...].astype(F32)
    centered = joined - jnp.mean(joined, axis=1, keepdims=True)
    spread = lax.rsqrt(jnp.mean(centered * centered, axis=1, keepdims=True) + LN_EPS)
    normed = centered * spread * vec_ref[1:2, :] + vec_ref[2:3, :]
    u_ref[...] = normed
    s_ref[...] = jnp.broadcast_to(spread, s_ref.shape)
    rounded = normed.astype(BF)
    pl.when(pl.program_id(0) == 0)(functools.partial(settle, buf, sems.at[1]))
    hidden(rounded, buf, bi_ref, gl_ref, gp_ref)


def join(scalars, seqs, rows, context, sources, vectors, bias_in):
    count, width = rows.shape
    wide = bias_in.shape[1]
    block = lambda cols: pl.BlockSpec((ROWS, cols), lambda i, n: (i, 0))
    return pl.pallas_call(
        functools.partial(join_body, seqs, tags_of(sources)),
        out_shape=(
            shape_of((count, width), F32),
            shape_of((count, 128), F32),
            shape_of((count, wide), BF),
            shape_of((count, wide), BF),
        ),
        grid_spec=pltpu.PrefetchScalarGridSpec(
            num_scalar_prefetch=1,
            grid=(count // ROWS,),
            in_specs=[
                block(width),
                block(width),
                pl.BlockSpec((8, width), lambda i, n: (0, 0)),
                pl.BlockSpec((1, wide), lambda i, n: (0, 0)),
                *([ANYWHERE] * len(sources)),
            ],
            out_specs=[block(width), block(128), block(wide), block(wide)],
            scratch_shapes=[
                pltpu.VMEM((width, width), BF),
                pltpu.VMEM((width, wide), BF),
                pltpu.SemaphoreType.DMA((2,)),
            ],
        ),
        compiler_params=params(),
        cost_estimate=cost(2 * count * width * (width + wide)),
        name="join",
    )(scalars, rows, context, vectors, bias_in, *arrays_of(sources))


TURN = 256


def turn_body(
    seqs, feed_tags, down_tags, len_ref, gl_ref, u_ref, s_ref, c_ref, vec_ref, gp_any, *refs
):
    feeds, downs = tagged(refs, feed_tags), tagged(refs[len(feed_tags) :], down_tags)
    y_ref, dh_ref, do_ref, gv_ref, gi_ref, out, buf, down, gp_ref, sems, gp_sems = refs[-11:]
    index = pl.program_id(0)
    first = index == 0
    width = u_ref.shape[1]
    wide = gl_ref.shape[1]
    parts = 4
    step = wide // parts
    steps = gp_ref.shape[0]
    slopes = [
        pltpu.make_async_copy(gp_any.at[pl.ds(n * TURN, TURN)], gp_ref.at[n], gp_sems.at[n])
        for n in range(steps)
    ]

    @pl.when(first)
    def _():
        place = place_of(len_ref, seqs)
        issue(downs, down, sems.at[0], place, wide // 32)
        slopes[0].start()
        issue(feeds, buf, sems.at[1], place, width // 32, width)
        issue(feeds, out, sems.at[2], place, width // 32)
        for copy in slopes[1:]:
            copy.start()
        gv_ref[...] = jnp.zeros_like(gv_ref)
        gi_ref[...] = jnp.zeros_like(gi_ref)
        settle(down, sems.at[0])

    gain_one, beta_one, gain_two, beta_two, bias_down = (vec_ref[n : n + 1, :] for n in range(1, 6))
    normed = u_ref[...]
    total = normed + bias_down + dot(gl_ref[...], down[...], 1, 0)
    centered = total - jnp.mean(total, axis=1, keepdims=True)
    spread = lax.rsqrt(jnp.mean(centered * centered, axis=1, keepdims=True) + LN_EPS)
    hat = centered * spread
    y_ref[...] = (hat * gain_two + beta_two).astype(BF)
    per_seq = L // TURN
    start = lax.rem(index, per_seq) * TURN
    live = lax.broadcasted_iota(jnp.int32, (TURN, 1), 0) + start < len_ref[index // per_seq]
    dy = jnp.where(live, c_ref[...].astype(F32), 0.0)
    gv_ref[4:5, :] += jnp.sum(dy, axis=0, keepdims=True)
    scaled = dy * gain_two
    d_two = spread * (
        scaled
        - jnp.mean(scaled, axis=1, keepdims=True)
        - hat * jnp.mean(scaled * hat, axis=1, keepdims=True)
    )
    d_branch = d_two.astype(BF)
    gv_ref[3:4, :] += jnp.sum(d_branch.astype(F32), axis=0, keepdims=True)
    pl.when(first)(functools.partial(settle, buf, sems.at[1]))
    for n in range(steps):
        pl.when(index == n)(slopes[n].wait)
    total = d_two
    for part in range(parts):
        rows = slice(part * step, (part + 1) * step)
        d_hidden = dot(d_branch, down[rows, :], 1, 1) * gp_ref[index, :, rows].astype(F32)
        d_hidden = d_hidden.astype(BF)
        gi_ref[:, rows] += jnp.sum(d_hidden.astype(F32), axis=0, keepdims=True)
        total = total + dot(d_hidden, buf[:, rows], 1, 1)
    gv_ref[2:3, :] += jnp.sum(total, axis=0, keepdims=True)
    scaled = total * gain_one
    hat = (normed - beta_one) * (1.0 / gain_one)
    d_one = s_ref[:, 0:1] * (
        scaled
        - jnp.mean(scaled, axis=1, keepdims=True)
        - hat * jnp.mean(scaled * hat, axis=1, keepdims=True)
    )
    dh_ref[...] = d_one
    d_att = d_one.astype(BF)
    gv_ref[1:2, :] += jnp.sum(d_att.astype(F32), axis=0, keepdims=True)

    pl.when(first)(functools.partial(settle, out, sems.at[2]))
    d_context = dot(d_att, out[...], 1, 1).astype(BF)
    do_ref[...] = d_context
    gv_ref[0:1, :] += jnp.sum(d_context.astype(F32), axis=0, keepdims=True)


def turn(scalars, seqs, gl, gp, normed, spread, cotangent, feeds, downs, vectors):
    count, width = normed.shape
    wide = gl.shape[1]
    steps = count // TURN
    block = lambda cols: pl.BlockSpec((TURN, cols), lambda i, n: (i, 0))
    return pl.pallas_call(
        functools.partial(turn_body, seqs, tags_of(feeds), tags_of(downs)),
        out_shape=(
            shape_of((count, width), BF),
            shape_of((count, width), F32),
            shape_of((count, width), BF),
            shape_of((8, width), F32),
            shape_of((1, wide), F32),
        ),
        grid_spec=pltpu.PrefetchScalarGridSpec(
            num_scalar_prefetch=1,
            grid=(steps,),
            in_specs=[
                block(wide),
                block(width),
                block(128),
                block(width),
                pl.BlockSpec((8, width), lambda i, n: (0, 0)),
                *([ANYWHERE] * (1 + len(feeds) + len(downs))),
            ],
            out_specs=[
                block(width),
                block(width),
                block(width),
                pl.BlockSpec((8, width), lambda i, n: (0, 0)),
                pl.BlockSpec((1, wide), lambda i, n: (0, 0)),
            ],
            scratch_shapes=[
                pltpu.VMEM((width, width), BF),
                pltpu.VMEM((width, wide), BF),
                pltpu.VMEM((wide, width), BF),
                pltpu.VMEM((steps, TURN, wide), BF),
                pltpu.SemaphoreType.DMA((3,)),
                pltpu.SemaphoreType.DMA((steps,)),
            ],
        ),
        compiler_params=params(),
        cost_estimate=cost(2 * count * width * (width + 3 * wide)),
        name="turn",
    )(
        scalars, gl, normed, spread, cotangent, vectors, gp, *arrays_of(feeds), *arrays_of(downs)
    )


WIDE = 512


def back_body(
    seqs, tags, len_ref, q_ref, k_ref, v_ref, o_ref, do_ref, r_ref, e_ref, dh_ref, *refs
):
    sources, (dx_ref, gq_ref, all_ref, w_ref, sem) = tagged(refs, tags), refs[len(tags) :]
    seq, quad = pl.program_id(0), pl.program_id(1)
    quads = pl.num_programs(1)
    width = dh_ref.shape[1]

    @pl.when((seq == 0) & (quad == 0))
    def _():
        issue(sources, w_ref, sem, place_of(len_ref, seqs), width // 32)
        gq_ref[...] = jnp.zeros_like(gq_ref)

    halves = lane_halves(BF)
    halves_wide = lane_halves(F32)
    lane = lax.broadcasted_iota(jnp.int32, (L, 128), 1)
    for pair in range(WIDE // 128):
        part = slice(pair * 128, (pair + 1) * 128)
        q_pair, k_pair, v_pair = (r[:, part] for r in (q_ref, k_ref, v_ref))
        do_pair = (do_ref[:, part].astype(F32) * r_ref[:, part]).astype(BF)
        products = do_pair.astype(F32) * o_ref[:, part].astype(F32)
        shifts = [jnp.sum(products * half, axis=1, keepdims=True) for half in halves_wide]
        rough = [shift.astype(BF).astype(F32) for shift in shifts]
        side = jnp.where(
            lane == 0,
            -rough[0],
            jnp.where(
                lane == 1,
                rough[0] - shifts[0],
                jnp.where(lane == 2, -rough[1], jnp.where(lane == 3, rough[1] - shifts[1], 0.0)),
            ),
        ).astype(BF)
        left = jnp.concatenate([do_pair, side], axis=1)
        q_turned = q_pair.T
        do_turned = do_pair.T
        d_scores, d_keys, d_values = [], [], []
        for head in range(2):
            rows = slice(head * HD, (head + 1) * HD)
            power = e_ref[2 * pair + head]
            marks = jnp.where(lane // 2 == head, 1.0, 0.0).astype(BF)
            right = jnp.concatenate([v_pair * halves[head], marks], axis=1)
            d_score = (power.astype(F32) * dot(left, right, 1, 1)).astype(BF)
            d_scores.append(d_score)
            d_keys.append(dot(q_turned[rows], d_score, 1, 0))
            d_values.append(dot(do_turned[rows], power, 1, 0))
        right = jnp.concatenate([k_pair * half for half in halves], axis=0)
        d_query = (dot(jnp.concatenate(d_scores, axis=1), right, 1, 0) * (HD**-0.5)).astype(BF)
        cols = pl.multiple_of(quad * WIDE + pair * 128, 128)
        gq_ref[:, pl.ds(cols, 128)] += jnp.sum(d_query.astype(F32), axis=0, keepdims=True)
        all_ref[:, pl.ds(cols, 128)] = d_query
        all_ref[:, pl.ds(width + cols, 128)] = jnp.concatenate(d_keys, axis=0).T.astype(BF)
        all_ref[:, pl.ds(2 * width + cols, 128)] = jnp.concatenate(d_values, axis=0).T.astype(BF)

    pl.when((seq == 0) & (quad == quads - 1))(functools.partial(settle, w_ref, sem))

    @pl.when(quad == quads - 1)
    def _():
        dx_ref[...] = (dh_ref[...] + dot(all_ref[...], w_ref[...], 1, 1)).astype(BF)


def back(scalars, seqs, qkv, context, d_context, inverse, powers, d_joined, sources):
    count, width = d_joined.shape
    quads = width // WIDE
    heads = WIDE // HD
    col = lambda n: pl.BlockSpec((L, WIDE), lambda i, j, s: (i, n * quads + j))
    return pl.pallas_call(
        functools.partial(back_body, seqs, tags_of(sources)),
        out_shape=(shape_of((count, width), BF), shape_of((1, width), F32)),
        grid_spec=pltpu.PrefetchScalarGridSpec(
            num_scalar_prefetch=1,
            grid=(seqs, quads),
            in_specs=[
                col(0),
                col(1),
                col(2),
                col(0),
                col(0),
                col(0),
                pl.BlockSpec((heads, L, L), lambda i, j, s: (i * quads + j, 0, 0)),
                pl.BlockSpec((L, width), lambda i, j, s: (i, 0)),
                *([ANYWHERE] * len(sources)),
            ],
            out_specs=[
                pl.BlockSpec((L, width), lambda i, j, s: (i, 0)),
                pl.BlockSpec((1, width), lambda i, j, s: (0, 0)),
            ],
            scratch_shapes=[
                pltpu.VMEM((L, 3 * width), BF),
                pltpu.VMEM((width, 3 * width), BF),
                pltpu.SemaphoreType.DMA,
            ],
        ),
        compiler_params=params(),
        cost_estimate=cost(2 * count * width * 3 * width + 20 * count * width * L),
        name="back",
    )(scalars, qkv, qkv, qkv, context, d_context, inverse, powers, d_joined, *arrays_of(sources))


BOTH = ("dp", "fsdp")


def hop(block, axis, flip):
    size = lax.axis_size(axis)
    return lax.ppermute(block, axis, [(i, i ^ flip) for i in range(size)])


def after_all(*values):
    return lax.optimization_barrier(values)


def over_x(block):
    return hop(block, "dp", 1)


def over_y(block):
    return hop(block, "dp", 2)


def over_core(block):
    return hop(block, "fsdp", 1)


def over_z(block, k):
    return hop(block, "fsdp", 2 * k)


def after(value, *earlier):
    return lax.optimization_barrier((value, *earlier))[0]


MOVES = {
    "x": over_x,
    "y": over_y,
    "c": over_core,
    "1": functools.partial(over_z, k=1),
    "2": functools.partial(over_z, k=2),
    "3": functools.partial(over_z, k=3),
}


def stage(lanes, blocks, *earlier):
    blocks = after(tuple(blocks), *earlier)
    return lax.optimization_barrier(tuple(MOVES[lane](block) for lane, block in zip(lanes, blocks)))


def both(mine, others):
    return [(array, (*tag, 0)) for array, tag in mine] + [
        (array, (*tag, 1)) for array, (_, tag) in zip(others, mine)
    ]


def whole(array):
    return [(array, None)]


def on_device(
    tokens, lengths, w_qkv, w_out, w_in, w_down, gain_one, gain_two,
    bias_q, bias_v, bias_out, beta_one, bias_in, bias_down, beta_two, cotangent,
):
    width = w_out.shape[1]
    seqs = lengths.shape[0]
    chip = lax.axis_index("fsdp")
    scalars = jnp.concatenate(
        [lengths, jnp.stack([lax.axis_index("dp"), chip // 2, chip % 2]).astype(jnp.int32)]
    )
    score_scale = HD**-0.5
    ones = jnp.ones((width,), F32)
    zeros = jnp.zeros((width,), F32)
    bias = jnp.concatenate([bias_q, zeros, bias_v])[None]
    scale = jnp.concatenate([ones * score_scale, ones, ones])[None]
    vectors = jnp.stack([bias_out, gain_one, beta_one, gain_two, beta_two, bias_down, zeros, zeros])
    special = (lax.axis_size("dp"), lax.axis_size("fsdp")) == (4, 8)
    if special:
        own, w_feed = pack(w_qkv, w_out, w_in, w_down)
        at_feed = w_qkv.shape[1]
        at_down = at_feed + w_feed.shape[1]
        z_one, z_two, z_three, near_x, near_y = stage("123xy", (w_qkv, w_qkv, w_qkv, own, own))
        tall, cols_feed = w_qkv.shape[0], w_feed.shape[1]
        z_one, scalars, bias, scale, vectors = after_all(z_one, scalars, bias, scale, vectors)
        (far,) = glue(
            (z_one, z_two, z_three), (at_feed, *((n, 0, tall, 0) for n in range(3)))
        )
        x_far, y_far, feed_two, own_core, near_x_core = stage(
            "xy2cc", (far, far, w_feed, own, near_x)
        )
        left, right = glue(
            (near_x, x_far, y_far),
            (at_feed, (0, 0, tall, 0), (1, 0, tall, 0)),
            (at_feed, (2, tall, 2 * tall, 0)),
        )
        crossed, crossed_more, feed_one, near_y_core, far_core = stage(
            "yx1cc", (left, right, w_feed, near_y, far), feed_two, own_core, near_x_core
        )
        x_far_core, y_far_core, crossed_core, crossed_more_core = stage(
            "cccc", (x_far, y_far, crossed, crossed_more), feed_one, near_y_core, far_core
        )
        near = (own, near_x, near_y)
        near_core = (own_core, near_x_core, near_y_core)
        rest = (1, 2, 3)
        qkv_parts = both(
            [
                *((array, (chip, (0,), 0)) for chip, array in enumerate(near)),
                (far, (0, rest, 0)),
                (x_far, (1, rest, 0)),
                (y_far, (2, rest, 0)),
                (crossed, (3, (0, 1), 0)),
                (crossed_more, (3, (2, 3), 0)),
            ],
            [*near_core, far_core, x_far_core, y_far_core, crossed_core, crossed_more_core],
        )
        pair, near_x_down = glue(
            (feed_one, feed_two, near_x),
            (cols_feed, (0, 0, tall, 0), (1, 0, tall, 0)),
            (w_down.shape[0] // tall * width, (2, 0, tall, at_down)),
        )
        x_pair, y_pair, feed_three, pair_core = stage(
            "xy3c", (pair, pair, w_feed, pair), y_far_core, crossed_core, crossed_more_core
        )
        first = after(tokens, pair)
    else:
        first = tokens
        w_feed = jnp.concatenate([w_out, w_in], axis=1)
        qkv_parts = whole(lax.all_gather(w_qkv, BOTH, axis=0, tiled=True))
        feed_parts = whole(lax.all_gather(w_feed, BOTH, axis=0, tiled=True))
        down_parts = whole(lax.all_gather(w_down, BOTH, axis=0, tiled=True))
    qkv = project(scalars, seqs, first, qkv_parts, bias, scale)
    if special:
        x_last, y_last, cross_down, down_one, down_two = stage(
            "xyy12", (feed_three, feed_three, near_x_down, w_down, w_down), qkv, pair_core
        )
    attended = []
    for seq in range(seqs):
        if special and seq == 1:
            x_last, y_last, *attended = after((x_last, y_last, *attended), cross_down, down_one)
            left, right = glue(
                (near_x, x_pair, y_pair, y_last),
                (cols_feed, (0, 0, tall, at_feed), (1, 0, tall, 0)),
                (cols_feed, (2, tall, tall, 0), (3, 0, tall, 0)),
            )
            crossed, crossed_more, down_three, x_pair_core, y_pair_core = stage(
                "yx3cc", (left, right, w_down, x_pair, y_pair), x_last, *attended
            )
        attended = attend(scalars, qkv, width, seq, attended)
    context, powers, inverse = attended
    if special:
        cores = stage(
            "ccccc", (feed_three, x_last, y_last, crossed, crossed_more), context, down_three
        )
        feed_parts = both(
            [
                *((array, (chip, (0,), at_feed)) for chip, array in enumerate(near)),
                (pair, (0, (1, 2), 0)),
                (x_pair, (1, (1, 2), 0)),
                (y_pair, (2, (1, 2), 0)),
                (feed_three, (0, (3,), 0)),
                (x_last, (1, (3,), 0)),
                (y_last, (2, (3,), 0)),
                (crossed, (3, (0, 1), 0)),
                (crossed_more, (3, (2, 3), 0)),
            ],
            [*near_core, pair_core, x_pair_core, y_pair_core, *cores],
        )
        (far,) = glue(
            (down_one, down_two, down_three),
            (width, *((n, 0, w_down.shape[0], 0) for n in range(3))),
        )
        x_far, y_far, *diagonal = stage(
            "xy123", (far, far, cross_down, cross_down, cross_down), *cores
        )
    normed, spread, gl, gp = join(
        scalars, seqs, tokens, context, feed_parts, vectors, bias_in[None]
    )
    if special:
        x_far, cross_down, gl = after((x_far, cross_down, gl), y_far, *diagonal)
    if special:
        mine = [
            (after(far, x_far), (0, rest, 0)),
            (x_far, (1, rest, 0)),
            (y_far, (2, rest, 0)),
            (cross_down, (3, (0,), 0)),
            *((block, (3, (k,), 0)) for block, k in zip(diagonal, rest)),
        ]
        down_parts = both(
            [*((array, (chip, (0,), at_down)) for chip, array in enumerate(near)), *mine],
            [*near_core, *(over_core(block) for block, _ in mine)],
        )
    output, d_joined, d_context, sums, sum_in = turn(
        scalars, seqs, gl, gp, normed, spread, cotangent, feed_parts, down_parts, vectors
    )
    input_grad, sum_q = back(scalars, seqs, qkv, context, d_context, inverse, powers, d_joined, qkv_parts)
    devices = lax.axis_size("dp") * lax.axis_size("fsdp")
    parts = (sum_q[0], sums[0], sums[1], sums[2], sum_in[0], sums[3], sums[4])
    rows = jnp.concatenate([part.reshape(devices, -1) for part in parts], axis=1)
    mine = jnp.sum(lax.all_to_all(rows, BOTH, 0, 0, tiled=True), axis=0)
    small = width // devices
    sizes = (small, small, small, small, sum_in.shape[1] // devices, small, small)
    shares, at = [], 0
    for size in sizes:
        shares.append(mine[at : at + size])
        at += size
    return (output, input_grad, *shares)


def solution(mesh):
    split, rows, copied = P(BOTH), P(BOTH, None), P()
    in_specs = (rows, split, rows, rows, rows, rows, *([copied] * 9), rows)
    out_specs = (rows, rows, *([split] * 7))
    return jax.shard_map(
        on_device, mesh=mesh, in_specs=in_specs, out_specs=out_specs, check_vma=False
    )
```

```python
import functools
import math

import jax
import jax.numpy as jnp
from jax import lax
from jax.experimental import pallas as pl
from jax.experimental.pallas import tpu as pltpu
from jax.sharding import PartitionSpec as P

HD = 64
L = 512
LN_EPS = 1e-12
MIB = 2**20
BF = jnp.bfloat16
F32 = jnp.float32


def params(limit=60, semantics=None):
    return pltpu.CompilerParams(vmem_limit_bytes=limit * MIB, dimension_semantics=semantics)


def dot(left, right, on_left, on_right):
    return lax.dot_general(
        left, right, (((on_left,), (on_right,)), ((), ())), preferred_element_type=F32
    )


def shape_of(dims, kind):
    return jax.ShapeDtypeStruct(dims, kind)


def cost(flops):
    return pl.CostEstimate(flops=flops, bytes_accessed=0, transcendentals=0)


def issue(sources, buf, sem, place, height, window=0):
    plane_at, z_at, core_at = place
    cols = buf.shape[1]
    for source, tag in sources:
        if tag is None:
            pltpu.make_async_copy(source.at[:, pl.ds(window, cols)], buf, sem).start()
            continue
        chip, zs, first, turned = tag
        tall = source.shape[0] // len(zs)
        for step, z in enumerate(zs):
            row = ((plane_at ^ chip) * 8 + (z_at ^ z) * 2 + (core_at ^ turned)) * height
            for block in range(height // tall):
                pltpu.make_async_copy(
                    source.at[pl.ds(step * tall, tall), pl.ds(first + window + block * cols, cols)],
                    buf.at[pl.ds(pl.multiple_of(row + block * tall, tall), tall)],
                    sem,
                ).start()


def settle(buf, sem):
    pltpu.make_async_copy(buf, buf, sem).wait()


def tagged(refs, tags):
    return list(zip(refs, tags))


def tags_of(sources):
    return [tag for _, tag in sources]


def arrays_of(sources):
    return [array for array, _ in sources]


def place_of(scalars, seqs):
    return scalars[seqs], scalars[seqs + 1], scalars[seqs + 2]


ANYWHERE = pl.BlockSpec(memory_space=pl.ANY)

def pack_body(qkv_ref, out_ref, in_ref, down_ref, own_ref, feed_ref, sem):
    height = qkv_ref.shape[0]
    copies, at = [], 0
    for ref in (qkv_ref, out_ref, in_ref):
        copies.append(pltpu.make_async_copy(ref, own_ref.at[:, pl.ds(at, ref.shape[1])], sem))
        at += ref.shape[1]
    for first in range(0, down_ref.shape[0], height):
        window = down_ref.at[pl.ds(first, height)]
        copies.append(pltpu.make_async_copy(window, own_ref.at[:, pl.ds(at, down_ref.shape[1])], sem))
        at += down_ref.shape[1]
    for copy in copies:
        copy.start()
    settle(own_ref, sem)
    first = qkv_ref.shape[1]
    feed_ref[...] = own_ref[:, first : first + feed_ref.shape[1]]


def pack(w_qkv, w_out, w_in, w_down):
    height = w_qkv.shape[0]
    feed_wide = w_out.shape[1] + w_in.shape[1]
    wide = w_qkv.shape[1] + feed_wide + w_down.shape[0] // height * w_down.shape[1]
    return pl.pallas_call(
        pack_body,
        out_shape=(shape_of((height, wide), BF), shape_of((height, feed_wide), BF)),
        in_specs=[ANYWHERE] * 4,
        scratch_shapes=[pltpu.SemaphoreType.DMA],
        compiler_params=params(),
        name="pack",
    )(w_qkv, w_out, w_in, w_down)


def glue_body(plans, count, *refs):
    sources, targets = refs[:count], refs[count:]
    for plan, target in zip(plans, targets):
        at = 0
        for number, top, rows, left in plan:
            target[at : at + rows, :] = sources[number][top : top + rows, left : left + target.shape[1]]
            at += rows


def glue(arrays, *plans):
    return pl.pallas_call(
        functools.partial(glue_body, [plan[1:] for plan in plans], len(arrays)),
        out_shape=[shape_of((sum(w[2] for w in plan[1:]), plan[0]), BF) for plan in plans],
        compiler_params=params(20),
        name="glue",
    )(*arrays)


def project_body(seqs, tags, len_ref, x_ref, bias_ref, scale_ref, *refs):
    sources, (out_ref, buf, sems) = tagged(refs, tags), refs[len(tags) :]
    here = pl.program_id(0)
    step = out_ref.shape[1]

    @pl.when(here == 0)
    def _():
        place = place_of(len_ref, seqs)
        for part in range(buf.shape[0]):
            issue(sources, buf.at[part], sems.at[part], place, buf.shape[1] // 32, part * step)

    settle(buf.at[here], sems.at[here])
    total = dot(x_ref[...], buf[here], 1, 0) + bias_ref[...]
    out_ref[...] = (total * scale_ref[...]).astype(BF)


def project(scalars, seqs, rows, sources, bias, scale):
    count, width = rows.shape
    wide = bias.shape[1]
    step = PROJECT
    return pl.pallas_call(
        functools.partial(project_body, seqs, tags_of(sources)),
        out_shape=shape_of((count, wide), BF),
        grid_spec=pltpu.PrefetchScalarGridSpec(
            num_scalar_prefetch=1,
            grid=(wide // step,),
            in_specs=[
                pl.BlockSpec((count, width), lambda j, n: (0, 0)),
                pl.BlockSpec((1, step), lambda j, n: (0, j)),
                pl.BlockSpec((1, step), lambda j, n: (0, j)),
                *([ANYWHERE] * len(sources)),
            ],
            out_specs=pl.BlockSpec((count, step), lambda j, n: (0, j)),
            scratch_shapes=[
                pltpu.VMEM((wide // step, width, step), BF),
                pltpu.SemaphoreType.DMA((wide // step,)),
            ],
        ),
        compiler_params=params(),
        cost_estimate=cost(2 * count * width * wide),
        name="project",
    )(scalars, rows, bias, scale, *arrays_of(sources))


PROJECT = 512


def lane_halves(kind):
    lane = lax.broadcasted_iota(jnp.int32, (1, 128), 1)
    return [(lane < HD).astype(F32).astype(kind), (lane >= HD).astype(F32).astype(kind)]


QUAD = 256


def attend_body(seq, len_ref, q_ref, k_ref, v_ref, *refs):
    o_ref, e_ref, r_ref = refs[-3:]
    length = len_ref[seq]
    halves = lane_halves(BF)
    lane = lax.broadcasted_iota(jnp.int32, (L, 128), 1)
    row = lax.broadcasted_iota(jnp.int32, (L, 128), 0)
    q_side = jnp.where(lane == 0, 1.0, 0.0).astype(BF)
    k_side = jnp.where((lane == 0) & (row >= length), -1e30, 0.0).astype(BF)
    for pair in range(QUAD // 128):
        part = slice(pair * 128, (pair + 1) * 128)
        q_pair = jnp.concatenate([q_ref[:, part], q_side], axis=1)
        k_pair = k_ref[:, part]
        v_pair = v_ref[:, part]
        powers = []
        for head in range(2):
            k_one = jnp.concatenate([k_pair * halves[head], k_side], axis=1)
            scores = dot(q_pair, k_one, 1, 1)
            peak = jnp.max(scores, axis=1, keepdims=True)
            power = jnp.exp(scores - peak).astype(BF)
            e_ref[2 * pair + head] = power
            powers.append(power)
        right = jnp.concatenate(
            [
                jnp.concatenate([v_pair * half, jnp.broadcast_to(half, (L, 128))], axis=1)
                for half in halves
            ],
            axis=0,
        )
        both = dot(jnp.concatenate(powers, axis=1), right, 1, 0)
        inverse = 1.0 / both[:, 128:]
        r_ref[:, part] = inverse
        o_ref[:, part] = (both[:, :128] * inverse).astype(BF)


def attend(scalars, qkv, width, seq, earlier):
    count = qkv.shape[0]
    quads = width // QUAD
    heads = QUAD // HD
    return pl.pallas_call(
        functools.partial(attend_body, seq),
        out_shape=(
            shape_of((count, width), BF),
            shape_of((count // L * width // HD, L, L), BF),
            shape_of((count, width), F32),
        ),
        grid_spec=pltpu.PrefetchScalarGridSpec(
            num_scalar_prefetch=1,
            grid=(quads,),
            in_specs=[
                pl.BlockSpec((L, QUAD), lambda j, n: (seq, j)),
                pl.BlockSpec((L, QUAD), lambda j, n: (seq, quads + j)),
                pl.BlockSpec((L, QUAD), lambda j, n: (seq, 2 * quads + j)),
                *([ANYWHERE] * len(earlier)),
            ],
            out_specs=[
                pl.BlockSpec((L, QUAD), lambda j, n: (seq, j)),
                pl.BlockSpec((heads, L, L), lambda j, n: (seq * quads + j, 0, 0)),
                pl.BlockSpec((L, QUAD), lambda j, n: (seq, j)),
            ],
        ),
        compiler_params=params(),
        input_output_aliases={4 + n: n for n in range(len(earlier))},
        cost_estimate=cost(16 * L * width * L),
        name="attend",
    )(scalars, qkv, qkv, qkv, *earlier)


ROWS = 256
FEED = 512


def hidden(rounded, buf, bi_ref, gl_ref, gp_ref):
    for part in range(gl_ref.shape[1] // FEED):
        cols = slice(part * FEED, (part + 1) * FEED)
        pre = dot(rounded, buf[:, cols], 1, 0) + bi_ref[:, cols]
        phi = 0.5 + 0.5 * lax.erf(pre * math.sqrt(0.5))
        power = (-0.5 / math.log(2.0)) * pre * pre - 0.5 * math.log2(2.0 * math.pi)
        gl_ref[:, cols] = (pre * phi).astype(BF)
        gp_ref[:, cols] = (phi + pre * jnp.exp2(power)).astype(BF)


def join_body(seqs, tags, len_ref, x_ref, o_ref, vec_ref, bi_ref, *refs):
    sources = tagged(refs, tags)
    u_ref, s_ref, gl_ref, gp_ref, out, buf, sems = refs[-7:]
    width = x_ref.shape[1]

    @pl.when(pl.program_id(0) == 0)
    def _():
        place = place_of(len_ref, seqs)
        issue(sources, out, sems.at[0], place, width // 32)
        issue(sources, buf, sems.at[1], place, width // 32, width)
        settle(out, sems.at[0])

    joined = dot(o_ref[...], out[...], 1, 0) + vec_ref[0:1, :] + x_ref[...].astype(F32)
    centered = joined - jnp.mean(joined, axis=1, keepdims=True)
    spread = lax.rsqrt(jnp.mean(centered * centered, axis=1, keepdims=True) + LN_EPS)
    normed = centered * spread * vec_ref[1:2, :] + vec_ref[2:3, :]
    u_ref[...] = normed
    s_ref[...] = jnp.broadcast_to(spread, s_ref.shape)
    rounded = normed.astype(BF)
    pl.when(pl.program_id(0) == 0)(functools.partial(settle, buf, sems.at[1]))
    hidden(rounded, buf, bi_ref, gl_ref, gp_ref)


def join(scalars, seqs, rows, context, sources, vectors, bias_in):
    count, width = rows.shape
    wide = bias_in.shape[1]
    block = lambda cols: pl.BlockSpec((ROWS, cols), lambda i, n: (i, 0))
    return pl.pallas_call(
        functools.partial(join_body, seqs, tags_of(sources)),
        out_shape=(
            shape_of((count, width), F32),
            shape_of((count, 128), F32),
            shape_of((count, wide), BF),
            shape_of((count, wide), BF),
        ),
        grid_spec=pltpu.PrefetchScalarGridSpec(
            num_scalar_prefetch=1,
            grid=(count // ROWS,),
            in_specs=[
                block(width),
                block(width),
                pl.BlockSpec((8, width), lambda i, n: (0, 0)),
                pl.BlockSpec((1, wide), lambda i, n: (0, 0)),
                *([ANYWHERE] * len(sources)),
            ],
            out_specs=[block(width), block(128), block(wide), block(wide)],
            scratch_shapes=[
                pltpu.VMEM((width, width), BF),
                pltpu.VMEM((width, wide), BF),
                pltpu.SemaphoreType.DMA((2,)),
            ],
        ),
        compiler_params=params(),
        cost_estimate=cost(2 * count * width * (width + wide)),
        name="join",
    )(scalars, rows, context, vectors, bias_in, *arrays_of(sources))


TURN = 256


def turn_body(
    seqs, feed_tags, down_tags, len_ref, gl_ref, u_ref, s_ref, c_ref, vec_ref, gp_any, *refs
):
    feeds, downs = tagged(refs, feed_tags), tagged(refs[len(feed_tags) :], down_tags)
    y_ref, dh_ref, do_ref, gv_ref, gi_ref, out, buf, down, gp_ref, sems, gp_sems = refs[-11:]
    index = pl.program_id(0)
    first = index == 0
    width = u_ref.shape[1]
    wide = gl_ref.shape[1]
    parts = 4
    step = wide // parts
    steps = gp_ref.shape[0]
    slopes = [
        pltpu.make_async_copy(gp_any.at[pl.ds(n * TURN, TURN)], gp_ref.at[n], gp_sems.at[n])
        for n in range(steps)
    ]

    @pl.when(first)
    def _():
        place = place_of(len_ref, seqs)
        issue(downs, down, sems.at[0], place, wide // 32)
        slopes[0].start()
        issue(feeds, buf, sems.at[1], place, width // 32, width)
        issue(feeds, out, sems.at[2], place, width // 32)
        for copy in slopes[1:]:
            copy.start()
        gv_ref[...] = jnp.zeros_like(gv_ref)
        gi_ref[...] = jnp.zeros_like(gi_ref)
        settle(down, sems.at[0])

    gain_one, beta_one, gain_two, beta_two, bias_down = (vec_ref[n : n + 1, :] for n in range(1, 6))
    normed = u_ref[...]
    total = normed + bias_down + dot(gl_ref[...], down[...], 1, 0)
    centered = total - jnp.mean(total, axis=1, keepdims=True)
    spread = lax.rsqrt(jnp.mean(centered * centered, axis=1, keepdims=True) + LN_EPS)
    hat = centered * spread
    y_ref[...] = (hat * gain_two + beta_two).astype(BF)
    per_seq = L // TURN
    start = lax.rem(index, per_seq) * TURN
    live = lax.broadcasted_iota(jnp.int32, (TURN, 1), 0) + start < len_ref[index // per_seq]
    dy = jnp.where(live, c_ref[...].astype(F32), 0.0)
    gv_ref[4:5, :] += jnp.sum(dy, axis=0, keepdims=True)
    scaled = dy * gain_two
    d_two = spread * (
        scaled
        - jnp.mean(scaled, axis=1, keepdims=True)
        - hat * jnp.mean(scaled * hat, axis=1, keepdims=True)
    )
    d_branch = d_two.astype(BF)
    gv_ref[3:4, :] += jnp.sum(d_branch.astype(F32), axis=0, keepdims=True)
    pl.when(first)(functools.partial(settle, buf, sems.at[1]))
    for n in range(steps):
        pl.when(index == n)(slopes[n].wait)
    total = d_two
    for part in range(parts):
        rows = slice(part * step, (part + 1) * step)
        d_hidden = dot(d_branch, down[rows, :], 1, 1) * gp_ref[index, :, rows].astype(F32)
        d_hidden = d_hidden.astype(BF)
        gi_ref[:, rows] += jnp.sum(d_hidden.astype(F32), axis=0, keepdims=True)
        total = total + dot(d_hidden, buf[:, rows], 1, 1)
    gv_ref[2:3, :] += jnp.sum(total, axis=0, keepdims=True)
    scaled = total * gain_one
    hat = (normed - beta_one) * (1.0 / gain_one)
    d_one = s_ref[:, 0:1] * (
        scaled
        - jnp.mean(scaled, axis=1, keepdims=True)
        - hat * jnp.mean(scaled * hat, axis=1, keepdims=True)
    )
    dh_ref[...] = d_one
    d_att = d_one.astype(BF)
    gv_ref[1:2, :] += jnp.sum(d_att.astype(F32), axis=0, keepdims=True)

    pl.when(first)(functools.partial(settle, out, sems.at[2]))
    d_context = dot(d_att, out[...], 1, 1).astype(BF)
    do_ref[...] = d_context
    gv_ref[0:1, :] += jnp.sum(d_context.astype(F32), axis=0, keepdims=True)


def turn(scalars, seqs, gl, gp, normed, spread, cotangent, feeds, downs, vectors):
    count, width = normed.shape
    wide = gl.shape[1]
    steps = count // TURN
    block = lambda cols: pl.BlockSpec((TURN, cols), lambda i, n: (i, 0))
    return pl.pallas_call(
        functools.partial(turn_body, seqs, tags_of(feeds), tags_of(downs)),
        out_shape=(
            shape_of((count, width), BF),
            shape_of((count, width), F32),
            shape_of((count, width), BF),
            shape_of((8, width), F32),
            shape_of((1, wide), F32),
        ),
        grid_spec=pltpu.PrefetchScalarGridSpec(
            num_scalar_prefetch=1,
            grid=(steps,),
            in_specs=[
                block(wide),
                block(width),
                block(128),
                block(width),
                pl.BlockSpec((8, width), lambda i, n: (0, 0)),
                *([ANYWHERE] * (1 + len(feeds) + len(downs))),
            ],
            out_specs=[
                block(width),
                block(width),
                block(width),
                pl.BlockSpec((8, width), lambda i, n: (0, 0)),
                pl.BlockSpec((1, wide), lambda i, n: (0, 0)),
            ],
            scratch_shapes=[
                pltpu.VMEM((width, width), BF),
                pltpu.VMEM((width, wide), BF),
                pltpu.VMEM((wide, width), BF),
                pltpu.VMEM((steps, TURN, wide), BF),
                pltpu.SemaphoreType.DMA((3,)),
                pltpu.SemaphoreType.DMA((steps,)),
            ],
        ),
        compiler_params=params(),
        cost_estimate=cost(2 * count * width * (width + 3 * wide)),
        name="turn",
    )(
        scalars, gl, normed, spread, cotangent, vectors, gp, *arrays_of(feeds), *arrays_of(downs)
    )


WIDE = 512


def back_body(
    seqs, tags, len_ref, q_ref, k_ref, v_ref, o_ref, do_ref, r_ref, e_ref, dh_any, *refs
):
    sources = tagged(refs, tags)
    dx_ref, gq_ref, all_ref, w_ref, dh_ref, sem, dh_sem = refs[len(tags) :]
    seq, quad = pl.program_id(0), pl.program_id(1)
    quads = pl.num_programs(1)
    width = dx_ref.shape[1]
    rows = pl.ds(pl.multiple_of(seq * L, L), L)
    joined = pltpu.make_async_copy(dh_any.at[rows], dh_ref, dh_sem)
    pl.when(quad == 0)(joined.start)

    @pl.when((seq == 0) & (quad == 0))
    def _():
        issue(sources, w_ref, sem, place_of(len_ref, seqs), width // 32)
        gq_ref[...] = jnp.zeros_like(gq_ref)

    halves = lane_halves(BF)
    halves_wide = lane_halves(F32)
    lane = lax.broadcasted_iota(jnp.int32, (L, 128), 1)
    for pair in range(WIDE // 128):
        part = slice(pair * 128, (pair + 1) * 128)
        q_pair, k_pair, v_pair = (r[:, part] for r in (q_ref, k_ref, v_ref))
        do_pair = (do_ref[:, part].astype(F32) * r_ref[:, part]).astype(BF)
        products = do_pair.astype(F32) * o_ref[:, part].astype(F32)
        shifts = [jnp.sum(products * half, axis=1, keepdims=True) for half in halves_wide]
        rough = [shift.astype(BF).astype(F32) for shift in shifts]
        side = jnp.where(
            lane == 0,
            -rough[0],
            jnp.where(
                lane == 1,
                rough[0] - shifts[0],
                jnp.where(lane == 2, -rough[1], jnp.where(lane == 3, rough[1] - shifts[1], 0.0)),
            ),
        ).astype(BF)
        left = jnp.concatenate([do_pair, side], axis=1)
        q_turned = q_pair.T
        do_turned = do_pair.T
        d_scores, d_keys, d_values = [], [], []
        for head in range(2):
            rows = slice(head * HD, (head + 1) * HD)
            power = e_ref[2 * pair + head]
            marks = jnp.where(lane // 2 == head, 1.0, 0.0).astype(BF)
            right = jnp.concatenate([v_pair * halves[head], marks], axis=1)
            d_score = (power.astype(F32) * dot(left, right, 1, 1)).astype(BF)
            d_scores.append(d_score)
            d_keys.append(dot(q_turned[rows], d_score, 1, 0))
            d_values.append(dot(do_turned[rows], power, 1, 0))
        right = jnp.concatenate([k_pair * half for half in halves], axis=0)
        d_query = (dot(jnp.concatenate(d_scores, axis=1), right, 1, 0) * (HD**-0.5)).astype(BF)
        cols = pl.multiple_of(quad * WIDE + pair * 128, 128)
        gq_ref[:, pl.ds(cols, 128)] += jnp.sum(d_query.astype(F32), axis=0, keepdims=True)
        all_ref[:, pl.ds(cols, 128)] = d_query
        all_ref[:, pl.ds(width + cols, 128)] = jnp.concatenate(d_keys, axis=0).T.astype(BF)
        all_ref[:, pl.ds(2 * width + cols, 128)] = jnp.concatenate(d_values, axis=0).T.astype(BF)

    pl.when((seq == 0) & (quad == quads - 1))(functools.partial(settle, w_ref, sem))

    @pl.when(quad == quads - 1)
    def _():
        joined.wait()
        dx_ref[...] = (dh_ref[...] + dot(all_ref[...], w_ref[...], 1, 1)).astype(BF)


def back(scalars, seqs, qkv, context, d_context, inverse, powers, d_joined, sources):
    count, width = d_joined.shape
    quads = width // WIDE
    heads = WIDE // HD
    col = lambda n: pl.BlockSpec((L, WIDE), lambda i, j, s: (i, n * quads + j))
    return pl.pallas_call(
        functools.partial(back_body, seqs, tags_of(sources)),
        out_shape=(shape_of((count, width), BF), shape_of((1, width), F32)),
        grid_spec=pltpu.PrefetchScalarGridSpec(
            num_scalar_prefetch=1,
            grid=(seqs, quads),
            in_specs=[
                col(0),
                col(1),
                col(2),
                col(0),
                col(0),
                col(0),
                pl.BlockSpec((heads, L, L), lambda i, j, s: (i * quads + j, 0, 0)),
                *([ANYWHERE] * (1 + len(sources))),
            ],
            out_specs=[
                pl.BlockSpec((L, width), lambda i, j, s: (i, 0)),
                pl.BlockSpec((1, width), lambda i, j, s: (0, 0)),
            ],
            scratch_shapes=[
                pltpu.VMEM((L, 3 * width), BF),
                pltpu.VMEM((width, 3 * width), BF),
                pltpu.VMEM((L, width), F32),
                pltpu.SemaphoreType.DMA,
                pltpu.SemaphoreType.DMA,
            ],
        ),
        compiler_params=params(),
        cost_estimate=cost(2 * count * width * 3 * width + 20 * count * width * L),
        name="back",
    )(scalars, qkv, qkv, qkv, context, d_context, inverse, powers, d_joined, *arrays_of(sources))


BOTH = ("dp", "fsdp")


def hop(block, axis, flip):
    size = lax.axis_size(axis)
    return lax.ppermute(block, axis, [(i, i ^ flip) for i in range(size)])


def after_all(*values):
    return lax.optimization_barrier(values)


def over_x(block):
    return hop(block, "dp", 1)


def over_y(block):
    return hop(block, "dp", 2)


def over_core(block):
    return hop(block, "fsdp", 1)


def over_z(block, k):
    return hop(block, "fsdp", 2 * k)


def after(value, *earlier):
    return lax.optimization_barrier((value, *earlier))[0]


MOVES = {
    "x": over_x,
    "y": over_y,
    "c": over_core,
    "1": functools.partial(over_z, k=1),
    "2": functools.partial(over_z, k=2),
    "3": functools.partial(over_z, k=3),
}


def stage(lanes, blocks, *earlier):
    blocks = after(tuple(blocks), *earlier)
    return lax.optimization_barrier(tuple(MOVES[lane](block) for lane, block in zip(lanes, blocks)))


def both(mine, others):
    return [(array, (*tag, 0)) for array, tag in mine] + [
        (array, (*tag, 1)) for array, (_, tag) in zip(others, mine)
    ]


def whole(array):
    return [(array, None)]


def on_device(
    tokens, lengths, w_qkv, w_out, w_in, w_down, gain_one, gain_two,
    bias_q, bias_v, bias_out, beta_one, bias_in, bias_down, beta_two, cotangent,
):
    width = w_out.shape[1]
    seqs = lengths.shape[0]
    chip = lax.axis_index("fsdp")
    scalars = jnp.concatenate(
        [lengths, jnp.stack([lax.axis_index("dp"), chip // 2, chip % 2]).astype(jnp.int32)]
    )
    score_scale = HD**-0.5
    ones = jnp.ones((width,), F32)
    zeros = jnp.zeros((width,), F32)
    bias = jnp.concatenate([bias_q, zeros, bias_v])[None]
    scale = jnp.concatenate([ones * score_scale, ones, ones])[None]
    vectors = jnp.stack([bias_out, gain_one, beta_one, gain_two, beta_two, bias_down, zeros, zeros])
    special = (lax.axis_size("dp"), lax.axis_size("fsdp")) == (4, 8)
    if special:
        own, w_feed = pack(w_qkv, w_out, w_in, w_down)
        at_feed = w_qkv.shape[1]
        at_down = at_feed + w_feed.shape[1]
        z_two, z_three, z_one, near_x, near_y = stage("231xy", (w_qkv, w_qkv, w_qkv, own, own))
        tall, cols_feed = w_qkv.shape[0], w_feed.shape[1]
        z_one, scalars, bias, scale, vectors = after_all(z_one, scalars, bias, scale, vectors)
        (far,) = glue(
            (z_one, z_two, z_three), (at_feed, *((n, 0, tall, 0) for n in range(3)))
        )
        x_far, y_far, feed_two, own_core, near_x_core = stage(
            "xy2cc", (far, far, w_feed, own, near_x)
        )
        left, right = glue(
            (near_x, x_far, y_far),
            (at_feed, (0, 0, tall, 0), (1, 0, tall, 0)),
            (at_feed, (2, tall, 2 * tall, 0)),
        )
        crossed, crossed_more, feed_one, near_y_core, far_core = stage(
            "yx1cc", (left, right, w_feed, near_y, far), feed_two, own_core, near_x_core
        )
        x_far_core, y_far_core, crossed_core, crossed_more_core = stage(
            "cccc", (x_far, y_far, crossed, crossed_more), feed_one, near_y_core, far_core
        )
        near = (own, near_x, near_y)
        near_core = (own_core, near_x_core, near_y_core)
        rest = (1, 2, 3)
        qkv_parts = both(
            [
                *((array, (chip, (0,), 0)) for chip, array in enumerate(near)),
                (far, (0, rest, 0)),
                (x_far, (1, rest, 0)),
                (y_far, (2, rest, 0)),
                (crossed, (3, (0, 1), 0)),
                (crossed_more, (3, (2, 3), 0)),
            ],
            [*near_core, far_core, x_far_core, y_far_core, crossed_core, crossed_more_core],
        )
        pair, near_x_down = glue(
            (feed_one, feed_two, near_x),
            (cols_feed, (0, 0, tall, 0), (1, 0, tall, 0)),
            (w_down.shape[0] // tall * width, (2, 0, tall, at_down)),
        )
        x_pair, y_pair, feed_three, pair_core = stage(
            "xy3c", (pair, pair, w_feed, pair), y_far_core, crossed_core, crossed_more_core
        )
        first = after(tokens, pair)
    else:
        first = tokens
        w_feed = jnp.concatenate([w_out, w_in], axis=1)
        qkv_parts = whole(lax.all_gather(w_qkv, BOTH, axis=0, tiled=True))
        feed_parts = whole(lax.all_gather(w_feed, BOTH, axis=0, tiled=True))
        down_parts = whole(lax.all_gather(w_down, BOTH, axis=0, tiled=True))
    qkv = project(scalars, seqs, first, qkv_parts, bias, scale)
    if special:
        x_last, y_last, down_two, down_one, cross_down = stage(
            "xy21y", (feed_three, feed_three, w_down, w_down, near_x_down), qkv, pair_core
        )
    attended = []
    for seq in range(seqs):
        if special and seq == 1:
            x_last, y_last, *attended = after((x_last, y_last, *attended), cross_down, down_one)
            left, right = glue(
                (near_x, x_pair, y_pair, y_last),
                (cols_feed, (0, 0, tall, at_feed), (1, 0, tall, 0)),
                (cols_feed, (2, tall, tall, 0), (3, 0, tall, 0)),
            )
            crossed, crossed_more, down_three, x_pair_core, y_pair_core = stage(
                "yx3cc", (left, right, w_down, x_pair, y_pair), x_last, *attended
            )
        attended = attend(scalars, qkv, width, seq, attended)
    context, powers, inverse = attended
    if special:
        cores = stage(
            "ccccc", (feed_three, x_last, y_last, crossed, crossed_more), context, down_three
        )
        feed_parts = both(
            [
                *((array, (chip, (0,), at_feed)) for chip, array in enumerate(near)),
                (pair, (0, (1, 2), 0)),
                (x_pair, (1, (1, 2), 0)),
                (y_pair, (2, (1, 2), 0)),
                (feed_three, (0, (3,), 0)),
                (x_last, (1, (3,), 0)),
                (y_last, (2, (3,), 0)),
                (crossed, (3, (0, 1), 0)),
                (crossed_more, (3, (2, 3), 0)),
            ],
            [*near_core, pair_core, x_pair_core, y_pair_core, *cores],
        )
        (far,) = glue(
            (down_one, down_two, down_three),
            (width, *((n, 0, w_down.shape[0], 0) for n in range(3))),
        )
        x_far, y_far, *diagonal = stage(
            "xy231", (far, far, cross_down, cross_down, cross_down), *cores
        )
    normed, spread, gl, gp = join(
        scalars, seqs, tokens, context, feed_parts, vectors, bias_in[None]
    )
    if special:
        x_far, cross_down, gl = after((x_far, cross_down, gl), y_far, *diagonal)
    if special:
        mine = [
            (after(far, x_far), (0, rest, 0)),
            (x_far, (1, rest, 0)),
            (y_far, (2, rest, 0)),
            (cross_down, (3, (0,), 0)),
            *((block, (3, (k,), 0)) for block, k in zip(diagonal, (2, 3, 1))),
        ]
        down_parts = both(
            [*((array, (chip, (0,), at_down)) for chip, array in enumerate(near)), *mine],
            [*near_core, *(over_core(block) for block, _ in mine)],
        )
    output, d_joined, d_context, sums, sum_in = turn(
        scalars, seqs, gl, gp, normed, spread, cotangent, feed_parts, down_parts, vectors
    )
    input_grad, sum_q = back(scalars, seqs, qkv, context, d_context, inverse, powers, d_joined, qkv_parts)
    devices = lax.axis_size("dp") * lax.axis_size("fsdp")
    parts = (sum_q[0], sums[0], sums[1], sums[2], sum_in[0], sums[3], sums[4])
    rows = jnp.concatenate([part.reshape(devices, -1) for part in parts], axis=1)
    mine = jnp.sum(lax.all_to_all(rows, BOTH, 0, 0, tiled=True), axis=0)
    small = width // devices
    sizes = (small, small, small, small, sum_in.shape[1] // devices, small, small)
    shares, at = [], 0
    for size in sizes:
        shares.append(mine[at : at + size])
        at += size
    return (output, input_grad, *shares)


def solution(mesh):
    split, rows, copied = P(BOTH), P(BOTH, None), P()
    in_specs = (rows, split, rows, rows, rows, rows, *([copied] * 9), rows)
    out_specs = (rows, rows, *([split] * 7))
    return jax.shard_map(
        on_device, mesh=mesh, in_specs=in_specs, out_specs=out_specs, check_vma=False
    )
```

```python
import functools
import math

import jax
import jax.numpy as jnp
from jax import lax
from jax.experimental import pallas as pl
from jax.experimental.pallas import tpu as pltpu
from jax.sharding import PartitionSpec as P

HD = 64
L = 512
LN_EPS = 1e-12
MIB = 2**20
BF = jnp.bfloat16
F32 = jnp.float32


def params(limit=60, semantics=None):
    return pltpu.CompilerParams(vmem_limit_bytes=limit * MIB, dimension_semantics=semantics)


def dot(left, right, on_left, on_right):
    return lax.dot_general(
        left, right, (((on_left,), (on_right,)), ((), ())), preferred_element_type=F32
    )


def shape_of(dims, kind):
    return jax.ShapeDtypeStruct(dims, kind)


def cost(flops):
    return pl.CostEstimate(flops=flops, bytes_accessed=0, transcendentals=0)


def issue(sources, buf, sem, place, height, window=0):
    plane_at, z_at, core_at = place
    cols = buf.shape[1]
    for source, tag in sources:
        if tag is None:
            pltpu.make_async_copy(source.at[:, pl.ds(window, cols)], buf, sem).start()
            continue
        chip, zs, first, turned = tag
        tall = source.shape[0] // len(zs)
        for step, z in enumerate(zs):
            row = ((plane_at ^ chip) * 8 + (z_at ^ z) * 2 + (core_at ^ turned)) * height
            for block in range(height // tall):
                pltpu.make_async_copy(
                    source.at[pl.ds(step * tall, tall), pl.ds(first + window + block * cols, cols)],
                    buf.at[pl.ds(pl.multiple_of(row + block * tall, tall), tall)],
                    sem,
                ).start()


def settle(buf, sem):
    pltpu.make_async_copy(buf, buf, sem).wait()


def tagged(refs, tags):
    return list(zip(refs, tags))


def tags_of(sources):
    return [tag for _, tag in sources]


def arrays_of(sources):
    return [array for array, _ in sources]


def place_of(scalars, seqs):
    return scalars[seqs], scalars[seqs + 1], scalars[seqs + 2]


ANYWHERE = pl.BlockSpec(memory_space=pl.ANY)

def pack_body(qkv_ref, out_ref, in_ref, down_ref, own_ref, feed_ref, sem):
    height = qkv_ref.shape[0]
    copies, at = [], 0
    for ref in (qkv_ref, out_ref, in_ref):
        copies.append(pltpu.make_async_copy(ref, own_ref.at[:, pl.ds(at, ref.shape[1])], sem))
        at += ref.shape[1]
    for first in range(0, down_ref.shape[0], height):
        window = down_ref.at[pl.ds(first, height)]
        copies.append(pltpu.make_async_copy(window, own_ref.at[:, pl.ds(at, down_ref.shape[1])], sem))
        at += down_ref.shape[1]
    for copy in copies:
        copy.start()
    settle(own_ref, sem)
    first = qkv_ref.shape[1]
    feed_ref[...] = own_ref[:, first : first + feed_ref.shape[1]]


def pack(w_qkv, w_out, w_in, w_down):
    height = w_qkv.shape[0]
    feed_wide = w_out.shape[1] + w_in.shape[1]
    wide = w_qkv.shape[1] + feed_wide + w_down.shape[0] // height * w_down.shape[1]
    return pl.pallas_call(
        pack_body,
        out_shape=(shape_of((height, wide), BF), shape_of((height, feed_wide), BF)),
        in_specs=[ANYWHERE] * 4,
        scratch_shapes=[pltpu.SemaphoreType.DMA],
        compiler_params=params(),
        name="pack",
    )(w_qkv, w_out, w_in, w_down)


def glue_body(plans, count, *refs):
    sources, targets = refs[:count], refs[count:]
    for plan, target in zip(plans, targets):
        at = 0
        for number, top, rows, left in plan:
            target[at : at + rows, :] = sources[number][top : top + rows, left : left + target.shape[1]]
            at += rows


def glue(arrays, *plans):
    return pl.pallas_call(
        functools.partial(glue_body, [plan[1:] for plan in plans], len(arrays)),
        out_shape=[shape_of((sum(w[2] for w in plan[1:]), plan[0]), BF) for plan in plans],
        compiler_params=params(20),
        name="glue",
    )(*arrays)


def project_body(seqs, tags, len_ref, x_ref, bias_ref, scale_ref, *refs):
    sources, (out_ref, buf, sems) = tagged(refs, tags), refs[len(tags) :]
    here = pl.program_id(0)
    step = out_ref.shape[1]

    @pl.when(here == 0)
    def _():
        place = place_of(len_ref, seqs)
        for part in range(buf.shape[0]):
            issue(sources, buf.at[part], sems.at[part], place, buf.shape[1] // 32, part * step)

    settle(buf.at[here], sems.at[here])
    total = dot(x_ref[...], buf[here], 1, 0) + bias_ref[...]
    out_ref[...] = (total * scale_ref[...]).astype(BF)


def project(scalars, seqs, rows, sources, bias, scale):
    count, width = rows.shape
    wide = bias.shape[1]
    step = PROJECT
    return pl.pallas_call(
        functools.partial(project_body, seqs, tags_of(sources)),
        out_shape=shape_of((count, wide), BF),
        grid_spec=pltpu.PrefetchScalarGridSpec(
            num_scalar_prefetch=1,
            grid=(wide // step,),
            in_specs=[
                pl.BlockSpec((count, width), lambda j, n: (0, 0)),
                pl.BlockSpec((1, step), lambda j, n: (0, j)),
                pl.BlockSpec((1, step), lambda j, n: (0, j)),
                *([ANYWHERE] * len(sources)),
            ],
            out_specs=pl.BlockSpec((count, step), lambda j, n: (0, j)),
            scratch_shapes=[
                pltpu.VMEM((wide // step, width, step), BF),
                pltpu.SemaphoreType.DMA((wide // step,)),
            ],
        ),
        compiler_params=params(),
        cost_estimate=cost(2 * count * width * wide),
        name="project",
    )(scalars, rows, bias, scale, *arrays_of(sources))


PROJECT = 512


def lane_halves(kind):
    lane = lax.broadcasted_iota(jnp.int32, (1, 128), 1)
    return [(lane < HD).astype(F32).astype(kind), (lane >= HD).astype(F32).astype(kind)]


QUAD = 256


def attend_body(seq, len_ref, q_ref, k_ref, v_ref, *refs):
    o_ref, e_ref, r_ref = refs[-3:]
    length = len_ref[seq]
    halves = lane_halves(BF)
    lane = lax.broadcasted_iota(jnp.int32, (L, 128), 1)
    row = lax.broadcasted_iota(jnp.int32, (L, 128), 0)
    q_side = jnp.where(lane == 0, 1.0, 0.0).astype(BF)
    k_side = jnp.where((lane == 0) & (row >= length), -1e30, 0.0).astype(BF)
    for pair in range(QUAD // 128):
        part = slice(pair * 128, (pair + 1) * 128)
        q_pair = jnp.concatenate([q_ref[:, part], q_side], axis=1)
        k_pair = k_ref[:, part]
        v_pair = v_ref[:, part]
        powers = []
        for head in range(2):
            k_one = jnp.concatenate([k_pair * halves[head], k_side], axis=1)
            scores = dot(q_pair, k_one, 1, 1)
            peak = jnp.max(scores, axis=1, keepdims=True)
            power = jnp.exp(scores - peak).astype(BF)
            e_ref[2 * pair + head] = power
            powers.append(power)
        right = jnp.concatenate(
            [
                jnp.concatenate([v_pair * half, jnp.broadcast_to(half, (L, 128))], axis=1)
                for half in halves
            ],
            axis=0,
        )
        both = dot(jnp.concatenate(powers, axis=1), right, 1, 0)
        inverse = 1.0 / both[:, 128:]
        r_ref[:, part] = inverse
        o_ref[:, part] = (both[:, :128] * inverse).astype(BF)


def attend(scalars, qkv, width, seq, earlier):
    count = qkv.shape[0]
    quads = width // QUAD
    heads = QUAD // HD
    return pl.pallas_call(
        functools.partial(attend_body, seq),
        out_shape=(
            shape_of((count, width), BF),
            shape_of((count // L * width // HD, L, L), BF),
            shape_of((count, width), F32),
        ),
        grid_spec=pltpu.PrefetchScalarGridSpec(
            num_scalar_prefetch=1,
            grid=(quads,),
            in_specs=[
                pl.BlockSpec((L, QUAD), lambda j, n: (seq, j)),
                pl.BlockSpec((L, QUAD), lambda j, n: (seq, quads + j)),
                pl.BlockSpec((L, QUAD), lambda j, n: (seq, 2 * quads + j)),
                *([ANYWHERE] * len(earlier)),
            ],
            out_specs=[
                pl.BlockSpec((L, QUAD), lambda j, n: (seq, j)),
                pl.BlockSpec((heads, L, L), lambda j, n: (seq * quads + j, 0, 0)),
                pl.BlockSpec((L, QUAD), lambda j, n: (seq, j)),
            ],
        ),
        compiler_params=params(),
        input_output_aliases={4 + n: n for n in range(len(earlier))},
        cost_estimate=cost(16 * L * width * L),
        name="attend",
    )(scalars, qkv, qkv, qkv, *earlier)


ROWS = 256
FEED = 512


def hidden(rounded, buf, bi_ref, gl_ref, gp_ref):
    for part in range(gl_ref.shape[1] // FEED):
        cols = slice(part * FEED, (part + 1) * FEED)
        pre = dot(rounded, buf[:, cols], 1, 0) + bi_ref[:, cols]
        phi = 0.5 + 0.5 * lax.erf(pre * math.sqrt(0.5))
        power = (-0.5 / math.log(2.0)) * pre * pre - 0.5 * math.log2(2.0 * math.pi)
        gl_ref[:, cols] = (pre * phi).astype(BF)
        gp_ref[:, cols] = (phi + pre * jnp.exp2(power)).astype(BF)


def join_body(seqs, tags, len_ref, x_ref, o_ref, vec_ref, bi_ref, *refs):
    sources = tagged(refs, tags)
    u_ref, s_ref, gl_ref, gp_ref, out, buf, sems = refs[-7:]
    width = x_ref.shape[1]

    @pl.when(pl.program_id(0) == 0)
    def _():
        place = place_of(len_ref, seqs)
        issue(sources, out, sems.at[0], place, width // 32)
        issue(sources, buf, sems.at[1], place, width // 32, width)
        settle(out, sems.at[0])

    joined = dot(o_ref[...], out[...], 1, 0) + vec_ref[0:1, :] + x_ref[...].astype(F32)
    centered = joined - jnp.mean(joined, axis=1, keepdims=True)
    spread = lax.rsqrt(jnp.mean(centered * centered, axis=1, keepdims=True) + LN_EPS)
    normed = centered * spread * vec_ref[1:2, :] + vec_ref[2:3, :]
    u_ref[...] = normed
    s_ref[...] = jnp.broadcast_to(spread, s_ref.shape)
    rounded = normed.astype(BF)
    pl.when(pl.program_id(0) == 0)(functools.partial(settle, buf, sems.at[1]))
    hidden(rounded, buf, bi_ref, gl_ref, gp_ref)


def join(scalars, seqs, rows, context, sources, vectors, bias_in):
    count, width = rows.shape
    wide = bias_in.shape[1]
    block = lambda cols: pl.BlockSpec((ROWS, cols), lambda i, n: (i, 0))
    return pl.pallas_call(
        functools.partial(join_body, seqs, tags_of(sources)),
        out_shape=(
            shape_of((count, width), F32),
            shape_of((count, 128), F32),
            shape_of((count, wide), BF),
            shape_of((count, wide), BF),
        ),
        grid_spec=pltpu.PrefetchScalarGridSpec(
            num_scalar_prefetch=1,
            grid=(count // ROWS,),
            in_specs=[
                block(width),
                block(width),
                pl.BlockSpec((8, width), lambda i, n: (0, 0)),
                pl.BlockSpec((1, wide), lambda i, n: (0, 0)),
                *([ANYWHERE] * len(sources)),
            ],
            out_specs=[block(width), block(128), block(wide), block(wide)],
            scratch_shapes=[
                pltpu.VMEM((width, width), BF),
                pltpu.VMEM((width, wide), BF),
                pltpu.SemaphoreType.DMA((2,)),
            ],
        ),
        compiler_params=params(),
        cost_estimate=cost(2 * count * width * (width + wide)),
        name="join",
    )(scalars, rows, context, vectors, bias_in, *arrays_of(sources))


TURN = 256


def turn_body(
    seqs, feed_tags, down_tags, len_ref, gl_ref, u_ref, s_ref, c_ref, vec_ref, gp_any, *refs
):
    feeds, downs = tagged(refs, feed_tags), tagged(refs[len(feed_tags) :], down_tags)
    y_ref, dh_ref, do_ref, gv_ref, gi_ref, out, buf, down, gp_ref, sems, gp_sems = refs[-11:]
    index = pl.program_id(0)
    first = index == 0
    width = u_ref.shape[1]
    wide = gl_ref.shape[1]
    parts = 4
    step = wide // parts
    steps = gp_ref.shape[0]
    slopes = [
        pltpu.make_async_copy(gp_any.at[pl.ds(n * TURN, TURN)], gp_ref.at[n], gp_sems.at[n])
        for n in range(steps)
    ]

    @pl.when(first)
    def _():
        place = place_of(len_ref, seqs)
        issue(downs, down, sems.at[0], place, wide // 32)
        slopes[0].start()
        issue(feeds, buf, sems.at[1], place, width // 32, width)
        issue(feeds, out, sems.at[2], place, width // 32)
        for copy in slopes[1:]:
            copy.start()
        gv_ref[...] = jnp.zeros_like(gv_ref)
        gi_ref[...] = jnp.zeros_like(gi_ref)
        settle(down, sems.at[0])

    gain_one, beta_one, gain_two, beta_two, bias_down = (vec_ref[n : n + 1, :] for n in range(1, 6))
    normed = u_ref[...]
    total = normed + bias_down + dot(gl_ref[...], down[...], 1, 0)
    centered = total - jnp.mean(total, axis=1, keepdims=True)
    spread = lax.rsqrt(jnp.mean(centered * centered, axis=1, keepdims=True) + LN_EPS)
    hat = centered * spread
    y_ref[...] = (hat * gain_two + beta_two).astype(BF)
    per_seq = L // TURN
    start = lax.rem(index, per_seq) * TURN
    live = lax.broadcasted_iota(jnp.int32, (TURN, 1), 0) + start < len_ref[index // per_seq]
    dy = jnp.where(live, c_ref[...].astype(F32), 0.0)
    gv_ref[4:5, :] += jnp.sum(dy, axis=0, keepdims=True)
    scaled = dy * gain_two
    d_two = spread * (
        scaled
        - jnp.mean(scaled, axis=1, keepdims=True)
        - hat * jnp.mean(scaled * hat, axis=1, keepdims=True)
    )
    d_branch = d_two.astype(BF)
    gv_ref[3:4, :] += jnp.sum(d_branch.astype(F32), axis=0, keepdims=True)
    pl.when(first)(functools.partial(settle, buf, sems.at[1]))
    for n in range(steps):
        pl.when(index == n)(slopes[n].wait)
    total = d_two
    for part in range(parts):
        rows = slice(part * step, (part + 1) * step)
        d_hidden = dot(d_branch, down[rows, :], 1, 1) * gp_ref[index, :, rows].astype(F32)
        d_hidden = d_hidden.astype(BF)
        gi_ref[:, rows] += jnp.sum(d_hidden.astype(F32), axis=0, keepdims=True)
        total = total + dot(d_hidden, buf[:, rows], 1, 1)
    gv_ref[2:3, :] += jnp.sum(total, axis=0, keepdims=True)
    scaled = total * gain_one
    hat = (normed - beta_one) * (1.0 / gain_one)
    d_one = s_ref[:, 0:1] * (
        scaled
        - jnp.mean(scaled, axis=1, keepdims=True)
        - hat * jnp.mean(scaled * hat, axis=1, keepdims=True)
    )
    dh_ref[...] = d_one
    d_att = d_one.astype(BF)
    gv_ref[1:2, :] += jnp.sum(d_att.astype(F32), axis=0, keepdims=True)

    pl.when(first)(functools.partial(settle, out, sems.at[2]))
    d_context = dot(d_att, out[...], 1, 1).astype(BF)
    do_ref[...] = d_context
    gv_ref[0:1, :] += jnp.sum(d_context.astype(F32), axis=0, keepdims=True)


def turn(scalars, seqs, gl, gp, normed, spread, cotangent, feeds, downs, vectors):
    count, width = normed.shape
    wide = gl.shape[1]
    steps = count // TURN
    block = lambda cols: pl.BlockSpec((TURN, cols), lambda i, n: (i, 0))
    return pl.pallas_call(
        functools.partial(turn_body, seqs, tags_of(feeds), tags_of(downs)),
        out_shape=(
            shape_of((count, width), BF),
            shape_of((count, width), F32),
            shape_of((count, width), BF),
            shape_of((8, width), F32),
            shape_of((1, wide), F32),
        ),
        grid_spec=pltpu.PrefetchScalarGridSpec(
            num_scalar_prefetch=1,
            grid=(steps,),
            in_specs=[
                block(wide),
                block(width),
                block(128),
                block(width),
                pl.BlockSpec((8, width), lambda i, n: (0, 0)),
                *([ANYWHERE] * (1 + len(feeds) + len(downs))),
            ],
            out_specs=[
                block(width),
                block(width),
                block(width),
                pl.BlockSpec((8, width), lambda i, n: (0, 0)),
                pl.BlockSpec((1, wide), lambda i, n: (0, 0)),
            ],
            scratch_shapes=[
                pltpu.VMEM((width, width), BF),
                pltpu.VMEM((width, wide), BF),
                pltpu.VMEM((wide, width), BF),
                pltpu.VMEM((steps, TURN, wide), BF),
                pltpu.SemaphoreType.DMA((3,)),
                pltpu.SemaphoreType.DMA((steps,)),
            ],
        ),
        compiler_params=params(),
        cost_estimate=cost(2 * count * width * (width + 3 * wide)),
        name="turn",
    )(
        scalars, gl, normed, spread, cotangent, vectors, gp, *arrays_of(feeds), *arrays_of(downs)
    )


WIDE = 512


def back_body(
    seqs, tags, len_ref, q_ref, k_ref, v_ref, o_ref, do_ref, r_ref, e_ref, dh_any, *refs
):
    sources = tagged(refs, tags)
    dx_ref, gq_ref, all_ref, w_ref, dh_ref, sem, dh_sem = refs[len(tags) :]
    seq, quad = pl.program_id(0), pl.program_id(1)
    quads = pl.num_programs(1)
    width = dx_ref.shape[1]
    rows = pl.ds(pl.multiple_of(seq * L, L), L)
    joined = pltpu.make_async_copy(dh_any.at[rows], dh_ref, dh_sem)
    pl.when(quad == 0)(joined.start)

    @pl.when((seq == 0) & (quad == 0))
    def _():
        issue(sources, w_ref, sem, place_of(len_ref, seqs), width // 32)
        gq_ref[...] = jnp.zeros_like(gq_ref)

    halves = lane_halves(BF)
    halves_wide = lane_halves(F32)
    lane = lax.broadcasted_iota(jnp.int32, (L, 128), 1)
    for pair in range(WIDE // 128):
        part = slice(pair * 128, (pair + 1) * 128)
        q_pair, k_pair, v_pair = (r[:, part] for r in (q_ref, k_ref, v_ref))
        do_pair = (do_ref[:, part].astype(F32) * r_ref[:, part]).astype(BF)
        products = do_pair.astype(F32) * o_ref[:, part].astype(F32)
        shifts = [jnp.sum(products * half, axis=1, keepdims=True) for half in halves_wide]
        rough = [shift.astype(BF).astype(F32) for shift in shifts]
        side = jnp.where(
            lane == 0,
            -rough[0],
            jnp.where(
                lane == 1,
                rough[0] - shifts[0],
                jnp.where(lane == 2, -rough[1], jnp.where(lane == 3, rough[1] - shifts[1], 0.0)),
            ),
        ).astype(BF)
        left = jnp.concatenate([do_pair, side], axis=1)
        q_turned = q_pair.T
        do_turned = do_pair.T
        d_scores, d_keys, d_values = [], [], []
        for head in range(2):
            rows = slice(head * HD, (head + 1) * HD)
            power = e_ref[2 * pair + head]
            marks = jnp.where(lane // 2 == head, 1.0, 0.0).astype(BF)
            right = jnp.concatenate([v_pair * halves[head], marks], axis=1)
            d_score = (power.astype(F32) * dot(left, right, 1, 1)).astype(BF)
            d_scores.append(d_score)
            d_keys.append(dot(q_turned[rows], d_score, 1, 0))
            d_values.append(dot(do_turned[rows], power, 1, 0))
        right = jnp.concatenate([k_pair * half for half in halves], axis=0)
        d_query = (dot(jnp.concatenate(d_scores, axis=1), right, 1, 0) * (HD**-0.5)).astype(BF)
        cols = pl.multiple_of(quad * WIDE + pair * 128, 128)
        gq_ref[:, pl.ds(cols, 128)] += jnp.sum(d_query.astype(F32), axis=0, keepdims=True)
        all_ref[:, pl.ds(cols, 128)] = d_query
        all_ref[:, pl.ds(width + cols, 128)] = jnp.concatenate(d_keys, axis=0).T.astype(BF)
        all_ref[:, pl.ds(2 * width + cols, 128)] = jnp.concatenate(d_values, axis=0).T.astype(BF)

    pl.when((seq == 0) & (quad == quads - 1))(functools.partial(settle, w_ref, sem))

    @pl.when(quad == quads - 1)
    def _():
        joined.wait()
        dx_ref[...] = (dh_ref[...] + dot(all_ref[...], w_ref[...], 1, 1)).astype(BF)


def back(scalars, seqs, qkv, context, d_context, inverse, powers, d_joined, sources):
    count, width = d_joined.shape
    quads = width // WIDE
    heads = WIDE // HD
    col = lambda n: pl.BlockSpec((L, WIDE), lambda i, j, s: (i, n * quads + j))
    return pl.pallas_call(
        functools.partial(back_body, seqs, tags_of(sources)),
        out_shape=(shape_of((count, width), BF), shape_of((1, width), F32)),
        grid_spec=pltpu.PrefetchScalarGridSpec(
            num_scalar_prefetch=1,
            grid=(seqs, quads),
            in_specs=[
                col(0),
                col(1),
                col(2),
                col(0),
                col(0),
                col(0),
                pl.BlockSpec((heads, L, L), lambda i, j, s: (i * quads + j, 0, 0)),
                *([ANYWHERE] * (1 + len(sources))),
            ],
            out_specs=[
                pl.BlockSpec((L, width), lambda i, j, s: (i, 0)),
                pl.BlockSpec((1, width), lambda i, j, s: (0, 0)),
            ],
            scratch_shapes=[
                pltpu.VMEM((L, 3 * width), BF),
                pltpu.VMEM((width, 3 * width), BF),
                pltpu.VMEM((L, width), F32),
                pltpu.SemaphoreType.DMA,
                pltpu.SemaphoreType.DMA,
            ],
        ),
        compiler_params=params(),
        cost_estimate=cost(2 * count * width * 3 * width + 20 * count * width * L),
        name="back",
    )(scalars, qkv, qkv, qkv, context, d_context, inverse, powers, d_joined, *arrays_of(sources))


BOTH = ("dp", "fsdp")


def hop(block, axis, flip):
    size = lax.axis_size(axis)
    return lax.ppermute(block, axis, [(i, i ^ flip) for i in range(size)])


def after_all(*values):
    return lax.optimization_barrier(values)


def over_x(block):
    return hop(block, "dp", 1)


def over_y(block):
    return hop(block, "dp", 2)


def over_core(block):
    return hop(block, "fsdp", 1)


def over_z(block, k):
    return hop(block, "fsdp", 2 * k)


def after(value, *earlier):
    return lax.optimization_barrier((value, *earlier))[0]


MOVES = {
    "x": over_x,
    "y": over_y,
    "c": over_core,
    "1": functools.partial(over_z, k=1),
    "2": functools.partial(over_z, k=2),
    "3": functools.partial(over_z, k=3),
}


def stage(lanes, blocks, *earlier):
    blocks = after(tuple(blocks), *earlier)
    return lax.optimization_barrier(tuple(MOVES[lane](block) for lane, block in zip(lanes, blocks)))


def both(mine, others):
    return [(array, (*tag, 0)) for array, tag in mine] + [
        (array, (*tag, 1)) for array, (_, tag) in zip(others, mine)
    ]


def whole(array):
    return [(array, None)]


def on_device(
    tokens, lengths, w_qkv, w_out, w_in, w_down, gain_one, gain_two,
    bias_q, bias_v, bias_out, beta_one, bias_in, bias_down, beta_two, cotangent,
):
    width = w_out.shape[1]
    seqs = lengths.shape[0]
    chip = lax.axis_index("fsdp")
    scalars = jnp.concatenate(
        [lengths, jnp.stack([lax.axis_index("dp"), chip // 2, chip % 2]).astype(jnp.int32)]
    )
    score_scale = HD**-0.5
    ones = jnp.ones((width,), F32)
    zeros = jnp.zeros((width,), F32)
    bias = jnp.concatenate([bias_q, zeros, bias_v])[None]
    scale = jnp.concatenate([ones * score_scale, ones, ones])[None]
    vectors = jnp.stack([bias_out, gain_one, beta_one, gain_two, beta_two, bias_down, zeros, zeros])
    special = (lax.axis_size("dp"), lax.axis_size("fsdp")) == (4, 8)
    if special:
        own, w_feed = pack(w_qkv, w_out, w_in, w_down)
        at_feed = w_qkv.shape[1]
        at_down = at_feed + w_feed.shape[1]
        z_two, z_three, z_one, near_x, near_y = stage("231xy", (w_qkv, w_qkv, w_qkv, own, own))
        tall, cols_feed = w_qkv.shape[0], w_feed.shape[1]
        z_one, scalars, bias, scale, vectors = after_all(z_one, scalars, bias, scale, vectors)
        (far,) = glue(
            (z_one, z_two, z_three), (at_feed, *((n, 0, tall, 0) for n in range(3)))
        )
        x_far, y_far, feed_two, own_core, near_x_core = stage(
            "xy2cc", (far, far, w_feed, own, near_x)
        )
        left, right = glue(
            (near_x, x_far, y_far),
            (at_feed, (0, 0, tall, 0), (1, 0, tall, 0)),
            (at_feed, (2, tall, 2 * tall, 0)),
        )
        crossed, crossed_more, feed_one, near_y_core, far_core = stage(
            "yx1cc", (left, right, w_feed, near_y, far), feed_two, own_core, near_x_core
        )
        x_far_core, y_far_core, crossed_core, crossed_more_core = stage(
            "cccc", (x_far, y_far, crossed, crossed_more), feed_one, near_y_core, far_core
        )
        near = (own, near_x, near_y)
        near_core = (own_core, near_x_core, near_y_core)
        rest = (1, 2, 3)
        qkv_parts = both(
            [
                *((array, (chip, (0,), 0)) for chip, array in enumerate(near)),
                (far, (0, rest, 0)),
                (x_far, (1, rest, 0)),
                (y_far, (2, rest, 0)),
                (crossed, (3, (0, 1), 0)),
                (crossed_more, (3, (2, 3), 0)),
            ],
            [*near_core, far_core, x_far_core, y_far_core, crossed_core, crossed_more_core],
        )
        pair, near_x_down = glue(
            (feed_one, feed_two, near_x),
            (cols_feed, (0, 0, tall, 0), (1, 0, tall, 0)),
            (w_down.shape[0] // tall * width, (2, 0, tall, at_down)),
        )
        x_pair, y_pair, feed_three, pair_core = stage(
            "xy3c", (pair, pair, w_feed, pair), y_far_core, crossed_core, crossed_more_core
        )
        first = after(tokens, pair)
    else:
        first = tokens
        w_feed = jnp.concatenate([w_out, w_in], axis=1)
        qkv_parts = whole(lax.all_gather(w_qkv, BOTH, axis=0, tiled=True))
        feed_parts = whole(lax.all_gather(w_feed, BOTH, axis=0, tiled=True))
        down_parts = whole(lax.all_gather(w_down, BOTH, axis=0, tiled=True))
    qkv = project(scalars, seqs, first, qkv_parts, bias, scale)
    if special:
        x_last, y_last, down_two, down_one, cross_down = stage(
            "xy21y", (feed_three, feed_three, w_down, w_down, near_x_down), qkv, pair_core
        )
    attended = []
    for seq in range(seqs):
        if special and seq == 1:
            x_last, y_last, *attended = after((x_last, y_last, *attended), cross_down, down_one)
            left, right = glue(
                (near_x, x_pair, y_pair, y_last),
                (cols_feed, (0, 0, tall, at_feed), (1, 0, tall, 0)),
                (cols_feed, (2, tall, tall, 0), (3, 0, tall, 0)),
            )
            crossed, crossed_more, down_three, x_pair_core, y_pair_core = stage(
                "yx3cc", (left, right, w_down, x_pair, y_pair), x_last, *attended
            )
        attended = attend(scalars, qkv, width, seq, attended)
    context, powers, inverse = attended
    if special:
        cores = stage(
            "ccccc", (feed_three, x_last, y_last, crossed, crossed_more), context, down_three
        )
        feed_parts = both(
            [
                *((array, (chip, (0,), at_feed)) for chip, array in enumerate(near)),
                (pair, (0, (1, 2), 0)),
                (x_pair, (1, (1, 2), 0)),
                (y_pair, (2, (1, 2), 0)),
                (feed_three, (0, (3,), 0)),
                (x_last, (1, (3,), 0)),
                (y_last, (2, (3,), 0)),
                (crossed, (3, (0, 1), 0)),
                (crossed_more, (3, (2, 3), 0)),
            ],
            [*near_core, pair_core, x_pair_core, y_pair_core, *cores],
        )
        (far,) = glue(
            (down_one, down_two, down_three),
            (width, *((n, 0, w_down.shape[0], 0) for n in range(3))),
        )
        x_far, y_far, *diagonal = stage(
            "xy231", (far, far, cross_down, cross_down, cross_down), *cores
        )
    normed, spread, gl, gp = join(
        scalars, seqs, tokens, context, feed_parts, vectors, bias_in[None]
    )
    if special:
        x_far, cross_down, gl = after((x_far, cross_down, gl), y_far, *diagonal)
    if special:
        mine = [
            (after(far, x_far), (0, rest, 0)),
            (x_far, (1, rest, 0)),
            (y_far, (2, rest, 0)),
            (cross_down, (3, (0,), 0)),
            *((block, (3, (k,), 0)) for block, k in zip(diagonal, (2, 3, 1))),
        ]
        down_parts = both(
            [*((array, (chip, (0,), at_down)) for chip, array in enumerate(near)), *mine],
            [*near_core, *(over_core(block) for block, _ in mine)],
        )
    output, d_joined, d_context, sums, sum_in = turn(
        scalars, seqs, gl, gp, normed, spread, cotangent, feed_parts, down_parts, vectors
    )
    input_grad, sum_q = back(scalars, seqs, qkv, context, d_context, inverse, powers, d_joined, qkv_parts)
    devices = lax.axis_size("dp") * lax.axis_size("fsdp")
    small = jnp.concatenate([sum_q, sums[:5]], axis=0).reshape(6, devices, -1).transpose(1, 0, 2)
    rows = jnp.concatenate([sum_in.reshape(devices, -1), small.reshape(devices, -1)], axis=1)
    mine = jnp.sum(lax.all_to_all(rows, BOTH, 0, 0, tiled=True), axis=0)
    wide = sum_in.shape[1] // devices
    six = mine[wide:].reshape(6, -1)
    shares = (six[0], six[1], six[2], six[3], mine[:wide], six[4], six[5])
    return (output, input_grad, *shares)


def solution(mesh):
    split, rows, copied = P(BOTH), P(BOTH, None), P()
    in_specs = (rows, split, rows, rows, rows, rows, *([copied] * 9), rows)
    out_specs = (rows, rows, *([split] * 7))
    return jax.shard_map(
        on_device, mesh=mesh, in_specs=in_specs, out_specs=out_specs, check_vma=False
    )
```

```python
import functools
import math

import jax
import jax.numpy as jnp
from jax import lax
from jax.experimental import pallas as pl
from jax.experimental.pallas import tpu as pltpu
from jax.sharding import PartitionSpec as P

HD = 64
L = 512
LN_EPS = 1e-12
MIB = 2**20
BF = jnp.bfloat16
F32 = jnp.float32


def params(limit=60, semantics=None):
    return pltpu.CompilerParams(vmem_limit_bytes=limit * MIB, dimension_semantics=semantics)


def dot(left, right, on_left, on_right):
    return lax.dot_general(
        left, right, (((on_left,), (on_right,)), ((), ())), preferred_element_type=F32
    )


def shape_of(dims, kind):
    return jax.ShapeDtypeStruct(dims, kind)


def cost(flops):
    return pl.CostEstimate(flops=flops, bytes_accessed=0, transcendentals=0)


def issue(sources, buf, sem, place, height, window=0):
    plane_at, z_at, core_at = place
    cols = buf.shape[1]
    for source, tag in sources:
        if tag is None:
            pltpu.make_async_copy(source.at[:, pl.ds(window, cols)], buf, sem).start()
            continue
        chip, zs, first, turned = tag
        tall = source.shape[0] // len(zs)
        for step, z in enumerate(zs):
            row = ((plane_at ^ chip) * 8 + (z_at ^ z) * 2 + (core_at ^ turned)) * height
            for block in range(height // tall):
                pltpu.make_async_copy(
                    source.at[pl.ds(step * tall, tall), pl.ds(first + window + block * cols, cols)],
                    buf.at[pl.ds(pl.multiple_of(row + block * tall, tall), tall)],
                    sem,
                ).start()


def settle(buf, sem):
    pltpu.make_async_copy(buf, buf, sem).wait()


def tagged(refs, tags):
    return list(zip(refs, tags))


def tags_of(sources):
    return [tag for _, tag in sources]


def arrays_of(sources):
    return [array for array, _ in sources]


def place_of(scalars, seqs):
    return scalars[seqs], scalars[seqs + 1], scalars[seqs + 2]


ANYWHERE = pl.BlockSpec(memory_space=pl.ANY)

def pack_body(qkv_ref, out_ref, in_ref, down_ref, own_ref, feed_ref, sem):
    height = qkv_ref.shape[0]
    copies, at = [], 0
    for ref in (qkv_ref, out_ref, in_ref):
        copies.append(pltpu.make_async_copy(ref, own_ref.at[:, pl.ds(at, ref.shape[1])], sem))
        at += ref.shape[1]
    for first in range(0, down_ref.shape[0], height):
        window = down_ref.at[pl.ds(first, height)]
        copies.append(pltpu.make_async_copy(window, own_ref.at[:, pl.ds(at, down_ref.shape[1])], sem))
        at += down_ref.shape[1]
    for copy in copies:
        copy.start()
    settle(own_ref, sem)
    first = qkv_ref.shape[1]
    feed_ref[...] = own_ref[:, first : first + feed_ref.shape[1]]


def pack(w_qkv, w_out, w_in, w_down):
    height = w_qkv.shape[0]
    feed_wide = w_out.shape[1] + w_in.shape[1]
    wide = w_qkv.shape[1] + feed_wide + w_down.shape[0] // height * w_down.shape[1]
    return pl.pallas_call(
        pack_body,
        out_shape=(shape_of((height, wide), BF), shape_of((height, feed_wide), BF)),
        in_specs=[ANYWHERE] * 4,
        scratch_shapes=[pltpu.SemaphoreType.DMA],
        compiler_params=params(),
        name="pack",
    )(w_qkv, w_out, w_in, w_down)


def glue_body(plans, count, *refs):
    sources, targets = refs[:count], refs[count:]
    for plan, target in zip(plans, targets):
        at = 0
        for number, top, rows, left in plan:
            target[at : at + rows, :] = sources[number][top : top + rows, left : left + target.shape[1]]
            at += rows


def glue(arrays, *plans):
    return pl.pallas_call(
        functools.partial(glue_body, [plan[1:] for plan in plans], len(arrays)),
        out_shape=[shape_of((sum(w[2] for w in plan[1:]), plan[0]), BF) for plan in plans],
        compiler_params=params(20),
        name="glue",
    )(*arrays)


def project_body(seqs, tags, len_ref, x_ref, bias_ref, scale_ref, *refs):
    sources, (out_ref, buf, sems) = tagged(refs, tags), refs[len(tags) :]
    here = pl.program_id(0)
    step = out_ref.shape[1]

    @pl.when(here == 0)
    def _():
        place = place_of(len_ref, seqs)
        for part in range(buf.shape[0]):
            issue(sources, buf.at[part], sems.at[part], place, buf.shape[1] // 32, part * step)

    settle(buf.at[here], sems.at[here])
    total = dot(x_ref[...], buf[here], 1, 0) + bias_ref[...]
    out_ref[...] = (total * scale_ref[...]).astype(BF)


def project(scalars, seqs, rows, sources, bias, scale):
    count, width = rows.shape
    wide = bias.shape[1]
    step = PROJECT
    return pl.pallas_call(
        functools.partial(project_body, seqs, tags_of(sources)),
        out_shape=shape_of((count, wide), BF),
        grid_spec=pltpu.PrefetchScalarGridSpec(
            num_scalar_prefetch=1,
            grid=(wide // step,),
            in_specs=[
                pl.BlockSpec((count, width), lambda j, n: (0, 0)),
                pl.BlockSpec((1, step), lambda j, n: (0, j)),
                pl.BlockSpec((1, step), lambda j, n: (0, j)),
                *([ANYWHERE] * len(sources)),
            ],
            out_specs=pl.BlockSpec((count, step), lambda j, n: (0, j)),
            scratch_shapes=[
                pltpu.VMEM((wide // step, width, step), BF),
                pltpu.SemaphoreType.DMA((wide // step,)),
            ],
        ),
        compiler_params=params(),
        cost_estimate=cost(2 * count * width * wide),
        name="project",
    )(scalars, rows, bias, scale, *arrays_of(sources))


PROJECT = 512


def lane_halves(kind):
    lane = lax.broadcasted_iota(jnp.int32, (1, 128), 1)
    return [(lane < HD).astype(F32).astype(kind), (lane >= HD).astype(F32).astype(kind)]


QUAD = 256


def attend_body(seq, len_ref, q_ref, k_ref, v_ref, *refs):
    o_ref, e_ref, r_ref = refs[-3:]
    length = len_ref[seq]
    halves = lane_halves(BF)
    lane = lax.broadcasted_iota(jnp.int32, (L, 128), 1)
    row = lax.broadcasted_iota(jnp.int32, (L, 128), 0)
    q_side = jnp.where(lane == 0, 1.0, 0.0).astype(BF)
    k_side = jnp.where((lane == 0) & (row >= length), -1e30, 0.0).astype(BF)
    for pair in range(QUAD // 128):
        part = slice(pair * 128, (pair + 1) * 128)
        q_pair = jnp.concatenate([q_ref[:, part], q_side], axis=1)
        k_pair = k_ref[:, part]
        v_pair = v_ref[:, part]
        powers = []
        for head in range(2):
            k_one = jnp.concatenate([k_pair * halves[head], k_side], axis=1)
            scores = dot(q_pair, k_one, 1, 1)
            peak = jnp.max(scores, axis=1, keepdims=True)
            power = jnp.exp(scores - peak).astype(BF)
            e_ref[2 * pair + head] = power
            powers.append(power)
        right = jnp.concatenate(
            [
                jnp.concatenate([v_pair * half, jnp.broadcast_to(half, (L, 128))], axis=1)
                for half in halves
            ],
            axis=0,
        )
        both = dot(jnp.concatenate(powers, axis=1), right, 1, 0)
        inverse = 1.0 / both[:, 128:]
        r_ref[:, part] = inverse
        o_ref[:, part] = (both[:, :128] * inverse).astype(BF)


def attend(scalars, qkv, width, seq, earlier):
    count = qkv.shape[0]
    quads = width // QUAD
    heads = QUAD // HD
    return pl.pallas_call(
        functools.partial(attend_body, seq),
        out_shape=(
            shape_of((count, width), BF),
            shape_of((count // L * width // HD, L, L), BF),
            shape_of((count, width), F32),
        ),
        grid_spec=pltpu.PrefetchScalarGridSpec(
            num_scalar_prefetch=1,
            grid=(quads,),
            in_specs=[
                pl.BlockSpec((L, QUAD), lambda j, n: (seq, j)),
                pl.BlockSpec((L, QUAD), lambda j, n: (seq, quads + j)),
                pl.BlockSpec((L, QUAD), lambda j, n: (seq, 2 * quads + j)),
                *([ANYWHERE] * len(earlier)),
            ],
            out_specs=[
                pl.BlockSpec((L, QUAD), lambda j, n: (seq, j)),
                pl.BlockSpec((heads, L, L), lambda j, n: (seq * quads + j, 0, 0)),
                pl.BlockSpec((L, QUAD), lambda j, n: (seq, j)),
            ],
        ),
        compiler_params=params(),
        input_output_aliases={4 + n: n for n in range(len(earlier))},
        cost_estimate=cost(16 * L * width * L),
        name="attend",
    )(scalars, qkv, qkv, qkv, *earlier)


ROWS = 256
FEED = 512


def hidden(rounded, buf, bi_ref, gl_ref, gp_ref):
    for part in range(gl_ref.shape[1] // FEED):
        cols = slice(part * FEED, (part + 1) * FEED)
        pre = dot(rounded, buf[:, cols], 1, 0) + bi_ref[:, cols]
        phi = 0.5 + 0.5 * lax.erf(pre * math.sqrt(0.5))
        power = (-0.5 / math.log(2.0)) * pre * pre - 0.5 * math.log2(2.0 * math.pi)
        gl_ref[:, cols] = (pre * phi).astype(BF)
        gp_ref[:, cols] = (phi + pre * jnp.exp2(power)).astype(BF)


def join_body(seqs, tags, len_ref, x_ref, o_ref, vec_ref, bi_ref, *refs):
    sources = tagged(refs, tags)
    u_ref, s_ref, gl_ref, gp_ref, out, buf, sems = refs[-7:]
    width = x_ref.shape[1]

    @pl.when(pl.program_id(0) == 0)
    def _():
        place = place_of(len_ref, seqs)
        issue(sources, out, sems.at[0], place, width // 32)
        issue(sources, buf, sems.at[1], place, width // 32, width)
        settle(out, sems.at[0])

    joined = dot(o_ref[...], out[...], 1, 0) + vec_ref[0:1, :] + x_ref[...].astype(F32)
    centered = joined - jnp.mean(joined, axis=1, keepdims=True)
    spread = lax.rsqrt(jnp.mean(centered * centered, axis=1, keepdims=True) + LN_EPS)
    normed = centered * spread * vec_ref[1:2, :] + vec_ref[2:3, :]
    u_ref[...] = normed
    s_ref[...] = jnp.broadcast_to(spread, s_ref.shape)
    rounded = normed.astype(BF)
    pl.when(pl.program_id(0) == 0)(functools.partial(settle, buf, sems.at[1]))
    hidden(rounded, buf, bi_ref, gl_ref, gp_ref)


def join(scalars, seqs, rows, context, sources, vectors, bias_in):
    count, width = rows.shape
    wide = bias_in.shape[1]
    block = lambda cols: pl.BlockSpec((ROWS, cols), lambda i, n: (i, 0))
    return pl.pallas_call(
        functools.partial(join_body, seqs, tags_of(sources)),
        out_shape=(
            shape_of((count, width), F32),
            shape_of((count, 128), F32),
            shape_of((count, wide), BF),
            shape_of((count, wide), BF),
        ),
        grid_spec=pltpu.PrefetchScalarGridSpec(
            num_scalar_prefetch=1,
            grid=(count // ROWS,),
            in_specs=[
                block(width),
                block(width),
                pl.BlockSpec((8, width), lambda i, n: (0, 0)),
                pl.BlockSpec((1, wide), lambda i, n: (0, 0)),
                *([ANYWHERE] * len(sources)),
            ],
            out_specs=[block(width), block(128), block(wide), block(wide)],
            scratch_shapes=[
                pltpu.VMEM((width, width), BF),
                pltpu.VMEM((width, wide), BF),
                pltpu.SemaphoreType.DMA((2,)),
            ],
        ),
        compiler_params=params(),
        cost_estimate=cost(2 * count * width * (width + wide)),
        name="join",
    )(scalars, rows, context, vectors, bias_in, *arrays_of(sources))


TURN = 256


def turn_body(
    seqs, feed_tags, down_tags, len_ref, gl_ref, u_ref, s_ref, c_ref, vec_ref, gp_any, *refs
):
    feeds, downs = tagged(refs, feed_tags), tagged(refs[len(feed_tags) :], down_tags)
    y_ref, dh_ref, do_ref, gv_ref, gi_ref, out, buf, down, gp_ref, sems, gp_sems = refs[-11:]
    index = pl.program_id(0)
    first = index == 0
    width = u_ref.shape[1]
    wide = gl_ref.shape[1]
    parts = 4
    step = wide // parts
    steps = gp_ref.shape[0]
    slopes = [
        pltpu.make_async_copy(gp_any.at[pl.ds(n * TURN, TURN)], gp_ref.at[n], gp_sems.at[n])
        for n in range(steps)
    ]

    @pl.when(first)
    def _():
        place = place_of(len_ref, seqs)
        issue(downs, down, sems.at[0], place, wide // 32)
        slopes[0].start()
        issue(feeds, buf, sems.at[1], place, width // 32, width)
        issue(feeds, out, sems.at[2], place, width // 32)
        for copy in slopes[1:]:
            copy.start()
        gv_ref[...] = jnp.zeros_like(gv_ref)
        gi_ref[...] = jnp.zeros_like(gi_ref)
        settle(down, sems.at[0])

    gain_one, beta_one, gain_two, beta_two, bias_down = (vec_ref[n : n + 1, :] for n in range(1, 6))
    normed = u_ref[...]
    total = normed + bias_down + dot(gl_ref[...], down[...], 1, 0)
    centered = total - jnp.mean(total, axis=1, keepdims=True)
    spread = lax.rsqrt(jnp.mean(centered * centered, axis=1, keepdims=True) + LN_EPS)
    hat = centered * spread
    y_ref[...] = (hat * gain_two + beta_two).astype(BF)
    per_seq = L // TURN
    start = lax.rem(index, per_seq) * TURN
    live = lax.broadcasted_iota(jnp.int32, (TURN, 1), 0) + start < len_ref[index // per_seq]
    dy = jnp.where(live, c_ref[...].astype(F32), 0.0)
    gv_ref[4:5, :] += jnp.sum(dy, axis=0, keepdims=True)
    scaled = dy * gain_two
    d_two = spread * (
        scaled
        - jnp.mean(scaled, axis=1, keepdims=True)
        - hat * jnp.mean(scaled * hat, axis=1, keepdims=True)
    )
    d_branch = d_two.astype(BF)
    gv_ref[3:4, :] += jnp.sum(d_branch.astype(F32), axis=0, keepdims=True)
    pl.when(first)(functools.partial(settle, buf, sems.at[1]))
    for n in range(steps):
        pl.when(index == n)(slopes[n].wait)
    total = d_two
    for part in range(parts):
        rows = slice(part * step, (part + 1) * step)
        d_hidden = dot(d_branch, down[rows, :], 1, 1) * gp_ref[index, :, rows].astype(F32)
        d_hidden = d_hidden.astype(BF)
        gi_ref[:, rows] += jnp.sum(d_hidden.astype(F32), axis=0, keepdims=True)
        total = total + dot(d_hidden, buf[:, rows], 1, 1)
    gv_ref[2:3, :] += jnp.sum(total, axis=0, keepdims=True)
    scaled = total * gain_one
    hat = (normed - beta_one) * (1.0 / gain_one)
    d_one = s_ref[:, 0:1] * (
        scaled
        - jnp.mean(scaled, axis=1, keepdims=True)
        - hat * jnp.mean(scaled * hat, axis=1, keepdims=True)
    )
    dh_ref[...] = d_one
    d_att = d_one.astype(BF)
    gv_ref[1:2, :] += jnp.sum(d_att.astype(F32), axis=0, keepdims=True)

    pl.when(first)(functools.partial(settle, out, sems.at[2]))
    d_context = dot(d_att, out[...], 1, 1).astype(BF)
    do_ref[...] = d_context
    gv_ref[0:1, :] += jnp.sum(d_context.astype(F32), axis=0, keepdims=True)


def turn(scalars, seqs, gl, gp, normed, spread, cotangent, feeds, downs, vectors):
    count, width = normed.shape
    wide = gl.shape[1]
    steps = count // TURN
    block = lambda cols: pl.BlockSpec((TURN, cols), lambda i, n: (i, 0))
    return pl.pallas_call(
        functools.partial(turn_body, seqs, tags_of(feeds), tags_of(downs)),
        out_shape=(
            shape_of((count, width), BF),
            shape_of((count, width), F32),
            shape_of((count, width), BF),
            shape_of((8, width), F32),
            shape_of((1, wide), F32),
        ),
        grid_spec=pltpu.PrefetchScalarGridSpec(
            num_scalar_prefetch=1,
            grid=(steps,),
            in_specs=[
                block(wide),
                block(width),
                block(128),
                block(width),
                pl.BlockSpec((8, width), lambda i, n: (0, 0)),
                *([ANYWHERE] * (1 + len(feeds) + len(downs))),
            ],
            out_specs=[
                block(width),
                block(width),
                block(width),
                pl.BlockSpec((8, width), lambda i, n: (0, 0)),
                pl.BlockSpec((1, wide), lambda i, n: (0, 0)),
            ],
            scratch_shapes=[
                pltpu.VMEM((width, width), BF),
                pltpu.VMEM((width, wide), BF),
                pltpu.VMEM((wide, width), BF),
                pltpu.VMEM((steps, TURN, wide), BF),
                pltpu.SemaphoreType.DMA((3,)),
                pltpu.SemaphoreType.DMA((steps,)),
            ],
        ),
        compiler_params=params(),
        cost_estimate=cost(2 * count * width * (width + 3 * wide)),
        name="turn",
    )(
        scalars, gl, normed, spread, cotangent, vectors, gp, *arrays_of(feeds), *arrays_of(downs)
    )


WIDE = 512


def back_body(
    seqs, tags, len_ref, q_ref, k_ref, v_ref, o_ref, do_ref, r_ref, e_ref, dh_any, *refs
):
    sources = tagged(refs, tags)
    dx_ref, gq_ref, all_ref, w_ref, dh_ref, sem, dh_sem = refs[len(tags) :]
    seq, quad = pl.program_id(0), pl.program_id(1)
    quads = pl.num_programs(1)
    width = dx_ref.shape[1]
    rows = pl.ds(pl.multiple_of(seq * L, L), L)
    joined = pltpu.make_async_copy(dh_any.at[rows], dh_ref, dh_sem)
    pl.when(quad == 0)(joined.start)

    @pl.when((seq == 0) & (quad == 0))
    def _():
        issue(sources, w_ref, sem, place_of(len_ref, seqs), width // 32)
        gq_ref[...] = jnp.zeros_like(gq_ref)

    halves = lane_halves(BF)
    halves_wide = lane_halves(F32)
    lane = lax.broadcasted_iota(jnp.int32, (L, 128), 1)
    for pair in range(WIDE // 128):
        part = slice(pair * 128, (pair + 1) * 128)
        q_pair, k_pair, v_pair = (r[:, part] for r in (q_ref, k_ref, v_ref))
        do_pair = (do_ref[:, part].astype(F32) * r_ref[:, part]).astype(BF)
        products = do_pair.astype(F32) * o_ref[:, part].astype(F32)
        shifts = [jnp.sum(products * half, axis=1, keepdims=True) for half in halves_wide]
        rough = [shift.astype(BF).astype(F32) for shift in shifts]
        side = jnp.where(
            lane == 0,
            -rough[0],
            jnp.where(
                lane == 1,
                rough[0] - shifts[0],
                jnp.where(lane == 2, -rough[1], jnp.where(lane == 3, rough[1] - shifts[1], 0.0)),
            ),
        ).astype(BF)
        left = jnp.concatenate([do_pair, side], axis=1)
        q_turned = q_pair.T
        do_turned = do_pair.T
        d_scores, d_keys, d_values = [], [], []
        for head in range(2):
            rows = slice(head * HD, (head + 1) * HD)
            power = e_ref[2 * pair + head]
            marks = jnp.where(lane // 2 == head, 1.0, 0.0).astype(BF)
            right = jnp.concatenate([v_pair * halves[head], marks], axis=1)
            d_score = (power.astype(F32) * dot(left, right, 1, 1)).astype(BF)
            d_scores.append(d_score)
            d_keys.append(dot(q_turned[rows], d_score, 1, 0))
            d_values.append(dot(do_turned[rows], power, 1, 0))
        right = jnp.concatenate([k_pair * half for half in halves], axis=0)
        d_query = (dot(jnp.concatenate(d_scores, axis=1), right, 1, 0) * (HD**-0.5)).astype(BF)
        cols = pl.multiple_of(quad * WIDE + pair * 128, 128)
        gq_ref[:, pl.ds(cols, 128)] += jnp.sum(d_query.astype(F32), axis=0, keepdims=True)
        all_ref[:, pl.ds(cols, 128)] = d_query
        all_ref[:, pl.ds(width + cols, 128)] = jnp.concatenate(d_keys, axis=0).T.astype(BF)
        all_ref[:, pl.ds(2 * width + cols, 128)] = jnp.concatenate(d_values, axis=0).T.astype(BF)

    pl.when((seq == 0) & (quad == quads - 1))(functools.partial(settle, w_ref, sem))

    @pl.when(quad == quads - 1)
    def _():
        joined.wait()
        dx_ref[...] = (dh_ref[...] + dot(all_ref[...], w_ref[...], 1, 1)).astype(BF)


def back(scalars, seqs, qkv, context, d_context, inverse, powers, d_joined, sources):
    count, width = d_joined.shape
    quads = width // WIDE
    heads = WIDE // HD
    col = lambda n: pl.BlockSpec((L, WIDE), lambda i, j, s: (i, n * quads + j))
    return pl.pallas_call(
        functools.partial(back_body, seqs, tags_of(sources)),
        out_shape=(shape_of((count, width), BF), shape_of((1, width), F32)),
        grid_spec=pltpu.PrefetchScalarGridSpec(
            num_scalar_prefetch=1,
            grid=(seqs, quads),
            in_specs=[
                col(0),
                col(1),
                col(2),
                col(0),
                col(0),
                col(0),
                pl.BlockSpec((heads, L, L), lambda i, j, s: (i * quads + j, 0, 0)),
                *([ANYWHERE] * (1 + len(sources))),
            ],
            out_specs=[
                pl.BlockSpec((L, width), lambda i, j, s: (i, 0)),
                pl.BlockSpec((1, width), lambda i, j, s: (0, 0)),
            ],
            scratch_shapes=[
                pltpu.VMEM((L, 3 * width), BF),
                pltpu.VMEM((width, 3 * width), BF),
                pltpu.VMEM((L, width), F32),
                pltpu.SemaphoreType.DMA,
                pltpu.SemaphoreType.DMA,
            ],
        ),
        compiler_params=params(),
        cost_estimate=cost(2 * count * width * 3 * width + 20 * count * width * L),
        name="back",
    )(scalars, qkv, qkv, qkv, context, d_context, inverse, powers, d_joined, *arrays_of(sources))


BOTH = ("dp", "fsdp")


def hop(block, axis, flip):
    size = lax.axis_size(axis)
    return lax.ppermute(block, axis, [(i, i ^ flip) for i in range(size)])


def after_all(*values):
    return lax.optimization_barrier(values)


def over_x(block):
    return hop(block, "dp", 1)


def over_y(block):
    return hop(block, "dp", 2)


def over_core(block):
    return hop(block, "fsdp", 1)


def over_z(block, k):
    return hop(block, "fsdp", 2 * k)


def after(value, *earlier):
    return lax.optimization_barrier((value, *earlier))[0]


MOVES = {
    "x": over_x,
    "y": over_y,
    "c": over_core,
    "1": functools.partial(over_z, k=1),
    "2": functools.partial(over_z, k=2),
    "3": functools.partial(over_z, k=3),
}


def stage(lanes, blocks, *earlier):
    blocks = after(tuple(blocks), *earlier)
    return lax.optimization_barrier(tuple(MOVES[lane](block) for lane, block in zip(lanes, blocks)))


def both(mine, others):
    return [(array, (*tag, 0)) for array, tag in mine] + [
        (array, (*tag, 1)) for array, (_, tag) in zip(others, mine)
    ]


def whole(array):
    return [(array, None)]


def on_device(
    tokens, lengths, w_qkv, w_out, w_in, w_down, gain_one, gain_two,
    bias_q, bias_v, bias_out, beta_one, bias_in, bias_down, beta_two, cotangent,
):
    width = w_out.shape[1]
    seqs = lengths.shape[0]
    chip = lax.axis_index("fsdp")
    scalars = jnp.concatenate(
        [lengths, jnp.stack([lax.axis_index("dp"), chip // 2, chip % 2]).astype(jnp.int32)]
    )
    score_scale = HD**-0.5
    ones = jnp.ones((width,), F32)
    zeros = jnp.zeros((width,), F32)
    bias = jnp.concatenate([bias_q, zeros, bias_v])[None]
    scale = jnp.concatenate([ones * score_scale, ones, ones])[None]
    vectors = jnp.stack([bias_out, gain_one, beta_one, gain_two, beta_two, bias_down, zeros, zeros])
    special = (lax.axis_size("dp"), lax.axis_size("fsdp")) == (4, 8)
    if special:
        own, w_feed = pack(w_qkv, w_out, w_in, w_down)
        at_feed = w_qkv.shape[1]
        at_down = at_feed + w_feed.shape[1]
        z_two, z_three, z_one, near_x, near_y = stage("231xy", (w_qkv, w_qkv, w_qkv, own, own))
        tall, cols_feed = w_qkv.shape[0], w_feed.shape[1]
        z_one, scalars, bias, scale, vectors = after_all(z_one, scalars, bias, scale, vectors)
        (far,) = glue(
            (z_one, z_two, z_three), (at_feed, *((n, 0, tall, 0) for n in range(3)))
        )
        x_far, y_far, feed_two, own_core, near_x_core = stage(
            "xy2cc", (far, far, w_feed, own, near_x)
        )
        left, right = glue(
            (near_x, x_far, y_far),
            (at_feed, (0, 0, tall, 0), (1, 0, tall, 0)),
            (at_feed, (2, tall, 2 * tall, 0)),
        )
        crossed, crossed_more, feed_one, near_y_core, far_core = stage(
            "yx1cc", (left, right, w_feed, near_y, far), feed_two, own_core, near_x_core
        )
        x_far_core, y_far_core, crossed_core, crossed_more_core = stage(
            "cccc", (x_far, y_far, crossed, crossed_more), feed_one, near_y_core, far_core
        )
        near = (own, near_x, near_y)
        near_core = (own_core, near_x_core, near_y_core)
        rest = (1, 2, 3)
        qkv_parts = both(
            [
                *((array, (chip, (0,), 0)) for chip, array in enumerate(near)),
                (far, (0, rest, 0)),
                (x_far, (1, rest, 0)),
                (y_far, (2, rest, 0)),
                (crossed, (3, (0, 1), 0)),
                (crossed_more, (3, (2, 3), 0)),
            ],
            [*near_core, far_core, x_far_core, y_far_core, crossed_core, crossed_more_core],
        )
        pair, near_x_down = glue(
            (feed_one, feed_two, near_x),
            (cols_feed, (0, 0, tall, 0), (1, 0, tall, 0)),
            (w_down.shape[0] // tall * width, (2, 0, tall, at_down)),
        )
        x_pair, y_pair, feed_three, pair_core = stage(
            "xy3c", (pair, pair, w_feed, pair), y_far_core, crossed_core, crossed_more_core
        )
        first = after(tokens, pair)
    else:
        first = tokens
        w_feed = jnp.concatenate([w_out, w_in], axis=1)
        qkv_parts = whole(lax.all_gather(w_qkv, BOTH, axis=0, tiled=True))
        feed_parts = whole(lax.all_gather(w_feed, BOTH, axis=0, tiled=True))
        down_parts = whole(lax.all_gather(w_down, BOTH, axis=0, tiled=True))
    qkv = project(scalars, seqs, first, qkv_parts, bias, scale)
    if special:
        x_last, y_last, down_two, down_one, cross_down = stage(
            "xy21y", (feed_three, feed_three, w_down, w_down, near_x_down), qkv, pair_core
        )
    attended = []
    for seq in range(seqs):
        if special and seq == 1:
            x_last, y_last, *attended = after((x_last, y_last, *attended), cross_down, down_one)
            left, right = glue(
                (near_x, x_pair, y_pair, y_last),
                (cols_feed, (0, 0, tall, at_feed), (1, 0, tall, 0)),
                (cols_feed, (2, tall, tall, 0), (3, 0, tall, 0)),
            )
            crossed, crossed_more, down_three, corner_one, x_pair_core = stage(
                "yx31c", (left, right, w_down, cross_down, x_pair), x_last, *attended
            )
        attended = attend(scalars, qkv, width, seq, attended)
    context, powers, inverse = attended
    if special:
        y_pair_core, *cores = stage(
            "cccccc",
            (y_pair, feed_three, x_last, y_last, crossed, crossed_more),
            context,
            down_three,
        )
        feed_parts = both(
            [
                *((array, (chip, (0,), at_feed)) for chip, array in enumerate(near)),
                (pair, (0, (1, 2), 0)),
                (x_pair, (1, (1, 2), 0)),
                (y_pair, (2, (1, 2), 0)),
                (feed_three, (0, (3,), 0)),
                (x_last, (1, (3,), 0)),
                (y_last, (2, (3,), 0)),
                (crossed, (3, (0, 1), 0)),
                (crossed_more, (3, (2, 3), 0)),
            ],
            [*near_core, pair_core, x_pair_core, y_pair_core, *cores],
        )
        (far,) = glue(
            (down_one, down_two, down_three),
            (width, *((n, 0, w_down.shape[0], 0) for n in range(3))),
        )
        x_far, y_far, *diagonal, far_core = stage(
            "xy23c", (far, far, cross_down, cross_down, far), *cores
        )
        diagonal.append(corner_one)
    normed, spread, gl, gp = join(
        scalars, seqs, tokens, context, feed_parts, vectors, bias_in[None]
    )
    if special:
        x_far, cross_down, gl = after((x_far, cross_down, gl), y_far, *diagonal)
    if special:
        mine = [
            (x_far, (1, rest, 0)),
            (y_far, (2, rest, 0)),
            (cross_down, (3, (0,), 0)),
            *((block, (3, (k,), 0)) for block, k in zip(diagonal, (2, 3, 1))),
        ]
        down_parts = both(
            [
                *((array, (chip, (0,), at_down)) for chip, array in enumerate(near)),
                (far, (0, rest, 0)),
                *mine,
            ],
            [*near_core, far_core, *(over_core(after(block, gl)) for block, _ in mine)],
        )
    output, d_joined, d_context, sums, sum_in = turn(
        scalars, seqs, gl, gp, normed, spread, cotangent, feed_parts, down_parts, vectors
    )
    input_grad, sum_q = back(scalars, seqs, qkv, context, d_context, inverse, powers, d_joined, qkv_parts)
    devices = lax.axis_size("dp") * lax.axis_size("fsdp")
    small = jnp.concatenate([sum_q, sums[:5]], axis=0).reshape(6, devices, -1).transpose(1, 0, 2)
    rows = jnp.concatenate([sum_in.reshape(devices, -1), small.reshape(devices, -1)], axis=1)
    mine = jnp.sum(lax.all_to_all(rows, BOTH, 0, 0, tiled=True), axis=0)
    wide = sum_in.shape[1] // devices
    six = mine[wide:].reshape(6, -1)
    shares = (six[0], six[1], six[2], six[3], mine[:wide], six[4], six[5])
    return (output, input_grad, *shares)


def solution(mesh):
    split, rows, copied = P(BOTH), P(BOTH, None), P()
    in_specs = (rows, split, rows, rows, rows, rows, *([copied] * 9), rows)
    out_specs = (rows, rows, *([split] * 7))
    return jax.shard_map(
        on_device, mesh=mesh, in_specs=in_specs, out_specs=out_specs, check_vma=False
    )
```
